256 devices in a mesh: elem: 16 (over z, x_lo), inner: 16 (over y, x_hi, core).
Axes of the slice: x: 4 (x_hi: 2, x_lo: 2; x = x_hi * 2 + x_lo), y: 4, z: 8, core: 2. Of those that a mesh axis runs over, the one named last changes fastest.
Arguments:
- basis: bfloat16 [32, 4, 512, 4096], P('elem', None, 'inner'), may hold values from -6 to 6, as said below
- potential: float32 [32, 4096], P('elem'), may hold values from 0.2 to 2
- face_index: int32 [32, 2, 128], P('elem'), may hold values from 0 to 4095, as said below
- face_match: int32 [32, 128], P('elem'), may hold values from 0 to 127, each once within a row
- vectors: bfloat16 [32, 512, 4096], P('elem', None, 'inner'), may hold values from -6 to 6
Outputs:
- filtered: float32 [32, 512, 4096], P('elem', None, 'inner')
The draws below stay inside these ranges and needn't reach their ends.
Inputs may be any that keep to these rules, and one draw needn't show every extreme that they name: `basis`: entries are independent, of mean zero and variance one. `face_index`: within one element the 256 listed grid points are distinct. Row e is a permutation; right-face point f of element e - 1 (modulo 32) meets left-face point face_match[e, f] of element e.
All inputs are finite; a program needn't handle non-finite values.
Results may differ from the reference program's by a relative error of at most 0.007.
The reference program's roundings to bfloat16 on the way count: a program that leaves them out, or rounds other values in their place, can miss the bound.
Values may be sent and summed in bfloat16 or wider, within the bound.
No kernel may reach another device: no remote copies, remote signals or barrier semaphores. Data moves between devices by JAX's collectives and lax.ppermute only.
A program may use at most 64 MiB of HBM per device.

```python
import math
import jax
import jax.numpy as jnp
from jax import lax

NB = 512
NG = 4096
F = 128
STEPS = 6
NE = 32
NV = 4096


def draw_basis(key, part):
    shape = (NE, 4, NB, NG)
    values = jnp.clip(jax.random.normal(key, shape, jnp.float32), -6.0, 6.0)
    return values.astype(jnp.bfloat16)


def draw_face_index(key, part):
    element_keys = jax.random.split(jax.random.fold_in(key, 7), NE)
    shuffled = jax.vmap(lambda subkey: jax.random.permutation(subkey, NG))(element_keys).astype(jnp.int32)
    leading_row = shuffled[0]
    moved = leading_row[0]
    leading_row = jnp.where(leading_row == 0, moved, leading_row).at[0].set(0)
    moved = leading_row[1]
    leading_row = jnp.where(leading_row == NG - 1, moved, leading_row).at[1].set(NG - 1)
    shuffled = shuffled.at[0].set(leading_row)
    return shuffled[:, :2 * F].reshape(NE, 2, F).astype(jnp.int32)


def level_of(rng, extent, cuts, least, largest):
    level, own = 1.0, jax.random.fold_in(rng, 6)
    for dim, shards_of in cuts:
        heights = jnp.exp(jax.random.uniform(jax.random.fold_in(own, dim), (shards_of,), jnp.float32, least / len(cuts), largest / len(cuts)))
        level = level * jnp.repeat(heights, extent[dim] // shards_of).reshape([-1 if axis == dim else 1 for axis in range(len(extent))])
    return level


def gaussian(own_key, dims, deviation, bound, cuts=(), held_as=jnp.bfloat16):
    level = level_of(own_key, dims, cuts, -0.22, 0.18) if cuts else 1.0
    entries = jax.random.normal(own_key, dims, jnp.float32) * deviation * level
    return jnp.minimum(jnp.maximum(entries, -bound), bound).astype(held_as)


def setup_inputs(seed: int = 0) -> dict:
    seeds = jax.random.split(jax.random.key(seed), 6)
    basis = draw_basis(jax.random.fold_in(seeds[5], 71), 0)
    potential = jnp.clip(jnp.exp(math.log(2.0) - 2.3025851 * jax.random.uniform(seeds[1], (NE, NG), jnp.float32) ** level_of(seeds[1], (NE, NG), ((0, 16),), -0.2, 0.2)), 0.2, 2.0)
    face_index = draw_face_index(jax.random.fold_in(seeds[5], 71), 0)
    face_match = jax.vmap(lambda own: jax.random.permutation(own, F))(jax.random.split(seeds[3], NE)).reshape((NE, F)).astype(jnp.int32)
    vectors = gaussian(seeds[4], (NE, NB, NV), 1.0, 6.0, ((0, 16), (2, 16)))
    return dict(basis=basis, potential=potential, face_index=face_index, face_match=face_match, vectors=vectors)


CENTER = 5.25
HALF_WIDTH = 2.75

def chebyshev_norm(count):
    ratio = (CENTER - 1.0) / HALF_WIDTH
    root = ratio + (ratio * ratio - 1.0) ** 0.5
    return 0.5 * (root ** count + root ** (-count))

def face_pair(leading, second):
    return jnp.einsum('nsaf,nsbf->nab', leading.astype(jnp.float32), jnp.flip(second, 1).astype(jnp.float32)) / (4.0 * F)

def element_terms(inputs):
    element_block, element_potential, right_points, left_points = inputs
    scaled = (jnp.sqrt(element_potential)[None, :] * element_block[0].astype(jnp.float32)).astype(jnp.bfloat16)
    volume = jnp.dot(scaled, scaled.T, preferred_element_type=jnp.float32)
    slopes = element_block[1:4].astype(jnp.float32)
    kinetic = jnp.einsum('cag,cbg->ab', slopes, slopes)
    gram_sum = (volume + 0.5 * kinetic) / NG
    right_found = jnp.take(element_block[0:2], right_points, axis=2)
    left_found = jnp.take(element_block[0:2], left_points, axis=2)
    right_flux = (0.5 * right_found[0].astype(jnp.float32) - 0.25 * right_found[1].astype(jnp.float32)).astype(jnp.bfloat16)
    left_flux = (-0.5 * left_found[0].astype(jnp.float32) - 0.25 * left_found[1].astype(jnp.float32)).astype(jnp.bfloat16)
    right_sides = jnp.stack((right_flux, right_found[0]))
    left_sides = jnp.stack((left_flux, -left_found[0]))
    return (gram_sum, right_sides, left_sides)

def reference(basis, potential, face_index, face_match, vectors):
    left_points = jnp.take_along_axis(face_index[:, 0, :], face_match, axis=1)
    gram_sum, right_sides, left_sides = lax.map(element_terms, (basis, potential, face_index[:, 1, :], left_points))
    diagonal = (gram_sum + face_pair(right_sides, right_sides) + face_pair(left_sides, left_sides)).astype(jnp.bfloat16)
    upper_blocks = face_pair(right_sides, jnp.roll(left_sides, -1, axis=0)).astype(jnp.bfloat16)
    diagonal_wide = diagonal.astype(jnp.float32)
    upper_wide = upper_blocks.astype(jnp.float32)
    lower_wide = jnp.roll(upper_wide, 1, axis=0)

    def apply_operator(current_bf):
        wide = current_bf.astype(jnp.float32)
        result = jnp.einsum('eab,ebv->eav', diagonal_wide, wide)
        result = result + jnp.einsum('eab,ebv->eav', upper_wide, jnp.roll(wide, -1, axis=0))
        result = result + jnp.einsum('eba,ebv->eav', lower_wide, jnp.roll(wide, 1, axis=0))
        return result
    previous = vectors.astype(jnp.float32)
    current = (apply_operator(vectors) - CENTER * previous) / HALF_WIDTH
    for iteration in range(1, STEPS):
        applied = apply_operator(current.astype(jnp.bfloat16))
        following = 2.0 * (applied - CENTER * current) / HALF_WIDTH - previous
        previous = current
        current = following
    return current / chebyshev_norm(STEPS)
```

```python
import jax
import jax.numpy as jnp
from jax import lax
from jax.experimental import pallas as pl
from jax.experimental.pallas import tpu as pltpu
from jax.sharding import PartitionSpec as P

NB = 512
NG = 4096
F = 128
STEPS = 6
CENTER = 5.25
HALF_WIDTH = 2.75
NZ, NY, NX = 8, 4, 4
BOTH = ("elem", "inner")
SLAB = NG // 8
PACKED = 10 * 128
PIECE = PACKED // 16
VMEM_LIMIT = 40 * 1024 * 1024
bf16 = jnp.bfloat16
f32 = jnp.float32


def flat(z, y, x, c):
    z, y, x = z % NZ, y % NY, x % NX
    return (z * 2 + x % 2) * 16 + y * 4 + (x // 2) * 2 + c


PLACES = [(z, y, x, c) for z in range(NZ) for y in range(NY) for x in range(NX) for c in range(2)]
SWAP = [(flat(z, y, x, c), flat(z, y, (x // 2) * 2 + c, x % 2)) for z, y, x, c in PLACES]
Z_EDGE = [(flat(z, y, x, c), flat(z + (1 if c else -1), y, x, 1 - c)) for z, y, x, c in PLACES]
C_EDGE = [(flat(z, y, x, c), flat(z, y, x, 1 - c)) for z, y, x, c in PLACES]
PLANE_CORE = [
    [flat(z, y, x, c) for y in range(NY) for x in range(NX)] for z in range(NZ) for c in range(2)
]

def chebyshev_norm(count):
    ratio = (CENTER - 1.0) / HALF_WIDTH
    root = ratio + (ratio * ratio - 1.0) ** 0.5
    return 0.5 * (root**count + root ** (-count))


def params():
    return pltpu.CompilerParams(vmem_limit_bytes=VMEM_LIMIT)


VMEM = pl.BlockSpec(memory_space=pltpu.VMEM)
SMEM = pl.BlockSpec(memory_space=pltpu.SMEM)


def dot_t(a, b):
    return lax.dot_general(a, b, (((1,), (1,)), ((), ())), preferred_element_type=f32)


def dot_n(a, b):
    return lax.dot_general(a, b, (((1,), (0,)), ((), ())), preferred_element_type=f32)


def slab_kernel(x_ref, o_ref):
    o_ref[0] = x_ref[...]


def to_slabs(basis):
    return pl.pallas_call(
        slab_kernel,
        grid=(8,),
        in_specs=[pl.BlockSpec((2, 4, 32, SLAB), lambda d: (0, 0, 0, d))],
        out_specs=pl.BlockSpec((1, 2, 4, 32, SLAB), lambda d: (d, 0, 0, 0, 0)),
        out_shape=jax.ShapeDtypeStruct((8, 2, 4, 32, SLAB), bf16),
        compiler_params=params(),
        name="to_slabs",
    )(basis)


def gram_kernel(r_ref, pot_ref, pts_ref, o_ref):
    comps = [r_ref[:, 32 * k : 32 * k + 32, :].reshape(NB, SLAB) for k in range(4)]
    scaled = (jnp.sqrt(pot_ref[...]) * comps[0].astype(f32)).astype(bf16)
    rows = lax.broadcasted_iota(jnp.int32, (SLAB, 2 * F), 0)
    pick = jnp.where(rows == pts_ref[...], 1.0, 0.0).astype(bf16)
    sign = jnp.where(lax.broadcasted_iota(jnp.int32, (1, 2 * F), 1) < F, 1.0, -1.0)
    value = dot_n(comps[0], pick) * sign
    slope = dot_n(comps[1], pick)
    jump = value.astype(bf16)
    flux = (0.5 * value - 0.25 * slope).astype(bf16)
    for big_i, big_j in ((0, 0), (1, 0), (1, 1)):
        left = slice(256 * big_i, 256 * big_i + 256)
        right = slice(256 * big_j, 256 * big_j + 256)
        kinetic = dot_t(comps[1][left], comps[1][right])
        kinetic = kinetic + dot_t(comps[2][left], comps[2][right])
        kinetic = kinetic + dot_t(comps[3][left], comps[3][right])
        total = (dot_t(scaled[left], scaled[right]) + 0.5 * kinetic) * (1.0 / NG)
        face = dot_t(flux[left], jump[right]) + dot_t(jump[left], flux[right])
        total = total + face * (1.0 / (4.0 * F))
        for i in range(2):
            for j in range(2):
                row, column = 2 * big_i + i, 2 * big_j + j
                if row >= column:
                    place = 128 * (row * (row + 1) // 2 + column)
                    block = total[128 * i : 128 * i + 128, 128 * j : 128 * j + 128]
                    o_ref[place : place + 128, :] = block


def partial_gram(received, potential, points):
    return pl.pallas_call(
        gram_kernel,
        in_specs=[VMEM] * 3,
        out_specs=VMEM,
        out_shape=jax.ShapeDtypeStruct((PACKED, 128), f32),
        compiler_params=params(),
        name="partial_gram",
    )(received, potential, points)


def unpack_kernel(core_ref, x_ref, o_ref):
    for slot in range(2):
        packed = x_ref[:, jnp.bitwise_xor(core_ref[0], slot)].reshape(PACKED, 128)
        for row in range(4):
            for column in range(row + 1):
                place = 128 * (row * (row + 1) // 2 + column)
                block = packed[place : place + 128]
                r, c = pl.ds(128 * row, 128), pl.ds(128 * column, 128)
                o_ref[slot, r, c] = block
                if row > column:
                    o_ref[slot, c, r] = block.astype(f32).T.astype(bf16)


def unpack(core, gathered):
    return pl.pallas_call(
        unpack_kernel,
        in_specs=[SMEM, VMEM],
        out_specs=VMEM,
        out_shape=jax.ShapeDtypeStruct((2, NB, NB), bf16),
        compiler_params=params(),
        name="unpack_diagonal",
    )(core, gathered)


def sides_kernel(flip_ref, x_ref, pts_ref, sign_ref, o_ref):
    chunk = 512
    for slot in range(2):
        block = x_ref[jnp.bitwise_xor(flip_ref[0], slot)].reshape(64, NG)
        points = pts_ref[slot : slot + 1, :]
        found = jnp.zeros((64, 2 * F), f32)
        for part in range(NG // chunk):
            rows = lax.broadcasted_iota(jnp.int32, (chunk, 2 * F), 0) + part * chunk
            pick = jnp.where(rows == points, 1.0, 0.0).astype(bf16)
            found = found + dot_n(block[:, part * chunk : (part + 1) * chunk], pick)
        value = found[:32] * sign_ref[slot : slot + 1, :]
        flux = 0.5 * value - 0.25 * found[32:]
        for side in range(2):
            lanes = slice(F * side, F * side + F)
            o_ref[slot, 2 * side] = flux[:, lanes].astype(bf16)
            o_ref[slot, 2 * side + 1] = value[:, lanes].astype(bf16)


def local_sides(flip, basis, points, signs):
    return pl.pallas_call(
        sides_kernel,
        grid=(1,),
        in_specs=[
            SMEM,
            pl.BlockSpec((2, 2, 32, NG), lambda d: (0, 0, 0, 0)),
            VMEM,
            VMEM,
        ],
        out_specs=VMEM,
        out_shape=jax.ShapeDtypeStruct((2, 4, 32, F), bf16),
        compiler_params=params(),
        name="local_sides",
    )(flip, basis, points, signs)


def couple_kernel(w_ref, z_ref, c_ref, o_ref):
    def pair(ref, *at):
        return ref[(slice(None),) + at].reshape(NB, F)

    def face(a_flux, a_jump, b_flux, b_jump):
        total = dot_t(a_flux, b_jump) + dot_t(a_jump, b_flux)
        return (total * (1.0 / (4.0 * F))).astype(bf16)

    outer = [(pair(w_ref, s, 0), pair(w_ref, s, 1)) for s in range(2)]
    inner = [(pair(w_ref, s, 2), pair(w_ref, s, 3)) for s in range(2)]
    o_ref[0] = face(*inner[0], *inner[1])
    o_ref[1] = face(*inner[1], *inner[0])
    o_ref[2] = face(*outer[0], pair(z_ref, 0), pair(z_ref, 1))
    o_ref[3] = face(*outer[1], pair(c_ref, 0), pair(c_ref, 1))


def couplings(sides, z_sides, c_sides):
    return pl.pallas_call(
        couple_kernel,
        in_specs=[VMEM] * 3,
        out_specs=VMEM,
        out_shape=jax.ShapeDtypeStruct((4, NB, NB), bf16),
        compiler_params=params(),
        name="couplings",
    )(sides, z_sides, c_sides)


def per_device(basis, potential, face_index, face_match, vectors):
    elem = lax.axis_index("elem")
    inner = lax.axis_index("inner")
    x_lo, core, chip = elem % 2, inner % 2, inner // 2
    left_points = jnp.take_along_axis(face_index[:, 0, :], face_match, axis=1)
    right_points = face_index[:, 1, :]

    slabs = to_slabs(basis).reshape(16, 128, SLAB)
    received = lax.all_to_all(slabs, "inner", 0, 0)
    own_points = jnp.concatenate((right_points, left_points), axis=1) - chip * SLAB
    own_points = lax.dynamic_slice(own_points, (core, 0), (1, 2 * F))
    own_potential = lax.dynamic_slice(potential, (core, chip * SLAB), (1, SLAB))
    packed = partial_gram(received, own_potential, own_points)

    lr = jnp.concatenate((left_points, right_points), axis=1)
    rl = jnp.concatenate((right_points, left_points), axis=1)
    slot_points = jnp.where(
        x_lo == 0, jnp.stack((lr[0], rl[1])), jnp.stack((rl[1], lr[0]))
    )
    minus = jnp.repeat(jnp.array([[-1.0, 1.0], [1.0, -1.0]], f32), F, axis=1)
    slot_signs = jnp.where(x_lo == 0, minus, -minus)
    sides = local_sides(x_lo.reshape(1), basis, slot_points, slot_signs)
    sides = lax.ppermute(sides, BOTH, SWAP)
    sides = lax.all_to_all(
        jnp.broadcast_to(sides[None], (16,) + sides.shape),
        BOTH, 0, 0, axis_index_groups=PLANE_CORE,
    )
    z_sides = lax.ppermute(sides[:, 0, 0:2], BOTH, Z_EDGE)
    c_sides = lax.ppermute(sides[:, 1, 0:2], BOTH, C_EDGE)
    couple = couplings(sides, z_sides, c_sides)

    start = [
        lax.ppermute(lax.dynamic_index_in_dim(vectors, x_lo ^ slot, 0, False), BOTH, SWAP)
        for slot in range(2)
    ]

    pieces = lax.all_to_all(packed.reshape(16, PIECE, 128), "inner", 0, 0)
    piece = jnp.sum(pieces.reshape(8, 2, PIECE, 128), axis=0).astype(bf16)
    piece = lax.ppermute(piece, BOTH, SWAP)
    gathered = lax.all_to_all(
        jnp.broadcast_to(piece[None], (16, 2, PIECE, 128)),
        BOTH, 0, 0, axis_index_groups=PLANE_CORE,
    )
    diagonal = unpack(core.reshape(1), gathered)

    def apply_operator(v0, v1):
        z_edge = lax.ppermute(v0, BOTH, Z_EDGE)
        c_edge = lax.ppermute(v1, BOTH, C_EDGE)
        r0 = dot_n(diagonal[0], v0) + dot_n(couple[0], v1)
        r1 = dot_n(diagonal[1], v1) + dot_n(couple[1], v0)
        r1 = r1 + dot_n(couple[3], c_edge)
        r0 = r0 + dot_n(couple[2], z_edge)
        return r0, r1

    previous = [v.astype(f32) for v in start]
    applied = apply_operator(*start)
    current = [(a - CENTER * p) / HALF_WIDTH for a, p in zip(applied, previous)]
    for _ in range(1, STEPS):
        applied = apply_operator(*[c.astype(bf16) for c in current])
        following = [
            2.0 * (a - CENTER * c) / HALF_WIDTH - p for a, c, p in zip(applied, current, previous)
        ]
        previous, current = current, following
    scale = 1.0 / chebyshev_norm(STEPS)
    own = [c * scale for c in current]
    moved = [lax.ppermute(o.astype(bf16), BOTH, SWAP).astype(f32) for o in own]
    result = [jnp.where(x_lo == core, o, m) for o, m in zip(own, moved)]
    return jnp.where(x_lo == 0, jnp.stack(result), jnp.stack(result[::-1]))


def solution(mesh):
    placed = (
        P("elem", None, "inner", None),
        P("elem", None),
        P("elem", None, None),
        P("elem", None),
        P("elem", None, "inner"),
    )
    return jax.shard_map(
        per_device, mesh=mesh, in_specs=placed, out_specs=P("elem", None, "inner"), check_vma=False
    )
```

```python
import jax
import jax.numpy as jnp
from jax import lax
from jax.experimental import pallas as pl
from jax.experimental.pallas import tpu as pltpu
from jax.sharding import PartitionSpec as P

NB = 512
NG = 4096
F = 128
STEPS = 6
CENTER = 5.25
HALF_WIDTH = 2.75
NZ, NY, NX = 8, 4, 4
BOTH = ("elem", "inner")
SLAB = NG // 8
PACKED = 10 * 128
PIECE = PACKED // 16
VMEM_LIMIT = 40 * 1024 * 1024
bf16 = jnp.bfloat16
f32 = jnp.float32


def flat(z, y, x, c):
    z, y, x = z % NZ, y % NY, x % NX
    return (z * 2 + x % 2) * 16 + y * 4 + (x // 2) * 2 + c


PLACES = [(z, y, x, c) for z in range(NZ) for y in range(NY) for x in range(NX) for c in range(2)]


def pair_of(z, c):
    return c if z % 2 else 1 - c


def moved_to(z, y, x, c):
    pair, column = x % 2, c
    return z, y, (x // 2) * 2 + column, pair if z % 2 else 1 - pair


def along(place, axis, step):
    z, y, x, c = place
    return (z, y + step, x, c) if c == axis else (z, y, x + step, c)


def pairs_of(move):
    return [(flat(*p), flat(*move(*p))) for p in PLACES]


SWAP = pairs_of(moved_to)
BACK = [(j, i) for i, j in SWAP]
Z_EDGE = pairs_of(lambda z, y, x, c: (z + (1 if pair_of(z, c) else -1), y, x, c))
C_EDGE = pairs_of(lambda z, y, x, c: (z, y, x, 1 - c))
FIRST = [pairs_of(lambda *p: along(moved_to(*p), 0, -r)) for r in range(4)]
SECOND = [pairs_of(lambda *p: along(p, 1, -q)) for q in range(4)]
PLANE_CORE = [
    [flat(z, y, x, c) for y in range(NY) for x in range(NX)]
    for z in range(NZ)
    for c in range(2)
]


def chebyshev_norm(count):
    ratio = (CENTER - 1.0) / HALF_WIDTH
    root = ratio + (ratio * ratio - 1.0) ** 0.5
    return 0.5 * (root**count + root ** (-count))


def params():
    return pltpu.CompilerParams(vmem_limit_bytes=VMEM_LIMIT)


VMEM = pl.BlockSpec(memory_space=pltpu.VMEM)
SMEM = pl.BlockSpec(memory_space=pltpu.SMEM)


def dot_t(a, b):
    return lax.dot_general(a, b, (((1,), (1,)), ((), ())), preferred_element_type=f32)


def dot_n(a, b):
    return lax.dot_general(a, b, (((1,), (0,)), ((), ())), preferred_element_type=f32)


def slab_kernel(x_ref, o_ref, sems):
    copies = [
        pltpu.make_async_copy(
            x_ref.at[:, :, :, pl.ds(SLAB * d, SLAB)], o_ref.at[d], sems.at[d]
        )
        for d in range(8)
    ]
    for copy in copies:
        copy.start()
    for copy in copies:
        copy.wait()


def to_slabs(basis):
    return pl.pallas_call(
        slab_kernel,
        in_specs=[pl.BlockSpec(memory_space=pl.ANY)],
        out_specs=pl.BlockSpec(memory_space=pl.ANY),
        out_shape=jax.ShapeDtypeStruct((8, 2, 4, 32, SLAB), bf16),
        scratch_shapes=[pltpu.SemaphoreType.DMA((8,))],
        compiler_params=pltpu.CompilerParams(vmem_limit_bytes=58 * 1024 * 1024),
        name="to_slabs",
    )(basis)


def gram_kernel(r_ref, pot_ref, pts_ref, o_ref):
    comps = [r_ref[:, 32 * k : 32 * k + 32, :].reshape(NB, SLAB) for k in range(4)]
    scaled = (jnp.sqrt(pot_ref[...]) * comps[0].astype(f32)).astype(bf16)
    rows = lax.broadcasted_iota(jnp.int32, (SLAB, 2 * F), 0)
    pick = jnp.where(rows == pts_ref[...], 1.0, 0.0).astype(bf16)
    sign = jnp.where(lax.broadcasted_iota(jnp.int32, (1, 2 * F), 1) < F, 1.0, -1.0)
    value = dot_n(comps[0], pick) * sign
    slope = dot_n(comps[1], pick)
    jump = value.astype(bf16)
    flux = (0.5 * value - 0.25 * slope).astype(bf16)
    for big_i, big_j in ((0, 0), (1, 0), (1, 1)):
        left = slice(256 * big_i, 256 * big_i + 256)
        right = slice(256 * big_j, 256 * big_j + 256)
        kinetic = dot_t(comps[1][left], comps[1][right])
        kinetic = kinetic + dot_t(comps[2][left], comps[2][right])
        kinetic = kinetic + dot_t(comps[3][left], comps[3][right])
        total = (dot_t(scaled[left], scaled[right]) + 0.5 * kinetic) * (1.0 / NG)
        face = dot_t(flux[left], jump[right]) + dot_t(jump[left], flux[right])
        total = total + face * (1.0 / (4.0 * F))
        for i in range(2):
            for j in range(2):
                row, column = 2 * big_i + i, 2 * big_j + j
                if row >= column:
                    place = 128 * (row * (row + 1) // 2 + column)
                    block = total[128 * i : 128 * i + 128, 128 * j : 128 * j + 128]
                    o_ref[place : place + 128, :] = block


def partial_gram(received, potential, points):
    return pl.pallas_call(
        gram_kernel,
        in_specs=[VMEM] * 3,
        out_specs=VMEM,
        out_shape=jax.ShapeDtypeStruct((PACKED, 128), f32),
        compiler_params=params(),
        name="partial_gram",
    )(received, potential, points)


def first_kernel(at_ref, x_ref, v_ref, part_ref, d_ref, new_ref, low_ref):
    packed = x_ref[:, at_ref[0]].reshape(PACKED, 128)
    for row in range(4):
        for column in range(row + 1):
            place = 128 * (row * (row + 1) // 2 + column)
            block = packed[place : place + 128]
            r, c = pl.ds(128 * row, 128), pl.ds(128 * column, 128)
            d_ref[r, c] = block
            if row > column:
                d_ref[c, r] = block.astype(f32).T.astype(bf16)
    v = v_ref[...]
    applied = dot_n(d_ref[...], v) + part_ref[...]
    new = (applied - CENTER * v.astype(f32)) * (1.0 / HALF_WIDTH)
    new_ref[...] = new
    low_ref[...] = new.astype(bf16)


def first_step(at, gathered, v, part):
    return pl.pallas_call(
        first_kernel,
        in_specs=[SMEM] + [VMEM] * 3,
        out_specs=[VMEM] * 3,
        out_shape=[
            jax.ShapeDtypeStruct((NB, NB), bf16),
            jax.ShapeDtypeStruct(v.shape, f32),
            jax.ShapeDtypeStruct(v.shape, bf16),
        ],
        compiler_params=params(),
        name="first_step",
    )(at, gathered, v, part)


def last_kernel(flags_ref, own0_ref, own1_ref, moved0_ref, moved1_ref, o_ref):
    flip = flags_ref[0]

    @pl.when(flags_ref[1] == 1)
    def _():
        o_ref[flip] = own0_ref[...]
        o_ref[1 - flip] = own1_ref[...]

    @pl.when(flags_ref[1] == 0)
    def _():
        o_ref[flip] = moved0_ref[...].astype(f32)
        o_ref[1 - flip] = moved1_ref[...].astype(f32)


def last_placing(flags, own, moved):
    return pl.pallas_call(
        last_kernel,
        in_specs=[SMEM] + [VMEM] * 4,
        out_specs=VMEM,
        out_shape=jax.ShapeDtypeStruct((2,) + own[0].shape, f32),
        compiler_params=params(),
        name="last_placing",
    )(flags, *own, *moved)


def sides_kernel(flip_ref, x_ref, pts_ref, sign_ref, o_ref):
    chunk = 512
    for slot in range(2):
        block = x_ref[jnp.bitwise_xor(flip_ref[0], slot)].reshape(64, NG)
        points = pts_ref[slot : slot + 1, :]
        found = jnp.zeros((64, 2 * F), f32)
        for part in range(NG // chunk):
            rows = lax.broadcasted_iota(jnp.int32, (chunk, 2 * F), 0) + part * chunk
            pick = jnp.where(rows == points, 1.0, 0.0).astype(bf16)
            found = found + dot_n(block[:, part * chunk : (part + 1) * chunk], pick)
        value = found[:32] * sign_ref[slot : slot + 1, :]
        flux = 0.5 * value - 0.25 * found[32:]
        for side in range(2):
            lanes = slice(F * side, F * side + F)
            o_ref[slot, 2 * side] = flux[:, lanes].astype(bf16)
            o_ref[slot, 2 * side + 1] = value[:, lanes].astype(bf16)


def local_sides(flip, basis, points, signs):
    return pl.pallas_call(
        sides_kernel,
        grid=(1,),
        in_specs=[
            SMEM,
            pl.BlockSpec((2, 2, 32, NG), lambda d: (0, 0, 0, 0)),
            VMEM,
            VMEM,
        ],
        out_specs=VMEM,
        out_shape=jax.ShapeDtypeStruct((2, 4, 32, F), bf16),
        compiler_params=params(),
        name="local_sides",
    )(flip, basis, points, signs)


def face(a_flux, a_jump, b_flux, b_jump):
    total = dot_t(a_flux, b_jump) + dot_t(a_jump, b_flux)
    return (total * (1.0 / (4.0 * F))).astype(bf16)


def arrange_kernel(rows_ref, b0, b1, b2, b3, z_ref, c_ref, m01_ref, m10_ref, inner):
    outer = (z_ref, c_ref)
    for q, b_ref in enumerate((b0, b1, b2, b3)):
        for r in range(4):
            rows = pl.ds(pl.multiple_of(rows_ref[4 * q + r], 32), 32)
            for slot in range(2):
                for k in range(2):
                    outer[slot][k, rows, :] = b_ref[r, slot, k]
                    inner[slot, k, rows, :] = b_ref[r, slot, 2 + k]
    m01_ref[...] = face(inner[0, 0], inner[0, 1], inner[1, 0], inner[1, 1])
    m10_ref[...] = face(inner[1, 0], inner[1, 1], inner[0, 0], inner[0, 1])


def arrange(rows, blocks):
    return pl.pallas_call(
        arrange_kernel,
        in_specs=[SMEM] + [VMEM] * 4,
        out_specs=[VMEM] * 4,
        out_shape=[jax.ShapeDtypeStruct((2, NB, F), bf16)] * 2
        + [jax.ShapeDtypeStruct((NB, NB), bf16)] * 2,
        scratch_shapes=[pltpu.VMEM((2, 2, NB, F), bf16)],
        compiler_params=params(),
        name="arrange_sides",
    )(rows, *blocks)


def edge_kernel(z_ref, zr_ref, c_ref, cr_ref, mz_ref, mc_ref):
    mz_ref[...] = face(z_ref[0], z_ref[1], zr_ref[0], zr_ref[1])
    mc_ref[...] = face(c_ref[0], c_ref[1], cr_ref[0], cr_ref[1])


def edge_couplings(*sides):
    return pl.pallas_call(
        edge_kernel,
        in_specs=[VMEM] * 4,
        out_specs=[VMEM] * 2,
        out_shape=[jax.ShapeDtypeStruct((NB, NB), bf16)] * 2,
        compiler_params=params(),
        name="edge_couplings",
    )(*sides)


def per_device(basis, potential, face_index, face_match, vectors):
    elem = lax.axis_index("elem")
    inner = lax.axis_index("inner")
    x_lo, core, chip = elem % 2, inner % 2, inner // 2
    z_even = 1 - (elem // 2) % 2
    pair = core ^ z_even

    slabs = to_slabs(basis).reshape(16, 128, SLAB)
    received = lax.all_to_all(slabs, "inner", 0, 0)

    start = lax.ppermute(vectors, BOTH, SWAP)

    hits = face_match[:, :, None] == lax.broadcasted_iota(jnp.int32, (1, 1, F), 2)
    left_points = jnp.sum(jnp.where(hits, face_index[:, None, 0, :], 0), axis=2)
    right_points = face_index[:, 1, :]
    own_points = jnp.concatenate((right_points, left_points), axis=1) - chip * SLAB
    own_points = lax.dynamic_slice(own_points, (core, 0), (1, 2 * F))
    own_potential = lax.dynamic_slice(potential, (core, chip * SLAB), (1, SLAB))

    lr = jnp.concatenate((left_points, right_points), axis=1)
    rl = jnp.concatenate((right_points, left_points), axis=1)
    slot_points = jnp.where(
        x_lo == 0, jnp.stack((lr[0], rl[1])), jnp.stack((rl[1], lr[0]))
    )
    minus = jnp.repeat(jnp.array([[-1.0, 1.0], [1.0, -1.0]], f32), F, axis=1)
    slot_signs = jnp.where(x_lo == 0, minus, -minus)
    sides = local_sides(x_lo.reshape(1), basis, slot_points, slot_signs)
    sides = jnp.stack([lax.ppermute(sides, BOTH, perm) for perm in FIRST])
    blocks = [sides] + [lax.ppermute(sides, BOTH, perm) for perm in SECOND[1:]]
    my_y, my_x = inner // 4, 2 * ((inner // 2) % 2) + x_lo
    q = lax.broadcasted_iota(jnp.int32, (16,), 0) // 4
    r = lax.broadcasted_iota(jnp.int32, (16,), 0) % 4
    from_y = (my_y + jnp.where(core == 0, r, q)) % 4
    from_x = (my_x + jnp.where(core == 0, q, r)) % 4
    rows = 32 * (4 * from_y + from_x)
    z_sides, c_sides, m01, m10 = arrange(rows, blocks)
    mz, mc = edge_couplings(
        z_sides, lax.ppermute(z_sides, BOTH, Z_EDGE),
        c_sides, lax.ppermute(c_sides, BOTH, C_EDGE),
    )

    v0 = lax.dynamic_index_in_dim(start, pair, 0, False)
    v1 = lax.dynamic_index_in_dim(start, 1 - pair, 0, False)

    def edges(v0, v1):
        return lax.ppermute(v0, BOTH, Z_EDGE), lax.ppermute(v1, BOTH, C_EDGE)

    zv, cv = edges(v0, v1)
    part0 = dot_n(m01, v1) + dot_n(mz, zv)
    part1 = dot_n(m10, v0) + dot_n(mc, cv)

    packed = partial_gram(received, own_potential, own_points)
    pieces = packed.astype(jnp.float16).reshape(16, PIECE, 128)
    pieces = lax.all_to_all(pieces, "inner", 0, 0)
    piece = jnp.sum(pieces.reshape(8, 2, PIECE, 128).astype(f32), axis=0).astype(bf16)
    piece = lax.ppermute(piece, BOTH, SWAP)
    gathered = lax.all_to_all(
        jnp.broadcast_to(piece[None], (16, 2, PIECE, 128)),
        BOTH, 0, 0, axis_index_groups=PLANE_CORE,
    )

    d0, new0, low0 = first_step(pair.reshape(1), gathered, v0, part0)
    d1, new1, low1 = first_step((1 - pair).reshape(1), gathered, v1, part1)
    previous = [v0.astype(f32), v1.astype(f32)]
    current = [new0, new1]
    low = [low0, low1]
    for _ in range(1, STEPS):
        zv, cv = edges(*low)
        a1 = dot_n(d1, low[1]) + dot_n(m10, low[0]) + dot_n(mc, cv)
        a0 = dot_n(d0, low[0]) + dot_n(m01, low[1]) + dot_n(mz, zv)
        following = [
            2.0 * (a - CENTER * c) / HALF_WIDTH - p for a, c, p in zip((a0, a1), current, previous)
        ]
        previous, current = current, following
        low = [c.astype(bf16) for c in current]
    scale = 1.0 / chebyshev_norm(STEPS)
    own = [c * scale for c in current]
    moved = [lax.ppermute(o.astype(bf16), BOTH, BACK) for o in own]
    flags = jnp.stack((x_lo, ((x_lo == core) & (z_even == 0)).astype(jnp.int32)))
    return last_placing(flags, own, moved)


def solution(mesh):
    placed = (
        P("elem", None, "inner", None),
        P("elem", None),
        P("elem", None, None),
        P("elem", None),
        P("elem", None, "inner"),
    )
    return jax.shard_map(
        per_device, mesh=mesh, in_specs=placed, out_specs=P("elem", None, "inner"), check_vma=False
    )
```

```python
import jax
import jax.numpy as jnp
from jax import lax
from jax.experimental import pallas as pl
from jax.experimental.pallas import tpu as pltpu
from jax.sharding import PartitionSpec as P

NB = 512
NG = 4096
F = 128
STEPS = 6
CENTER = 5.25
HALF_WIDTH = 2.75
NZ, NY, NX = 8, 4, 4
BOTH = ("elem", "inner")
SLAB = NG // 8
PACKED = 10 * 128
PIECE = PACKED // 8
bf16 = jnp.bfloat16
f32 = jnp.float32


def flat(z, y, x, c):
    z, y, x = z % NZ, y % NY, x % NX
    return (z * 2 + x % 2) * 16 + y * 4 + (x // 2) * 2 + c


PLACES = [(z, y, x, c) for z in range(NZ) for y in range(NY) for x in range(NX) for c in range(2)]


def pair_of(z, c):
    return c if z % 2 else 1 - c


def moved_to(z, y, x, c):
    pair, column = x % 2, c
    return z, y, (x // 2) * 2 + column, pair if z % 2 else 1 - pair


def along(place, axis, step):
    z, y, x, c = place
    return (z, y + step, x, c) if c == axis else (z, y, x + step, c)


def pairs_of(move):
    return [(flat(*p), flat(*move(*p))) for p in PLACES]


SWAP = pairs_of(moved_to)
BACK = [(j, i) for i, j in SWAP]
Z_EDGE = pairs_of(lambda z, y, x, c: (z + (1 if pair_of(z, c) else -1), y, x, c))
C_EDGE = pairs_of(lambda z, y, x, c: (z, y, x, 1 - c))
FIRST = [pairs_of(lambda *p: along(moved_to(*p), 0, -r)) for r in range(4)]
SECOND = [pairs_of(lambda *p: along(p, 1, -q)) for q in range(4)]
CHIPS = [[c + 2 * k for k in range(8)] for c in range(2)]


def chebyshev_norm(count):
    ratio = (CENTER - 1.0) / HALF_WIDTH
    root = ratio + (ratio * ratio - 1.0) ** 0.5
    return 0.5 * (root**count + root ** (-count))


def params(mib=16):
    return pltpu.CompilerParams(vmem_limit_bytes=mib * 1024 * 1024)


VMEM = pl.BlockSpec(memory_space=pltpu.VMEM)
SMEM = pl.BlockSpec(memory_space=pltpu.SMEM)


def dot_t(a, b):
    return lax.dot_general(a, b, (((1,), (1,)), ((), ())), preferred_element_type=f32)


def dot_n(a, b):
    return lax.dot_general(a, b, (((1,), (0,)), ((), ())), preferred_element_type=f32)


def slab_kernel(x_ref, o_ref):
    o_ref[0] = x_ref[...]


def to_slabs(basis):
    return pl.pallas_call(
        slab_kernel,
        grid=(8,),
        in_specs=[pl.BlockSpec((2, 4, 32, SLAB), lambda d: (0, 0, 0, d))],
        out_specs=pl.BlockSpec((1, 2, 4, 32, SLAB), lambda d: (d, 0, 0, 0, 0)),
        out_shape=jax.ShapeDtypeStruct((8, 2, 4, 32, SLAB), bf16),
        compiler_params=params(58),
        name="to_slabs",
    )(basis)


def gram_kernel(at_ref, r_ref, pot_ref, pts_ref, o_ref):
    comps = [r_ref[:, 32 * k : 32 * k + 32, :].reshape(NB, SLAB) for k in range(4)]
    lanes = pl.ds(pl.multiple_of(at_ref[1] * SLAB, SLAB), SLAB)
    potential = jnp.where(at_ref[0] == 0, pot_ref[0:1, lanes], pot_ref[1:2, lanes])
    scaled = (jnp.sqrt(potential) * comps[0].astype(f32)).astype(bf16)
    rows = lax.broadcasted_iota(jnp.int32, (SLAB, 2 * F), 0)
    pick = jnp.where(rows == pts_ref[...], 1.0, 0.0).astype(bf16)
    sign = jnp.where(lax.broadcasted_iota(jnp.int32, (1, 2 * F), 1) < F, 1.0, -1.0)
    value = dot_n(comps[0], pick) * sign
    slope = dot_n(comps[1], pick)
    jump = value.astype(bf16)
    flux = (0.5 * value - 0.25 * slope).astype(bf16)
    for big_i, big_j in ((0, 0), (1, 0), (1, 1)):
        left = slice(256 * big_i, 256 * big_i + 256)
        right = slice(256 * big_j, 256 * big_j + 256)
        kinetic = dot_t(comps[1][left], comps[1][right])
        kinetic = kinetic + dot_t(comps[2][left], comps[2][right])
        kinetic = kinetic + dot_t(comps[3][left], comps[3][right])
        total = (dot_t(scaled[left], scaled[right]) + 0.5 * kinetic) * (1.0 / NG)
        face = dot_t(flux[left], jump[right]) + dot_t(jump[left], flux[right])
        total = total + face * (1.0 / (4.0 * F))
        for i in range(2):
            for j in range(2):
                row, column = 2 * big_i + i, 2 * big_j + j
                if row >= column:
                    place = 128 * (row * (row + 1) // 2 + column)
                    block = total[128 * i : 128 * i + 128, 128 * j : 128 * j + 128]
                    o_ref[place : place + 128, :] = block


def partial_gram(at, received, potential, points):
    return pl.pallas_call(
        gram_kernel,
        in_specs=[SMEM] + [VMEM] * 3,
        out_specs=VMEM,
        out_shape=jax.ShapeDtypeStruct((PACKED, 128), f32),
        compiler_params=params(32),
        name="partial_gram",
    )(at, received, potential, points)


def unpack(packed, d_ref):
    for row in range(4):
        for column in range(row + 1):
            place = 128 * (row * (row + 1) // 2 + column)
            block = packed[place : place + 128, :]
            r, c = pl.ds(128 * row, 128), pl.ds(128 * column, 128)
            d_ref[r, c] = block
            if row > column:
                d_ref[c, r] = block.astype(f32).T.astype(bf16)


def begin(d_ref, v_ref, part_ref, new_ref, low_ref):
    v = v_ref[...]
    applied = dot_n(d_ref[...], v) + part_ref[...]
    new = (applied - CENTER * v.astype(f32)) * (1.0 / HALF_WIDTH)
    new_ref[...] = new
    low_ref[...] = new.astype(bf16)


def first_kernel(at_ref, b0, b1, b2, b3, v_ref, part_ref, d_ref, new_ref, low_ref, packed_ref):
    for q, b_ref in enumerate((b0, b1, b2, b3)):
        for r in range(4):
            k = 4 * q + r
            rows = pl.ds(pl.multiple_of(at_ref[1, k], PIECE), PIECE)
            packed_ref[at_ref[0, k], rows, :] = b_ref[r]
    unpack(packed_ref.at[0], d_ref)
    begin(d_ref, v_ref, part_ref, new_ref, low_ref)


def second_kernel(packed_ref, v_ref, part_ref, d_ref, new_ref, low_ref):
    unpack(packed_ref.at[1], d_ref)
    begin(d_ref, v_ref, part_ref, new_ref, low_ref)


def first_step(at, blocks, v0, v1, part0, part1):
    shapes = [
        jax.ShapeDtypeStruct((NB, NB), bf16),
        jax.ShapeDtypeStruct(v0.shape, f32),
        jax.ShapeDtypeStruct(v0.shape, bf16),
    ]
    *first, packed = pl.pallas_call(
        first_kernel,
        in_specs=[SMEM] + [VMEM] * 6,
        out_specs=[VMEM] * 4,
        out_shape=shapes + [jax.ShapeDtypeStruct((2, PACKED, 128), bf16)],
        compiler_params=params(),
        name="first_step_slot0",
    )(at, *blocks, v0, part0)
    second = pl.pallas_call(
        second_kernel,
        in_specs=[VMEM] * 3,
        out_specs=[VMEM] * 3,
        out_shape=shapes,
        compiler_params=params(),
        name="first_step_slot1",
    )(packed, v1, part1)
    return first, second


def last_kernel(flip_ref, m0_ref, m1_ref, o_ref):
    flip = flip_ref[0]
    o_ref[flip] = m0_ref[...].astype(f32)
    o_ref[1 - flip] = m1_ref[...].astype(f32)


def last_placing(flip, moved):
    rows, columns = moved[0].shape
    part = pl.BlockSpec((rows // 4, columns), lambda i: (i, 0))
    return pl.pallas_call(
        last_kernel,
        grid=(4,),
        in_specs=[SMEM, part, part],
        out_specs=pl.BlockSpec((2, rows // 4, columns), lambda i: (0, i, 0)),
        out_shape=jax.ShapeDtypeStruct((2, rows, columns), f32),
        compiler_params=params(),
        name="last_placing",
    )(flip, *moved)


def sides_kernel(flip_ref, x_ref, pts_ref, sign_ref, o_ref):
    chunk = 512
    for slot in range(2):
        block = x_ref[jnp.bitwise_xor(flip_ref[0], slot)].reshape(64, NG)
        points = pts_ref[slot : slot + 1, :]
        found = jnp.zeros((64, 2 * F), f32)
        for part in range(NG // chunk):
            rows = lax.broadcasted_iota(jnp.int32, (chunk, 2 * F), 0) + part * chunk
            pick = jnp.where(rows == points, 1.0, 0.0).astype(bf16)
            found = found + dot_n(block[:, part * chunk : (part + 1) * chunk], pick)
        value = found[:32] * sign_ref[slot : slot + 1, :]
        flux = 0.5 * value - 0.25 * found[32:]
        for side in range(2):
            lanes = slice(F * side, F * side + F)
            o_ref[slot, 2 * side] = flux[:, lanes].astype(bf16)
            o_ref[slot, 2 * side + 1] = value[:, lanes].astype(bf16)


def local_sides(flip, basis, points, signs):
    return pl.pallas_call(
        sides_kernel,
        grid=(1,),
        in_specs=[
            SMEM,
            pl.BlockSpec((2, 2, 32, NG), lambda d: (0, 0, 0, 0)),
            VMEM,
            VMEM,
        ],
        out_specs=VMEM,
        out_shape=jax.ShapeDtypeStruct((2, 4, 32, F), bf16),
        compiler_params=params(),
        name="local_sides",
    )(flip, basis, points, signs)


def face(a_flux, a_jump, b_flux, b_jump):
    total = dot_t(a_flux, b_jump) + dot_t(a_jump, b_flux)
    return (total * (1.0 / (4.0 * F))).astype(bf16)


def arrange_kernel(rows_ref, b0, b1, b2, b3, z_ref, c_ref, m01_ref, m10_ref, inner):
    outer = (z_ref, c_ref)
    for q, b_ref in enumerate((b0, b1, b2, b3)):
        for r in range(4):
            rows = pl.ds(pl.multiple_of(rows_ref[4 * q + r], 32), 32)
            for slot in range(2):
                for k in range(2):
                    outer[slot][k, rows, :] = b_ref[r, slot, k]
                    inner[slot, k, rows, :] = b_ref[r, slot, 2 + k]
    m01_ref[...] = face(inner[0, 0], inner[0, 1], inner[1, 0], inner[1, 1])
    m10_ref[...] = face(inner[1, 0], inner[1, 1], inner[0, 0], inner[0, 1])


def arrange(rows, blocks):
    return pl.pallas_call(
        arrange_kernel,
        in_specs=[SMEM] + [VMEM] * 4,
        out_specs=[VMEM] * 4,
        out_shape=[jax.ShapeDtypeStruct((2, NB, F), bf16)] * 2
        + [jax.ShapeDtypeStruct((NB, NB), bf16)] * 2,
        scratch_shapes=[pltpu.VMEM((2, 2, NB, F), bf16)],
        compiler_params=params(),
        name="arrange_sides",
    )(rows, *blocks)


def edge_kernel(z_ref, zr_ref, c_ref, cr_ref, mz_ref, mc_ref):
    mz_ref[...] = face(z_ref[0], z_ref[1], zr_ref[0], zr_ref[1])
    mc_ref[...] = face(c_ref[0], c_ref[1], cr_ref[0], cr_ref[1])


def edge_couplings(*sides):
    return pl.pallas_call(
        edge_kernel,
        in_specs=[VMEM] * 4,
        out_specs=[VMEM] * 2,
        out_shape=[jax.ShapeDtypeStruct((NB, NB), bf16)] * 2,
        compiler_params=params(),
        name="edge_couplings",
    )(*sides)


def gather_plane(x):
    first = jnp.stack([lax.ppermute(x, BOTH, perm) for perm in FIRST])
    return [first] + [lax.ppermute(first, BOTH, perm) for perm in SECOND[1:]]


def per_device(basis, potential, face_index, face_match, vectors):
    elem = lax.axis_index("elem")
    inner = lax.axis_index("inner")
    x_lo, core, chip = elem % 2, inner % 2, inner // 2
    z_even = 1 - (elem // 2) % 2
    pair = core ^ z_even

    slabs = to_slabs(basis).reshape(16, 128, SLAB)
    received = lax.all_to_all(slabs, "inner", 0, 0)

    hits = face_match[:, :, None] == lax.broadcasted_iota(jnp.int32, (1, 1, F), 2)
    left_points = jnp.sum(jnp.where(hits, face_index[:, None, 0, :], 0), axis=2)
    right_points = face_index[:, 1, :]
    own_points = jnp.concatenate((right_points, left_points), axis=1) - chip * SLAB
    own_points = lax.dynamic_slice(own_points, (core, 0), (1, 2 * F))

    lr = jnp.concatenate((left_points, right_points), axis=1)
    rl = jnp.concatenate((right_points, left_points), axis=1)
    slot_points = jnp.where(
        x_lo == 0, jnp.stack((lr[0], rl[1])), jnp.stack((rl[1], lr[0]))
    )
    minus = jnp.repeat(jnp.array([[-1.0, 1.0], [1.0, -1.0]], f32), F, axis=1)
    slot_signs = jnp.where(x_lo == 0, minus, -minus)
    sides = local_sides(x_lo.reshape(1), basis, slot_points, slot_signs)
    blocks = gather_plane(sides)
    my_y, my_x = inner // 4, 2 * ((inner // 2) % 2) + x_lo
    q = lax.broadcasted_iota(jnp.int32, (16,), 0) // 4
    r = lax.broadcasted_iota(jnp.int32, (16,), 0) % 4
    from_y = (my_y + jnp.where(core == 0, r, q)) % 4
    from_x = (my_x + jnp.where(core == 0, q, r)) % 4
    rows = 32 * (4 * from_y + from_x)
    pieces_at = jnp.stack(((from_x % 2) ^ pair, PIECE * (2 * from_y + from_x // 2)))
    z_sides, c_sides, m01, m10 = arrange(rows, blocks)
    mz, mc = edge_couplings(
        z_sides, lax.ppermute(z_sides, BOTH, Z_EDGE),
        c_sides, lax.ppermute(c_sides, BOTH, C_EDGE),
    )

    packed = partial_gram(jnp.stack((core, chip)), received, potential, own_points)
    pieces = lax.all_to_all(
        packed.reshape(8, PIECE, 128), "inner", 0, 0, axis_index_groups=CHIPS
    )

    vectors, _ = lax.optimization_barrier((vectors, packed))
    start = lax.ppermute(vectors, BOTH, SWAP)
    v0 = lax.dynamic_index_in_dim(start, pair, 0, False)
    v1 = lax.dynamic_index_in_dim(start, 1 - pair, 0, False)

    def edges(v0, v1):
        return lax.ppermute(v0, BOTH, Z_EDGE), lax.ppermute(v1, BOTH, C_EDGE)

    zv, cv = edges(v0, v1)
    part0 = dot_n(m01, v1) + dot_n(mz, zv)
    part1 = dot_n(m10, v0) + dot_n(mc, cv)

    piece = jnp.sum(pieces, axis=0).astype(bf16)
    gathered = gather_plane(piece)
    (d0, new0, low0), (d1, new1, low1) = first_step(pieces_at, gathered, v0, v1, part0, part1)
    previous = [v0.astype(f32), v1.astype(f32)]
    current = [new0, new1]
    low = [low0, low1]
    scale = 1.0 / chebyshev_norm(STEPS)
    for step in range(1, STEPS):
        zv, cv = edges(*low)

        def following(a, at):
            return 2.0 * (a - CENTER * current[at]) / HALF_WIDTH - previous[at]

        new1 = following(dot_n(d1, low[1]) + dot_n(m10, low[0]) + dot_n(mc, cv), 1)
        if step == STEPS - 1:
            last1 = (new1 * scale).astype(bf16)
            moved1 = lax.ppermute(last1, BOTH, BACK)
            zv, _ = lax.optimization_barrier((zv, last1))
        new0 = following(dot_n(d0, low[0]) + dot_n(m01, low[1]) + dot_n(mz, zv), 0)
        previous, current = current, [new0, new1]
        low = [c.astype(bf16) for c in current]
    moved = [lax.ppermute((new0 * scale).astype(bf16), BOTH, BACK), moved1]
    return last_placing(x_lo.reshape(1), moved)


def solution(mesh):
    placed = (
        P("elem", None, "inner", None),
        P("elem", None),
        P("elem", None, None),
        P("elem", None),
        P("elem", None, "inner"),
    )
    return jax.shard_map(
        per_device, mesh=mesh, in_specs=placed, out_specs=P("elem", None, "inner"), check_vma=False
    )
```

```python
import jax
import jax.numpy as jnp
from jax import lax
from jax.experimental import pallas as pl
from jax.experimental.pallas import tpu as pltpu
from jax.sharding import PartitionSpec as P

NB = 512
NG = 4096
F = 128
STEPS = 6
CENTER = 5.25
HALF_WIDTH = 2.75
NZ, NY, NX = 8, 4, 4
BOTH = ("elem", "inner")
SLAB = NG // 8
PACKED = 10 * 128
PIECE = PACKED // 8
bf16 = jnp.bfloat16
f32 = jnp.float32


def flat(z, y, x, c):
    z, y, x = z % NZ, y % NY, x % NX
    return (z * 2 + x % 2) * 16 + y * 4 + (x // 2) * 2 + c


PLACES = [(z, y, x, c) for z in range(NZ) for y in range(NY) for x in range(NX) for c in range(2)]


def pair_of(z, c):
    return c if z % 2 else 1 - c


def moved_to(z, y, x, c):
    pair, column = x % 2, c
    return z, y, (x // 2) * 2 + column, pair if z % 2 else 1 - pair


def along(place, axis, step):
    z, y, x, c = place
    return (z, y + step, x, c) if c == axis else (z, y, x + step, c)


def pairs_of(move):
    return [(flat(*p), flat(*move(*p))) for p in PLACES]


SWAP = pairs_of(moved_to)
BACK = [(j, i) for i, j in SWAP]
Z_EDGE = pairs_of(lambda z, y, x, c: (z + (1 if pair_of(z, c) else -1), y, x, c))
C_EDGE = pairs_of(lambda z, y, x, c: (z, y, x, 1 - c))
FIRST = [pairs_of(lambda *p: along(moved_to(*p), 0, -r)) for r in range(4)]
SECOND = [pairs_of(lambda *p: along(p, 1, -q)) for q in range(4)]
CHIPS = [[c + 2 * k for k in range(8)] for c in range(2)]


def chebyshev_norm(count):
    ratio = (CENTER - 1.0) / HALF_WIDTH
    root = ratio + (ratio * ratio - 1.0) ** 0.5
    return 0.5 * (root**count + root ** (-count))


def params(mib=16):
    return pltpu.CompilerParams(vmem_limit_bytes=mib * 1024 * 1024)


VMEM = pl.BlockSpec(memory_space=pltpu.VMEM)
SMEM = pl.BlockSpec(memory_space=pltpu.SMEM)


TINY = pl.CostEstimate(flops=1, bytes_accessed=1, transcendentals=0)


def dot_t(a, b):
    return lax.dot_general(a, b, (((1,), (1,)), ((), ())), preferred_element_type=f32)


def dot_n(a, b):
    return lax.dot_general(a, b, (((1,), (0,)), ((), ())), preferred_element_type=f32)


def slab_kernel(x_ref, o_ref):
    o_ref[0] = x_ref[...]


def to_slabs(basis):
    return pl.pallas_call(
        slab_kernel,
        grid=(8,),
        in_specs=[pl.BlockSpec((2, 4, 32, SLAB), lambda d: (0, 0, 0, d))],
        out_specs=pl.BlockSpec((1, 2, 4, 32, SLAB), lambda d: (d, 0, 0, 0, 0)),
        out_shape=jax.ShapeDtypeStruct((8, 2, 4, 32, SLAB), bf16),
        compiler_params=params(40),
        cost_estimate=pl.CostEstimate(flops=0, bytes_accessed=1 << 26, transcendentals=0),
        name="to_slabs",
    )(basis)


def gram_kernel(at_ref, r_ref, pot_ref, pts_ref, o_ref):
    comps = [r_ref[:, 32 * k : 32 * k + 32, :].reshape(NB, SLAB) for k in range(4)]
    lanes = pl.ds(pl.multiple_of(at_ref[1] * SLAB, SLAB), SLAB)
    potential = jnp.where(at_ref[0] == 0, pot_ref[0:1, lanes], pot_ref[1:2, lanes])
    scaled = (jnp.sqrt(potential) * comps[0].astype(f32)).astype(bf16)
    rows = lax.broadcasted_iota(jnp.int32, (SLAB, 2 * F), 0)
    pick = jnp.where(rows == pts_ref[...], 1.0, 0.0).astype(bf16)
    sign = jnp.where(lax.broadcasted_iota(jnp.int32, (1, 2 * F), 1) < F, 1.0, -1.0)
    value = dot_n(comps[0], pick) * sign
    slope = dot_n(comps[1], pick)
    jump = value.astype(bf16)
    flux = (0.5 * value - 0.25 * slope).astype(bf16)
    for big_i, big_j in ((0, 0), (1, 0), (1, 1)):
        left = slice(256 * big_i, 256 * big_i + 256)
        right = slice(256 * big_j, 256 * big_j + 256)
        kinetic = dot_t(comps[1][left], comps[1][right])
        kinetic = kinetic + dot_t(comps[2][left], comps[2][right])
        kinetic = kinetic + dot_t(comps[3][left], comps[3][right])
        total = (dot_t(scaled[left], scaled[right]) + 0.5 * kinetic) * (1.0 / NG)
        face = dot_t(flux[left], jump[right]) + dot_t(jump[left], flux[right])
        total = total + face * (1.0 / (4.0 * F))
        for i in range(2):
            for j in range(2):
                row, column = 2 * big_i + i, 2 * big_j + j
                if row >= column:
                    place = 128 * (row * (row + 1) // 2 + column)
                    block = total[128 * i : 128 * i + 128, 128 * j : 128 * j + 128]
                    o_ref[place : place + 128, :] = block


def partial_gram(at, received, potential, points):
    return pl.pallas_call(
        gram_kernel,
        in_specs=[SMEM] + [VMEM] * 3,
        out_specs=VMEM,
        out_shape=jax.ShapeDtypeStruct((PACKED, 128), f32),
        compiler_params=params(32),
        name="partial_gram",
    )(at, received, potential, points)


def unpack(packed, d_ref):
    for row in range(4):
        for column in range(row + 1):
            place = 128 * (row * (row + 1) // 2 + column)
            block = packed[place : place + 128, :]
            r, c = pl.ds(128 * row, 128), pl.ds(128 * column, 128)
            d_ref[r, c] = block
            if row > column:
                d_ref[c, r] = block.astype(f32).T.astype(bf16)


def begin(d_ref, v_ref, part_ref, new_ref, low_ref):
    v = v_ref[...]
    applied = dot_n(d_ref[...], v) + part_ref[...]
    new = (applied - CENTER * v.astype(f32)) * (1.0 / HALF_WIDTH)
    new_ref[...] = new
    low_ref[...] = new.astype(bf16)


def first_kernel(at_ref, b0, b1, b2, b3, v_ref, part_ref, d_ref, new_ref, low_ref, packed_ref):
    for q, b_ref in enumerate((b0, b1, b2, b3)):
        for r in range(4):
            k = 4 * q + r
            rows = pl.ds(pl.multiple_of(at_ref[1, k], PIECE), PIECE)
            packed_ref[at_ref[0, k], rows, :] = b_ref[r]
    unpack(packed_ref.at[0], d_ref)
    begin(d_ref, v_ref, part_ref, new_ref, low_ref)


def second_kernel(packed_ref, v_ref, part_ref, d_ref, new_ref, low_ref):
    unpack(packed_ref.at[1], d_ref)
    begin(d_ref, v_ref, part_ref, new_ref, low_ref)


def first_step(at, blocks, v0, v1, part0, part1):
    shapes = [
        jax.ShapeDtypeStruct((NB, NB), bf16),
        jax.ShapeDtypeStruct(v0.shape, f32),
        jax.ShapeDtypeStruct(v0.shape, bf16),
    ]
    *first, packed = pl.pallas_call(
        first_kernel,
        in_specs=[SMEM] + [VMEM] * 6,
        out_specs=[VMEM] * 4,
        out_shape=shapes + [jax.ShapeDtypeStruct((2, PACKED, 128), bf16)],
        compiler_params=params(),
        name="first_step_slot0",
    )(at, *blocks, v0, part0)
    second = pl.pallas_call(
        second_kernel,
        in_specs=[VMEM] * 3,
        out_specs=[VMEM] * 3,
        out_shape=shapes,
        compiler_params=params(),
        name="first_step_slot1",
    )(packed, v1, part1)
    return first, second


def last_kernel(flip_ref, m0_ref, m1_ref, o_ref):
    flip = flip_ref[0]
    o_ref[flip] = m0_ref[...].astype(f32)
    o_ref[1 - flip] = m1_ref[...].astype(f32)


def last_placing(flip, moved):
    rows, columns = moved[0].shape
    part = pl.BlockSpec((rows // 4, columns), lambda i: (i, 0))
    return pl.pallas_call(
        last_kernel,
        grid=(4,),
        in_specs=[SMEM, part, part],
        out_specs=pl.BlockSpec((2, rows // 4, columns), lambda i: (0, i, 0)),
        out_shape=jax.ShapeDtypeStruct((2, rows, columns), f32),
        compiler_params=params(),
        name="last_placing",
    )(flip, *moved)


def sides_kernel(flip_ref, x_ref, pts_ref, sign_ref, o_ref):
    chunk = 512
    for slot in range(2):
        block = x_ref[jnp.bitwise_xor(flip_ref[0], slot)].reshape(64, NG)
        points = pts_ref[slot : slot + 1, :]
        found = jnp.zeros((64, 2 * F), f32)
        for part in range(NG // chunk):
            rows = lax.broadcasted_iota(jnp.int32, (chunk, 2 * F), 0) + part * chunk
            pick = jnp.where(rows == points, 1.0, 0.0).astype(bf16)
            found = found + dot_n(block[:, part * chunk : (part + 1) * chunk], pick)
        value = found[:32] * sign_ref[slot : slot + 1, :]
        flux = 0.5 * value - 0.25 * found[32:]
        for side in range(2):
            lanes = slice(F * side, F * side + F)
            o_ref[slot, 2 * side] = flux[:, lanes].astype(bf16)
            o_ref[slot, 2 * side + 1] = value[:, lanes].astype(bf16)


def local_sides(flip, basis, points, signs):
    return pl.pallas_call(
        sides_kernel,
        grid=(1,),
        in_specs=[
            SMEM,
            pl.BlockSpec((2, 2, 32, NG), lambda d: (0, 0, 0, 0)),
            VMEM,
            VMEM,
        ],
        out_specs=VMEM,
        out_shape=jax.ShapeDtypeStruct((2, 4, 32, F), bf16),
        compiler_params=params(),
        name="local_sides",
    )(flip, basis, points, signs)


def face(a_flux, a_jump, b_flux, b_jump):
    total = dot_t(a_flux, b_jump) + dot_t(a_jump, b_flux)
    return (total * (1.0 / (4.0 * F))).astype(bf16)


def arrange_kernel(rows_ref, b0, b1, b2, b3, z_ref, c_ref, m01_ref, m10_ref, inner):
    outer = (z_ref, c_ref)
    for q, b_ref in enumerate((b0, b1, b2, b3)):
        for r in range(4):
            rows = pl.ds(pl.multiple_of(rows_ref[4 * q + r], 32), 32)
            for slot in range(2):
                for k in range(2):
                    outer[slot][k, rows, :] = b_ref[r, slot, k]
                    inner[slot, k, rows, :] = b_ref[r, slot, 2 + k]
    m01_ref[...] = face(inner[0, 0], inner[0, 1], inner[1, 0], inner[1, 1])
    m10_ref[...] = face(inner[1, 0], inner[1, 1], inner[0, 0], inner[0, 1])


def arrange(rows, blocks):
    return pl.pallas_call(
        arrange_kernel,
        in_specs=[SMEM] + [VMEM] * 4,
        out_specs=[VMEM] * 4,
        out_shape=[jax.ShapeDtypeStruct((2, NB, F), bf16)] * 2
        + [jax.ShapeDtypeStruct((NB, NB), bf16)] * 2,
        scratch_shapes=[pltpu.VMEM((2, 2, NB, F), bf16)],
        compiler_params=params(),
        cost_estimate=TINY,
        name="arrange_sides",
    )(rows, *blocks)


def edge_kernel(z_ref, zr_ref, c_ref, cr_ref, mz_ref, mc_ref):
    mz_ref[...] = face(z_ref[0], z_ref[1], zr_ref[0], zr_ref[1])
    mc_ref[...] = face(c_ref[0], c_ref[1], cr_ref[0], cr_ref[1])


def edge_couplings(*sides):
    return pl.pallas_call(
        edge_kernel,
        in_specs=[VMEM] * 4,
        out_specs=[VMEM] * 2,
        out_shape=[jax.ShapeDtypeStruct((NB, NB), bf16)] * 2,
        compiler_params=params(),
        cost_estimate=TINY,
        name="edge_couplings",
    )(*sides)


def gather_plane(x):
    return gather_second(gather_first(x))


def gather_first(x):
    return jnp.stack([lax.ppermute(x, BOTH, perm) for perm in FIRST])


def gather_second(first):
    return [first] + [lax.ppermute(first, BOTH, perm) for perm in SECOND[1:]]


def per_device(basis, potential, face_index, face_match, vectors):
    elem = lax.axis_index("elem")
    inner = lax.axis_index("inner")
    x_lo, core, chip = elem % 2, inner % 2, inner // 2
    z_even = 1 - (elem // 2) % 2
    pair = core ^ z_even

    slabs = to_slabs(basis).reshape(16, 128, SLAB)
    received = lax.all_to_all(slabs, "inner", 0, 0)

    hits = face_match[:, :, None] == lax.broadcasted_iota(jnp.int32, (1, 1, F), 2)
    left_points = jnp.sum(jnp.where(hits, face_index[:, None, 0, :], 0), axis=2)
    right_points = face_index[:, 1, :]
    own_points = jnp.concatenate((right_points, left_points), axis=1) - chip * SLAB
    own_points = lax.dynamic_slice(own_points, (core, 0), (1, 2 * F))

    lr = jnp.concatenate((left_points, right_points), axis=1)
    rl = jnp.concatenate((right_points, left_points), axis=1)
    slot_points = jnp.where(
        x_lo == 0, jnp.stack((lr[0], rl[1])), jnp.stack((rl[1], lr[0]))
    )
    minus = jnp.repeat(jnp.array([[-1.0, 1.0], [1.0, -1.0]], f32), F, axis=1)
    slot_signs = jnp.where(x_lo == 0, minus, -minus)
    sides = local_sides(x_lo.reshape(1), basis, slot_points, slot_signs)
    first_sides = gather_first(sides)
    start = lax.ppermute(vectors, BOTH, SWAP)
    v0 = lax.dynamic_index_in_dim(start, pair, 0, False)
    v1 = lax.dynamic_index_in_dim(start, 1 - pair, 0, False)
    received, first_sides, v0, v1 = lax.optimization_barrier((received, first_sides, v0, v1))
    my_y, my_x = inner // 4, 2 * ((inner // 2) % 2) + x_lo
    q = lax.broadcasted_iota(jnp.int32, (16,), 0) // 4
    r = lax.broadcasted_iota(jnp.int32, (16,), 0) % 4
    from_y = (my_y + jnp.where(core == 0, r, q)) % 4
    from_x = (my_x + jnp.where(core == 0, q, r)) % 4
    rows = 32 * (4 * from_y + from_x)
    pieces_at = jnp.stack(((from_x % 2) ^ pair, PIECE * (2 * from_y + from_x // 2)))
    packed = partial_gram(jnp.stack((core, chip)), received, potential, own_points)
    pieces = lax.all_to_all(
        packed.reshape(8, PIECE, 128), "inner", 0, 0, axis_index_groups=CHIPS
    )

    first_sides, v0, v1, _ = lax.optimization_barrier((first_sides, v0, v1, packed))
    blocks = gather_second(first_sides)

    def edges(v0, v1):
        return lax.ppermute(v0, BOTH, Z_EDGE), lax.ppermute(v1, BOTH, C_EDGE)

    zv, cv = edges(v0, v1)
    blocks, pieces = lax.optimization_barrier((blocks, pieces))
    z_sides, c_sides, m01, m10 = arrange(rows, blocks)
    mz, mc = edge_couplings(
        z_sides, lax.ppermute(z_sides, BOTH, Z_EDGE),
        c_sides, lax.ppermute(c_sides, BOTH, C_EDGE),
    )
    part0 = dot_n(m01, v1) + dot_n(mz, zv)
    part1 = dot_n(m10, v0) + dot_n(mc, cv)

    piece = jnp.sum(pieces, axis=0).astype(bf16)
    gathered = gather_plane(piece)
    (d0, new0, low0), (d1, new1, low1) = first_step(pieces_at, gathered, v0, v1, part0, part1)
    previous = [v0.astype(f32), v1.astype(f32)]
    current = [new0, new1]
    low = [low0, low1]
    scale = 1.0 / chebyshev_norm(STEPS)
    for step in range(1, STEPS):
        zv, cv = edges(*low)

        def following(a, at):
            return 2.0 * (a - CENTER * current[at]) / HALF_WIDTH - previous[at]

        new1 = following(dot_n(d1, low[1]) + dot_n(m10, low[0]) + dot_n(mc, cv), 1)
        if step == STEPS - 1:
            last1 = (new1 * scale).astype(bf16)
            moved1 = lax.ppermute(last1, BOTH, BACK)
            zv, _ = lax.optimization_barrier((zv, last1))
        new0 = following(dot_n(d0, low[0]) + dot_n(m01, low[1]) + dot_n(mz, zv), 0)
        previous, current = current, [new0, new1]
        low = [c.astype(bf16) for c in current]
    moved = [lax.ppermute((new0 * scale).astype(bf16), BOTH, BACK), moved1]
    return last_placing(x_lo.reshape(1), moved)


def solution(mesh):
    placed = (
        P("elem", None, "inner", None),
        P("elem", None),
        P("elem", None, None),
        P("elem", None),
        P("elem", None, "inner"),
    )
    return jax.shard_map(
        per_device, mesh=mesh, in_specs=placed, out_specs=P("elem", None, "inner"), check_vma=False
    )
```

```python
import jax
import jax.numpy as jnp
from jax import lax
from jax.experimental import pallas as pl
from jax.experimental.pallas import tpu as pltpu
from jax.sharding import PartitionSpec as P

NB = 512
NG = 4096
F = 128
STEPS = 6
CENTER = 5.25
HALF_WIDTH = 2.75
NZ, NY, NX = 8, 4, 4
BOTH = ("elem", "inner")
SLAB = NG // 8
PACKED = 10 * 128
PIECE = PACKED // 8
bf16 = jnp.bfloat16
f32 = jnp.float32


def flat(z, y, x, c):
    z, y, x = z % NZ, y % NY, x % NX
    return (z * 2 + x % 2) * 16 + y * 4 + (x // 2) * 2 + c


PLACES = [(z, y, x, c) for z in range(NZ) for y in range(NY) for x in range(NX) for c in range(2)]


def pair_of(z, c):
    return c if z % 2 else 1 - c


def moved_to(z, y, x, c):
    pair, column = x % 2, c
    return z, y, (x // 2) * 2 + column, pair if z % 2 else 1 - pair


def along(place, axis, step):
    z, y, x, c = place
    return (z, y + step, x, c) if c == axis else (z, y, x + step, c)


def pairs_of(move):
    return [(flat(*p), flat(*move(*p))) for p in PLACES]


SWAP = pairs_of(moved_to)
BACK = [(j, i) for i, j in SWAP]
Z_EDGE = pairs_of(lambda z, y, x, c: (z + (1 if pair_of(z, c) else -1), y, x, c))
C_EDGE = pairs_of(lambda z, y, x, c: (z, y, x, 1 - c))
FIRST = [pairs_of(lambda *p: along(moved_to(*p), 0, -r)) for r in range(4)]
SECOND = [pairs_of(lambda *p: along(p, 1, -q)) for q in range(4)]
CHIPS = [[c + 2 * k for k in range(8)] for c in range(2)]


def chebyshev_norm(count):
    ratio = (CENTER - 1.0) / HALF_WIDTH
    root = ratio + (ratio * ratio - 1.0) ** 0.5
    return 0.5 * (root**count + root ** (-count))


def params(mib=16):
    return pltpu.CompilerParams(vmem_limit_bytes=mib * 1024 * 1024)


VMEM = pl.BlockSpec(memory_space=pltpu.VMEM)
SMEM = pl.BlockSpec(memory_space=pltpu.SMEM)


TINY = pl.CostEstimate(flops=1, bytes_accessed=1, transcendentals=0)


def dot_t(a, b):
    return lax.dot_general(a, b, (((1,), (1,)), ((), ())), preferred_element_type=f32)


def dot_n(a, b):
    return lax.dot_general(a, b, (((1,), (0,)), ((), ())), preferred_element_type=f32)


def slab_kernel(x_ref, o_ref):
    o_ref[0] = x_ref[...]


def to_slabs(basis, half):
    return pl.pallas_call(
        slab_kernel,
        grid=(8,),
        in_specs=[pl.BlockSpec((2, 2, 32, SLAB), lambda d: (0, half, 0, d))],
        out_specs=pl.BlockSpec((1, 2, 2, 32, SLAB), lambda d: (d, 0, 0, 0, 0)),
        out_shape=jax.ShapeDtypeStruct((8, 2, 2, 32, SLAB), bf16),
        compiler_params=params(),
        name="to_slabs",
    )(basis)


def component(r_ref, k):
    return r_ref[:, 32 * k : 32 * k + 32, :].reshape(NB, SLAB)


def packed_blocks():
    for big_i, big_j in ((0, 0), (1, 0), (1, 1)):
        small = []
        for i in range(2):
            for j in range(2):
                row, column = 2 * big_i + i, 2 * big_j + j
                if row >= column:
                    small.append((128 * i, 128 * j, 128 * (row * (row + 1) // 2 + column)))
        yield slice(256 * big_i, 256 * big_i + 256), slice(256 * big_j, 256 * big_j + 256), small


def gram_kernel(at_ref, r_ref, pot_ref, pts_ref, o_ref):
    values, slopes = component(r_ref, 0), component(r_ref, 1)
    lanes = pl.ds(pl.multiple_of(at_ref[1] * SLAB, SLAB), SLAB)
    potential = jnp.where(at_ref[0] == 0, pot_ref[0:1, lanes], pot_ref[1:2, lanes])
    scaled = (jnp.sqrt(potential) * values.astype(f32)).astype(bf16)
    rows = lax.broadcasted_iota(jnp.int32, (SLAB, 2 * F), 0)
    pick = jnp.where(rows == pts_ref[...], 1.0, 0.0).astype(bf16)
    sign = jnp.where(lax.broadcasted_iota(jnp.int32, (1, 2 * F), 1) < F, 1.0, -1.0)
    value = dot_n(values, pick) * sign
    slope = dot_n(slopes, pick)
    jump = value.astype(bf16)
    flux = (0.5 * value - 0.25 * slope).astype(bf16)
    for left, right, small in packed_blocks():
        total = dot_t(scaled[left], scaled[right]) + 0.5 * dot_t(slopes[left], slopes[right])
        face = dot_t(flux[left], jump[right]) + dot_t(jump[left], flux[right])
        total = total * (1.0 / NG) + face * (1.0 / (4.0 * F))
        for i, j, place in small:
            o_ref[place : place + 128, :] = total[i : i + 128, j : j + 128]


def gram_first(at, received, potential, points):
    return pl.pallas_call(
        gram_kernel,
        in_specs=[SMEM] + [VMEM] * 3,
        out_specs=VMEM,
        out_shape=jax.ShapeDtypeStruct((PACKED, 128), f32),
        compiler_params=params(24),
        name="gram_first",
    )(at, received, potential, points)


def rest_kernel(r_ref, first_ref, o_ref):
    two, three = component(r_ref, 0), component(r_ref, 1)
    for left, right, small in packed_blocks():
        total = dot_t(two[left], two[right]) + dot_t(three[left], three[right])
        total = total * (0.5 / NG)
        for i, j, place in small:
            rows = slice(place, place + 128)
            o_ref[rows, :] = first_ref[rows, :] + total[i : i + 128, j : j + 128]


def gram_rest(received, first):
    return pl.pallas_call(
        rest_kernel,
        in_specs=[VMEM] * 2,
        out_specs=VMEM,
        out_shape=jax.ShapeDtypeStruct((PACKED, 128), f32),
        compiler_params=params(24),
        name="gram_rest",
    )(received, first)


def unpack(packed, d_ref):
    for row in range(4):
        for column in range(row + 1):
            place = 128 * (row * (row + 1) // 2 + column)
            block = packed[place : place + 128, :]
            r, c = pl.ds(128 * row, 128), pl.ds(128 * column, 128)
            d_ref[r, c] = block
            if row > column:
                d_ref[c, r] = block.astype(f32).T.astype(bf16)


def begin(d_ref, v_ref, part_ref, new_ref, low_ref):
    v = v_ref[...]
    applied = dot_n(d_ref[...], v) + part_ref[...]
    new = (applied - CENTER * v.astype(f32)) * (1.0 / HALF_WIDTH)
    new_ref[...] = new
    low_ref[...] = new.astype(bf16)


def first_kernel(at_ref, b0, b1, b2, b3, v_ref, part_ref, d_ref, new_ref, low_ref, packed_ref):
    for q, b_ref in enumerate((b0, b1, b2, b3)):
        for r in range(4):
            k = 4 * q + r
            rows = pl.ds(pl.multiple_of(at_ref[1, k], PIECE), PIECE)
            packed_ref[at_ref[0, k], rows, :] = b_ref[r]
    unpack(packed_ref.at[0], d_ref)
    begin(d_ref, v_ref, part_ref, new_ref, low_ref)


def second_kernel(packed_ref, v_ref, part_ref, d_ref, new_ref, low_ref):
    unpack(packed_ref.at[1], d_ref)
    begin(d_ref, v_ref, part_ref, new_ref, low_ref)


def first_step(at, blocks, v0, v1, part0, part1):
    shapes = [
        jax.ShapeDtypeStruct((NB, NB), bf16),
        jax.ShapeDtypeStruct(v0.shape, f32),
        jax.ShapeDtypeStruct(v0.shape, bf16),
    ]
    *first, packed = pl.pallas_call(
        first_kernel,
        in_specs=[SMEM] + [VMEM] * 6,
        out_specs=[VMEM] * 4,
        out_shape=shapes + [jax.ShapeDtypeStruct((2, PACKED, 128), bf16)],
        compiler_params=params(),
        name="first_step_slot0",
    )(at, *blocks, v0, part0)
    second = pl.pallas_call(
        second_kernel,
        in_specs=[VMEM] * 3,
        out_specs=[VMEM] * 3,
        out_shape=shapes,
        compiler_params=params(),
        name="first_step_slot1",
    )(packed, v1, part1)
    return first, second


def last_kernel(flip_ref, m0_ref, m1_ref, o_ref):
    flip = flip_ref[0]
    o_ref[flip] = m0_ref[...].astype(f32)
    o_ref[1 - flip] = m1_ref[...].astype(f32)


def last_placing(flip, moved):
    rows, columns = moved[0].shape
    part = pl.BlockSpec((rows // 4, columns), lambda i: (i, 0))
    return pl.pallas_call(
        last_kernel,
        grid=(4,),
        in_specs=[SMEM, part, part],
        out_specs=pl.BlockSpec((2, rows // 4, columns), lambda i: (0, i, 0)),
        out_shape=jax.ShapeDtypeStruct((2, rows, columns), f32),
        compiler_params=params(),
        name="last_placing",
    )(flip, *moved)


def sides_kernel(flip_ref, x_ref, pts_ref, sign_ref, o_ref):
    chunk = 512
    for slot in range(2):
        block = x_ref[jnp.bitwise_xor(flip_ref[0], slot)].reshape(64, NG)
        points = pts_ref[slot : slot + 1, :]
        found = jnp.zeros((64, 2 * F), f32)
        for part in range(NG // chunk):
            rows = lax.broadcasted_iota(jnp.int32, (chunk, 2 * F), 0) + part * chunk
            pick = jnp.where(rows == points, 1.0, 0.0).astype(bf16)
            found = found + dot_n(block[:, part * chunk : (part + 1) * chunk], pick)
        value = found[:32] * sign_ref[slot : slot + 1, :]
        flux = 0.5 * value - 0.25 * found[32:]
        for side in range(2):
            lanes = slice(F * side, F * side + F)
            o_ref[slot, 2 * side] = flux[:, lanes].astype(bf16)
            o_ref[slot, 2 * side + 1] = value[:, lanes].astype(bf16)


def local_sides(flip, basis, points, signs):
    return pl.pallas_call(
        sides_kernel,
        grid=(1,),
        in_specs=[
            SMEM,
            pl.BlockSpec((2, 2, 32, NG), lambda d: (0, 0, 0, 0)),
            VMEM,
            VMEM,
        ],
        out_specs=VMEM,
        out_shape=jax.ShapeDtypeStruct((2, 4, 32, F), bf16),
        compiler_params=params(),
        name="local_sides",
    )(flip, basis, points, signs)


def face(a_flux, a_jump, b_flux, b_jump):
    total = dot_t(a_flux, b_jump) + dot_t(a_jump, b_flux)
    return (total * (1.0 / (4.0 * F))).astype(bf16)


def arrange_kernel(rows_ref, b0, b1, b2, b3, z_ref, c_ref, m01_ref, m10_ref, inner):
    outer = (z_ref, c_ref)
    for q, b_ref in enumerate((b0, b1, b2, b3)):
        for r in range(4):
            rows = pl.ds(pl.multiple_of(rows_ref[4 * q + r], 32), 32)
            for slot in range(2):
                for k in range(2):
                    outer[slot][k, rows, :] = b_ref[r, slot, k]
                    inner[slot, k, rows, :] = b_ref[r, slot, 2 + k]
    m01_ref[...] = face(inner[0, 0], inner[0, 1], inner[1, 0], inner[1, 1])
    m10_ref[...] = face(inner[1, 0], inner[1, 1], inner[0, 0], inner[0, 1])


def arrange(rows, blocks):
    return pl.pallas_call(
        arrange_kernel,
        in_specs=[SMEM] + [VMEM] * 4,
        out_specs=[VMEM] * 4,
        out_shape=[jax.ShapeDtypeStruct((2, NB, F), bf16)] * 2
        + [jax.ShapeDtypeStruct((NB, NB), bf16)] * 2,
        scratch_shapes=[pltpu.VMEM((2, 2, NB, F), bf16)],
        compiler_params=params(),
        cost_estimate=TINY,
        name="arrange_sides",
    )(rows, *blocks)


def edge_kernel(z_ref, zr_ref, c_ref, cr_ref, mz_ref, mc_ref):
    mz_ref[...] = face(z_ref[0], z_ref[1], zr_ref[0], zr_ref[1])
    mc_ref[...] = face(c_ref[0], c_ref[1], cr_ref[0], cr_ref[1])


def edge_couplings(*sides):
    return pl.pallas_call(
        edge_kernel,
        in_specs=[VMEM] * 4,
        out_specs=[VMEM] * 2,
        out_shape=[jax.ShapeDtypeStruct((NB, NB), bf16)] * 2,
        compiler_params=params(),
        cost_estimate=TINY,
        name="edge_couplings",
    )(*sides)


def gather_plane(x):
    return gather_second(gather_first(x))


def gather_first(x):
    return jnp.stack([lax.ppermute(x, BOTH, perm) for perm in FIRST])


def gather_second(first):
    return [first] + [lax.ppermute(first, BOTH, perm) for perm in SECOND[1:]]


def per_device(basis, potential, face_index, face_match, vectors):
    elem = lax.axis_index("elem")
    inner = lax.axis_index("inner")
    x_lo, core, chip = elem % 2, inner % 2, inner // 2
    z_even = 1 - (elem // 2) % 2
    pair = core ^ z_even

    slabs = [to_slabs(basis, half).reshape(16, 64, SLAB) for half in range(2)]
    received = lax.all_to_all(slabs[0], "inner", 0, 0)

    hits = face_match[:, :, None] == lax.broadcasted_iota(jnp.int32, (1, 1, F), 2)
    left_points = jnp.sum(jnp.where(hits, face_index[:, None, 0, :], 0), axis=2)
    right_points = face_index[:, 1, :]
    own_points = jnp.concatenate((right_points, left_points), axis=1) - chip * SLAB
    own_points = lax.dynamic_slice(own_points, (core, 0), (1, 2 * F))

    lr = jnp.concatenate((left_points, right_points), axis=1)
    rl = jnp.concatenate((right_points, left_points), axis=1)
    slot_points = jnp.where(
        x_lo == 0, jnp.stack((lr[0], rl[1])), jnp.stack((rl[1], lr[0]))
    )
    minus = jnp.repeat(jnp.array([[-1.0, 1.0], [1.0, -1.0]], f32), F, axis=1)
    slot_signs = jnp.where(x_lo == 0, minus, -minus)
    sides = local_sides(x_lo.reshape(1), basis, slot_points, slot_signs)
    first_sides = gather_first(sides)
    start = lax.ppermute(vectors, BOTH, SWAP)
    v0 = lax.dynamic_index_in_dim(start, pair, 0, False)
    v1 = lax.dynamic_index_in_dim(start, 1 - pair, 0, False)
    received, first_sides, v0, v1, slab = lax.optimization_barrier(
        (received, first_sides, v0, v1, slabs[1])
    )
    rest = lax.all_to_all(slab, "inner", 0, 0)
    my_y, my_x = inner // 4, 2 * ((inner // 2) % 2) + x_lo
    q = lax.broadcasted_iota(jnp.int32, (16,), 0) // 4
    r = lax.broadcasted_iota(jnp.int32, (16,), 0) % 4
    from_y = (my_y + jnp.where(core == 0, r, q)) % 4
    from_x = (my_x + jnp.where(core == 0, q, r)) % 4
    rows = 32 * (4 * from_y + from_x)
    pieces_at = jnp.stack(((from_x % 2) ^ pair, PIECE * (2 * from_y + from_x // 2)))
    def edges(v0, v1):
        return lax.ppermute(v0, BOTH, Z_EDGE), lax.ppermute(v1, BOTH, C_EDGE)

    packed = gram_first(jnp.stack((core, chip)), received, potential, own_points)
    blocks = gather_second(first_sides)
    zv, cv = edges(v0, v1)
    z_sides, c_sides, m01, m10 = arrange(rows, blocks)
    rest, packed, z_sides, c_sides, m01, m10, zv, cv = lax.optimization_barrier(
        (rest, packed, z_sides, c_sides, m01, m10, zv, cv)
    )

    packed = gram_rest(rest, packed)
    pieces = lax.all_to_all(
        packed.reshape(8, PIECE, 128), "inner", 0, 0, axis_index_groups=CHIPS
    )
    z_sides, c_sides, _ = lax.optimization_barrier((z_sides, c_sides, packed))
    z_near, c_near = edges(z_sides, c_sides)
    z_near, c_near, pieces = lax.optimization_barrier((z_near, c_near, pieces))
    mz, mc = edge_couplings(z_sides, z_near, c_sides, c_near)
    part0 = dot_n(m01, v1) + dot_n(mz, zv)
    part1 = dot_n(m10, v0) + dot_n(mc, cv)

    piece = jnp.sum(pieces, axis=0).astype(bf16)
    gathered = gather_plane(piece)
    (d0, new0, low0), (d1, new1, low1) = first_step(pieces_at, gathered, v0, v1, part0, part1)
    previous = [v0.astype(f32), v1.astype(f32)]
    current = [new0, new1]
    low = [low0, low1]
    scale = 1.0 / chebyshev_norm(STEPS)
    for step in range(1, STEPS):
        zv, cv = edges(*low)

        def following(a, at):
            return 2.0 * (a - CENTER * current[at]) / HALF_WIDTH - previous[at]

        new1 = following(dot_n(d1, low[1]) + dot_n(m10, low[0]) + dot_n(mc, cv), 1)
        if step == STEPS - 1:
            last1 = (new1 * scale).astype(bf16)
            moved1 = lax.ppermute(last1, BOTH, BACK)
            zv, _ = lax.optimization_barrier((zv, last1))
        new0 = following(dot_n(d0, low[0]) + dot_n(m01, low[1]) + dot_n(mz, zv), 0)
        previous, current = current, [new0, new1]
        low = [c.astype(bf16) for c in current]
    moved = [lax.ppermute((new0 * scale).astype(bf16), BOTH, BACK), moved1]
    return last_placing(x_lo.reshape(1), moved)


def solution(mesh):
    placed = (
        P("elem", None, "inner", None),
        P("elem", None),
        P("elem", None, None),
        P("elem", None),
        P("elem", None, "inner"),
    )
    return jax.shard_map(
        per_device, mesh=mesh, in_specs=placed, out_specs=P("elem", None, "inner"), check_vma=False
    )
```

```python
import jax
import jax.numpy as jnp
from jax import lax
from jax.experimental import pallas as pl
from jax.experimental.pallas import tpu as pltpu
from jax.sharding import PartitionSpec as P

NB = 512
NG = 4096
F = 128
STEPS = 6
CENTER = 5.25
HALF_WIDTH = 2.75
NZ, NY, NX = 8, 4, 4
BOTH = ("elem", "inner")
SLAB = NG // 8
PACKED = 10 * 128
PIECE = PACKED // 8
bf16 = jnp.bfloat16
f32 = jnp.float32


def flat(z, y, x, c):
    z, y, x = z % NZ, y % NY, x % NX
    return (z * 2 + x % 2) * 16 + y * 4 + (x // 2) * 2 + c


PLACES = [(z, y, x, c) for z in range(NZ) for y in range(NY) for x in range(NX) for c in range(2)]


def pair_of(z, c):
    return c if z % 2 else 1 - c


def moved_to(z, y, x, c):
    pair, column = x % 2, c
    return z, y, (x // 2) * 2 + column, pair if z % 2 else 1 - pair


def along(place, axis, step):
    z, y, x, c = place
    return (z, y + step, x, c) if c == axis else (z, y, x + step, c)


def pairs_of(move):
    return [(flat(*p), flat(*move(*p))) for p in PLACES]


SWAP = pairs_of(moved_to)
BACK = [(j, i) for i, j in SWAP]
Z_EDGE = pairs_of(lambda z, y, x, c: (z + (1 if pair_of(z, c) else -1), y, x, c))
C_EDGE = pairs_of(lambda z, y, x, c: (z, y, x, 1 - c))
FIRST = [pairs_of(lambda *p: along(moved_to(*p), 0, -r)) for r in range(4)]
SECOND = [pairs_of(lambda *p: along(p, 1, -q)) for q in range(4)]
CHIPS = [[c + 2 * k for k in range(8)] for c in range(2)]


def chebyshev_norm(count):
    ratio = (CENTER - 1.0) / HALF_WIDTH
    root = ratio + (ratio * ratio - 1.0) ** 0.5
    return 0.5 * (root**count + root ** (-count))


def params(mib=16):
    return pltpu.CompilerParams(vmem_limit_bytes=mib * 1024 * 1024)


VMEM = pl.BlockSpec(memory_space=pltpu.VMEM)
SMEM = pl.BlockSpec(memory_space=pltpu.SMEM)


TINY = pl.CostEstimate(flops=1, bytes_accessed=1, transcendentals=0)


def dot_t(a, b):
    return lax.dot_general(a, b, (((1,), (1,)), ((), ())), preferred_element_type=f32)


def dot_n(a, b):
    return lax.dot_general(a, b, (((1,), (0,)), ((), ())), preferred_element_type=f32)


def slab_kernel(x_ref, o_ref):
    o_ref[0] = x_ref[...]


def to_slabs(basis):
    return pl.pallas_call(
        slab_kernel,
        grid=(8,),
        in_specs=[pl.BlockSpec((2, 4, 32, SLAB), lambda d: (0, 0, 0, d))],
        out_specs=pl.BlockSpec((1, 2, 4, 32, SLAB), lambda d: (d, 0, 0, 0, 0)),
        out_shape=jax.ShapeDtypeStruct((8, 2, 4, 32, SLAB), bf16),
        compiler_params=params(40),
        cost_estimate=pl.CostEstimate(flops=0, bytes_accessed=1 << 26, transcendentals=0),
        name="to_slabs",
    )(basis)


def gram_kernel(at_ref, r_ref, pot_ref, pts_ref, o_ref):
    comps = [r_ref[:, 32 * k : 32 * k + 32, :].reshape(NB, SLAB) for k in range(4)]
    lanes = pl.ds(pl.multiple_of(at_ref[1] * SLAB, SLAB), SLAB)
    potential = jnp.where(at_ref[0] == 0, pot_ref[0:1, lanes], pot_ref[1:2, lanes])
    scaled = (jnp.sqrt(potential) * comps[0].astype(f32)).astype(bf16)
    rows = lax.broadcasted_iota(jnp.int32, (SLAB, 2 * F), 0)
    pick = jnp.where(rows == pts_ref[...], 1.0, 0.0).astype(bf16)
    sign = jnp.where(lax.broadcasted_iota(jnp.int32, (1, 2 * F), 1) < F, 1.0, -1.0)
    value = dot_n(comps[0], pick) * sign
    slope = dot_n(comps[1], pick)
    jump = value.astype(bf16)
    flux = (0.5 * value - 0.25 * slope).astype(bf16)
    for big_i, big_j in ((0, 0), (1, 0), (1, 1)):
        left = slice(256 * big_i, 256 * big_i + 256)
        right = slice(256 * big_j, 256 * big_j + 256)
        kinetic = dot_t(comps[1][left], comps[1][right])
        kinetic = kinetic + dot_t(comps[2][left], comps[2][right])
        kinetic = kinetic + dot_t(comps[3][left], comps[3][right])
        total = (dot_t(scaled[left], scaled[right]) + 0.5 * kinetic) * (1.0 / NG)
        face = dot_t(flux[left], jump[right]) + dot_t(jump[left], flux[right])
        total = total + face * (1.0 / (4.0 * F))
        for i in range(2):
            for j in range(2):
                row, column = 2 * big_i + i, 2 * big_j + j
                if row >= column:
                    place = 128 * (row * (row + 1) // 2 + column)
                    block = total[128 * i : 128 * i + 128, 128 * j : 128 * j + 128]
                    o_ref[place : place + 128, :] = block


def partial_gram(at, received, potential, points):
    return pl.pallas_call(
        gram_kernel,
        in_specs=[SMEM] + [VMEM] * 3,
        out_specs=VMEM,
        out_shape=jax.ShapeDtypeStruct((PACKED, 128), f32),
        compiler_params=params(32),
        name="partial_gram",
    )(at, received, potential, points)


def unpack(packed, d_ref):
    for row in range(4):
        for column in range(row + 1):
            place = 128 * (row * (row + 1) // 2 + column)
            block = packed[place : place + 128, :]
            r, c = pl.ds(128 * row, 128), pl.ds(128 * column, 128)
            d_ref[r, c] = block
            if row > column:
                d_ref[c, r] = block.astype(f32).T.astype(bf16)


def begin(d_ref, v_ref, part_ref, new_ref, low_ref):
    v = v_ref[...]
    applied = dot_n(d_ref[...], v) + part_ref[...]
    new = (applied - CENTER * v.astype(f32)) * (1.0 / HALF_WIDTH)
    new_ref[...] = new
    low_ref[...] = new.astype(bf16)


def first_kernel(at_ref, b0, b1, b2, b3, v_ref, part_ref, d_ref, new_ref, low_ref, packed_ref):
    for q, b_ref in enumerate((b0, b1, b2, b3)):
        for r in range(4):
            k = 4 * q + r
            rows = pl.ds(pl.multiple_of(at_ref[1, k], PIECE), PIECE)
            packed_ref[at_ref[0, k], rows, :] = b_ref[r]
    unpack(packed_ref.at[0], d_ref)
    begin(d_ref, v_ref, part_ref, new_ref, low_ref)


def second_kernel(packed_ref, v_ref, part_ref, d_ref, new_ref, low_ref):
    unpack(packed_ref.at[1], d_ref)
    begin(d_ref, v_ref, part_ref, new_ref, low_ref)


def first_step(at, blocks, v0, v1, part0, part1):
    shapes = [
        jax.ShapeDtypeStruct((NB, NB), bf16),
        jax.ShapeDtypeStruct(v0.shape, f32),
        jax.ShapeDtypeStruct(v0.shape, bf16),
    ]
    *first, packed = pl.pallas_call(
        first_kernel,
        in_specs=[SMEM] + [VMEM] * 6,
        out_specs=[VMEM] * 4,
        out_shape=shapes + [jax.ShapeDtypeStruct((2, PACKED, 128), bf16)],
        compiler_params=params(),
        name="first_step_slot0",
    )(at, *blocks, v0, part0)
    second = pl.pallas_call(
        second_kernel,
        in_specs=[VMEM] * 3,
        out_specs=[VMEM] * 3,
        out_shape=shapes,
        compiler_params=params(),
        name="first_step_slot1",
    )(packed, v1, part1)
    return first, second


def inside_kernel(d_ref, m_ref, v_ref, w_ref, cur_ref, prev_ref, o_ref):
    applied = dot_n(d_ref[...], v_ref[...]) + dot_n(m_ref[...], w_ref[...])
    applied = applied - CENTER * cur_ref[...].astype(f32)
    o_ref[...] = applied * (2.0 / HALF_WIDTH) - prev_ref[...].astype(f32)


def inside(d, m, v, w, current, previous):
    return pl.pallas_call(
        inside_kernel,
        in_specs=[VMEM] * 6,
        out_specs=VMEM,
        out_shape=jax.ShapeDtypeStruct(v.shape, f32),
        compiler_params=params(),
        name="inside",
    )(d, m, v, w, current, previous)


def outside_kernel(acc_ref, m_ref, halo_ref, new_ref, low_ref):
    new = acc_ref[...] + dot_n(m_ref[...], halo_ref[...]) * (2.0 / HALF_WIDTH)
    new_ref[...] = new
    low_ref[...] = new.astype(bf16)


def outside_last_kernel(acc_ref, m_ref, halo_ref, low_ref):
    new = acc_ref[...] + dot_n(m_ref[...], halo_ref[...]) * (2.0 / HALF_WIDTH)
    low_ref[...] = (new * (1.0 / chebyshev_norm(STEPS))).astype(bf16)


def outside(acc, m, halo, last):
    low = jax.ShapeDtypeStruct(acc.shape, bf16)
    return pl.pallas_call(
        outside_last_kernel if last else outside_kernel,
        in_specs=[VMEM] * 3,
        out_specs=VMEM if last else [VMEM] * 2,
        out_shape=low if last else [jax.ShapeDtypeStruct(acc.shape, f32), low],
        compiler_params=params(),
        name="outside",
    )(acc, m, halo)


def last_kernel(flip_ref, m0_ref, m1_ref, o_ref):
    flip = flip_ref[0]
    o_ref[flip] = m0_ref[...].astype(f32)
    o_ref[1 - flip] = m1_ref[...].astype(f32)


def last_placing(flip, moved):
    rows, columns = moved[0].shape
    part = pl.BlockSpec((rows // 4, columns), lambda i: (i, 0))
    return pl.pallas_call(
        last_kernel,
        grid=(4,),
        in_specs=[SMEM, part, part],
        out_specs=pl.BlockSpec((2, rows // 4, columns), lambda i: (0, i, 0)),
        out_shape=jax.ShapeDtypeStruct((2, rows, columns), f32),
        compiler_params=params(),
        name="last_placing",
    )(flip, *moved)


def sides_kernel(flip_ref, x_ref, pts_ref, sign_ref, o_ref):
    chunk = 512
    for slot in range(2):
        block = x_ref[jnp.bitwise_xor(flip_ref[0], slot)].reshape(64, NG)
        points = pts_ref[slot : slot + 1, :]
        found = jnp.zeros((64, 2 * F), f32)
        for part in range(NG // chunk):
            rows = lax.broadcasted_iota(jnp.int32, (chunk, 2 * F), 0) + part * chunk
            pick = jnp.where(rows == points, 1.0, 0.0).astype(bf16)
            found = found + dot_n(block[:, part * chunk : (part + 1) * chunk], pick)
        value = found[:32] * sign_ref[slot : slot + 1, :]
        flux = 0.5 * value - 0.25 * found[32:]
        for side in range(2):
            lanes = slice(F * side, F * side + F)
            o_ref[slot, 2 * side] = flux[:, lanes].astype(bf16)
            o_ref[slot, 2 * side + 1] = value[:, lanes].astype(bf16)


def local_sides(flip, basis, points, signs):
    return pl.pallas_call(
        sides_kernel,
        grid=(1,),
        in_specs=[
            SMEM,
            pl.BlockSpec((2, 2, 32, NG), lambda d: (0, 0, 0, 0)),
            VMEM,
            VMEM,
        ],
        out_specs=VMEM,
        out_shape=jax.ShapeDtypeStruct((2, 4, 32, F), bf16),
        compiler_params=params(),
        name="local_sides",
    )(flip, basis, points, signs)


def face(a_flux, a_jump, b_flux, b_jump):
    total = dot_t(a_flux, b_jump) + dot_t(a_jump, b_flux)
    return (total * (1.0 / (4.0 * F))).astype(bf16)


def arrange_kernel(rows_ref, b0, b1, b2, b3, z_ref, c_ref, m01_ref, m10_ref, inner):
    outer = (z_ref, c_ref)
    for q, b_ref in enumerate((b0, b1, b2, b3)):
        for r in range(4):
            rows = pl.ds(pl.multiple_of(rows_ref[4 * q + r], 32), 32)
            for slot in range(2):
                for k in range(2):
                    outer[slot][k, rows, :] = b_ref[r, slot, k]
                    inner[slot, k, rows, :] = b_ref[r, slot, 2 + k]
    m01_ref[...] = face(inner[0, 0], inner[0, 1], inner[1, 0], inner[1, 1])
    m10_ref[...] = face(inner[1, 0], inner[1, 1], inner[0, 0], inner[0, 1])


def arrange(rows, blocks):
    return pl.pallas_call(
        arrange_kernel,
        in_specs=[SMEM] + [VMEM] * 4,
        out_specs=[VMEM] * 4,
        out_shape=[jax.ShapeDtypeStruct((2, NB, F), bf16)] * 2
        + [jax.ShapeDtypeStruct((NB, NB), bf16)] * 2,
        scratch_shapes=[pltpu.VMEM((2, 2, NB, F), bf16)],
        compiler_params=params(),
        cost_estimate=TINY,
        name="arrange_sides",
    )(rows, *blocks)


def edge_kernel(z_ref, zr_ref, c_ref, cr_ref, mz_ref, mc_ref):
    mz_ref[...] = face(z_ref[0], z_ref[1], zr_ref[0], zr_ref[1])
    mc_ref[...] = face(c_ref[0], c_ref[1], cr_ref[0], cr_ref[1])


def edge_couplings(*sides):
    return pl.pallas_call(
        edge_kernel,
        in_specs=[VMEM] * 4,
        out_specs=[VMEM] * 2,
        out_shape=[jax.ShapeDtypeStruct((NB, NB), bf16)] * 2,
        compiler_params=params(),
        cost_estimate=TINY,
        name="edge_couplings",
    )(*sides)


def gather_plane(x):
    return gather_second(gather_first(x))


def gather_first(x):
    return jnp.stack([lax.ppermute(x, BOTH, perm) for perm in FIRST])


def gather_second(first):
    return [first] + [lax.ppermute(first, BOTH, perm) for perm in SECOND[1:]]


def per_device(basis, potential, face_index, face_match, vectors):
    elem = lax.axis_index("elem")
    inner = lax.axis_index("inner")
    x_lo, core, chip = elem % 2, inner % 2, inner // 2
    z_even = 1 - (elem // 2) % 2
    pair = core ^ z_even

    hits = face_match[:, :, None] == lax.broadcasted_iota(jnp.int32, (1, 1, F), 2)
    left_points = jnp.sum(jnp.where(hits, face_index[:, None, 0, :], 0), axis=2)
    right_points = face_index[:, 1, :]
    own_points = jnp.concatenate((right_points, left_points), axis=1) - chip * SLAB
    own_points = lax.dynamic_slice(own_points, (core, 0), (1, 2 * F))

    lr = jnp.concatenate((left_points, right_points), axis=1)
    rl = jnp.concatenate((right_points, left_points), axis=1)
    slot_points = jnp.where(
        x_lo == 0, jnp.stack((lr[0], rl[1])), jnp.stack((rl[1], lr[0]))
    )
    minus = jnp.repeat(jnp.array([[-1.0, 1.0], [1.0, -1.0]], f32), F, axis=1)
    slot_signs = jnp.where(x_lo == 0, minus, -minus)
    sides = local_sides(x_lo.reshape(1), basis, slot_points, slot_signs)
    first_sides = gather_first(sides)
    slabs = to_slabs(basis).reshape(16, 128, SLAB)
    slabs, first_sides = lax.optimization_barrier((slabs, first_sides))
    received = lax.all_to_all(slabs, "inner", 0, 0)
    blocks = gather_second(first_sides)
    start = lax.ppermute(vectors, BOTH, SWAP)
    v0 = lax.dynamic_index_in_dim(start, pair, 0, False)
    v1 = lax.dynamic_index_in_dim(start, 1 - pair, 0, False)
    my_y, my_x = inner // 4, 2 * ((inner // 2) % 2) + x_lo
    q = lax.broadcasted_iota(jnp.int32, (16,), 0) // 4
    r = lax.broadcasted_iota(jnp.int32, (16,), 0) % 4
    from_y = (my_y + jnp.where(core == 0, r, q)) % 4
    from_x = (my_x + jnp.where(core == 0, q, r)) % 4
    rows = 32 * (4 * from_y + from_x)
    pieces_at = jnp.stack(((from_x % 2) ^ pair, PIECE * (2 * from_y + from_x // 2)))
    received, blocks, v0, v1 = lax.optimization_barrier((received, blocks, v0, v1))

    packed = partial_gram(jnp.stack((core, chip)), received, potential, own_points)
    pieces = lax.all_to_all(
        packed.reshape(8, PIECE, 128), "inner", 0, 0, axis_index_groups=CHIPS
    )

    def edges(v0, v1):
        return lax.ppermute(v0, BOTH, Z_EDGE), lax.ppermute(v1, BOTH, C_EDGE)

    z_sides, c_sides, m01, m10 = arrange(rows, blocks)
    z_sides, c_sides, v0, v1, _ = lax.optimization_barrier((z_sides, c_sides, v0, v1, packed))
    z_near, c_near = edges(z_sides, c_sides)
    zv, cv = edges(v0, v1)
    z_near, c_near, zv, cv, pieces = lax.optimization_barrier((z_near, c_near, zv, cv, pieces))
    mz, mc = edge_couplings(z_sides, z_near, c_sides, c_near)
    part0 = dot_n(m01, v1) + dot_n(mz, zv)
    part1 = dot_n(m10, v0) + dot_n(mc, cv)

    piece = jnp.sum(pieces, axis=0).astype(bf16)
    gathered = gather_plane(piece)
    (d0, new0, low0), (d1, new1, low1) = first_step(pieces_at, gathered, v0, v1, part0, part1)
    previous, current, low = [v0, v1], [new0, new1], [low0, low1]
    for step in range(1, STEPS):
        last = step == STEPS - 1
        zv, cv = edges(*low)
        acc1 = inside(d1, m10, low[1], low[0], current[1], previous[1])
        acc0 = inside(d0, m01, low[0], low[1], current[0], previous[0])
        next1 = outside(acc1, mc, cv, last)
        if last:
            moved1 = lax.ppermute(next1, BOTH, BACK)
            moved0 = lax.ppermute(outside(acc0, mz, zv, last), BOTH, BACK)
            break
        next0 = outside(acc0, mz, zv, last)
        previous, current = current, [next0[0], next1[0]]
        low = [next0[1], next1[1]]
    moved = [moved0, moved1]
    return last_placing(x_lo.reshape(1), moved)


def solution(mesh):
    placed = (
        P("elem", None, "inner", None),
        P("elem", None),
        P("elem", None, None),
        P("elem", None),
        P("elem", None, "inner"),
    )
    return jax.shard_map(
        per_device, mesh=mesh, in_specs=placed, out_specs=P("elem", None, "inner"), check_vma=False
    )
```

```python
import jax
import jax.numpy as jnp
from jax import lax
from jax.experimental import pallas as pl
from jax.experimental.pallas import tpu as pltpu
from jax.sharding import PartitionSpec as P

NB = 512
NG = 4096
F = 128
STEPS = 6
CENTER = 5.25
HALF_WIDTH = 2.75
NZ, NY, NX = 8, 4, 4
BOTH = ("elem", "inner")
SLAB = NG // 8
PACKED = 10 * 128
PIECE = PACKED // 8
bf16 = jnp.bfloat16
f32 = jnp.float32


def flat(z, y, x, c):
    z, y, x = z % NZ, y % NY, x % NX
    return (z * 2 + x % 2) * 16 + y * 4 + (x // 2) * 2 + c


PLACES = [(z, y, x, c) for z in range(NZ) for y in range(NY) for x in range(NX) for c in range(2)]


def pair_of(z, c):
    return c if z % 2 else 1 - c


def moved_to(z, y, x, c):
    pair, column = x % 2, c
    return z, y, (x // 2) * 2 + column, pair if z % 2 else 1 - pair


def along(place, axis, step):
    z, y, x, c = place
    return (z, y + step, x, c) if c == axis else (z, y, x + step, c)


def pairs_of(move):
    return [(flat(*p), flat(*move(*p))) for p in PLACES]


SWAP = pairs_of(moved_to)
BACK = [(j, i) for i, j in SWAP]
Z_EDGE = pairs_of(lambda z, y, x, c: (z + (1 if pair_of(z, c) else -1), y, x, c))
C_EDGE = pairs_of(lambda z, y, x, c: (z, y, x, 1 - c))
FIRST = [pairs_of(lambda *p: along(moved_to(*p), 0, -r)) for r in range(4)]
SECOND = [pairs_of(lambda *p: along(p, 1, -q)) for q in range(4)]
CHIPS = [[c + 2 * k for k in range(8)] for c in range(2)]


def chebyshev_norm(count):
    ratio = (CENTER - 1.0) / HALF_WIDTH
    root = ratio + (ratio * ratio - 1.0) ** 0.5
    return 0.5 * (root**count + root ** (-count))


def params(mib=16):
    return pltpu.CompilerParams(vmem_limit_bytes=mib * 1024 * 1024)


VMEM = pl.BlockSpec(memory_space=pltpu.VMEM)
SMEM = pl.BlockSpec(memory_space=pltpu.SMEM)


TINY = pl.CostEstimate(flops=1, bytes_accessed=1, transcendentals=0)
LONG = pl.CostEstimate(flops=0, bytes_accessed=1 << 26, transcendentals=0)


def dot_t(a, b):
    return lax.dot_general(a, b, (((1,), (1,)), ((), ())), preferred_element_type=f32)


def dot_n(a, b):
    return lax.dot_general(a, b, (((1,), (0,)), ((), ())), preferred_element_type=f32)


def slab_kernel(x_ref, o_ref):
    o_ref[0] = x_ref[...]


def to_slabs(basis):
    return pl.pallas_call(
        slab_kernel,
        grid=(8,),
        in_specs=[pl.BlockSpec((2, 4, 32, SLAB), lambda d: (0, 0, 0, d))],
        out_specs=pl.BlockSpec((1, 2, 4, 32, SLAB), lambda d: (d, 0, 0, 0, 0)),
        out_shape=jax.ShapeDtypeStruct((8, 2, 4, 32, SLAB), bf16),
        compiler_params=params(40),
        cost_estimate=pl.CostEstimate(flops=0, bytes_accessed=1 << 26, transcendentals=0),
        name="to_slabs",
    )(basis)


def gram_kernel(at_ref, r_ref, pot_ref, pts_ref, o_ref):
    comps = [r_ref[:, 32 * k : 32 * k + 32, :].reshape(NB, SLAB) for k in range(4)]
    lanes = pl.ds(pl.multiple_of(at_ref[1] * SLAB, SLAB), SLAB)
    potential = jnp.where(at_ref[0] == 0, pot_ref[0:1, lanes], pot_ref[1:2, lanes])
    scaled = (jnp.sqrt(potential) * comps[0].astype(f32)).astype(bf16)
    rows = lax.broadcasted_iota(jnp.int32, (SLAB, 2 * F), 0)
    pick = jnp.where(rows == pts_ref[...], 1.0, 0.0).astype(bf16)
    sign = jnp.where(lax.broadcasted_iota(jnp.int32, (1, 2 * F), 1) < F, 1.0, -1.0)
    value = dot_n(comps[0], pick) * sign
    slope = dot_n(comps[1], pick)
    jump = value.astype(bf16)
    flux = (0.5 * value - 0.25 * slope).astype(bf16)
    for big_i, big_j in ((0, 0), (1, 0), (1, 1)):
        left = slice(256 * big_i, 256 * big_i + 256)
        right = slice(256 * big_j, 256 * big_j + 256)
        kinetic = dot_t(comps[1][left], comps[1][right])
        kinetic = kinetic + dot_t(comps[2][left], comps[2][right])
        kinetic = kinetic + dot_t(comps[3][left], comps[3][right])
        total = (dot_t(scaled[left], scaled[right]) + 0.5 * kinetic) * (1.0 / NG)
        face = dot_t(flux[left], jump[right]) + dot_t(jump[left], flux[right])
        total = total + face * (1.0 / (4.0 * F))
        for i in range(2):
            for j in range(2):
                row, column = 2 * big_i + i, 2 * big_j + j
                if row >= column:
                    place = 128 * (row * (row + 1) // 2 + column)
                    block = total[128 * i : 128 * i + 128, 128 * j : 128 * j + 128]
                    o_ref[place : place + 128, :] = block


def partial_gram(at, received, potential, points):
    return pl.pallas_call(
        gram_kernel,
        in_specs=[SMEM] + [VMEM] * 3,
        out_specs=VMEM,
        out_shape=jax.ShapeDtypeStruct((PACKED, 128), f32),
        compiler_params=params(32),
        name="partial_gram",
    )(at, received, potential, points)


def unpack(packed, d_ref):
    for row in range(4):
        for column in range(row + 1):
            place = 128 * (row * (row + 1) // 2 + column)
            block = packed[place : place + 128, :]
            r, c = pl.ds(128 * row, 128), pl.ds(128 * column, 128)
            d_ref[r, c] = block
            if row > column:
                d_ref[c, r] = block.astype(f32).T.astype(bf16)


def begin(d_ref, v_ref, part_ref, new_ref, low_ref):
    v = v_ref[...]
    applied = dot_n(d_ref[...], v) + part_ref[...]
    new = (applied - CENTER * v.astype(f32)) * (1.0 / HALF_WIDTH)
    new_ref[...] = new
    low_ref[...] = new.astype(bf16)


def first_kernel(at_ref, b0, b1, b2, b3, v_ref, part_ref, d_ref, new_ref, low_ref, packed_ref):
    for q, b_ref in enumerate((b0, b1, b2, b3)):
        for r in range(4):
            k = 4 * q + r
            rows = pl.ds(pl.multiple_of(at_ref[1, k], PIECE), PIECE)
            packed_ref[at_ref[0, k], rows, :] = b_ref[r]
    unpack(packed_ref.at[0], d_ref)
    begin(d_ref, v_ref, part_ref, new_ref, low_ref)


def second_kernel(packed_ref, v_ref, part_ref, d_ref, new_ref, low_ref):
    unpack(packed_ref.at[1], d_ref)
    begin(d_ref, v_ref, part_ref, new_ref, low_ref)


def first_shapes(v):
    return [
        jax.ShapeDtypeStruct((NB, NB), bf16),
        jax.ShapeDtypeStruct(v.shape, f32),
        jax.ShapeDtypeStruct(v.shape, bf16),
    ]


def first_step(at, blocks, v, part):
    return pl.pallas_call(
        first_kernel,
        in_specs=[SMEM] + [VMEM] * 6,
        out_specs=[VMEM] * 4,
        out_shape=first_shapes(v) + [jax.ShapeDtypeStruct((2, PACKED, 128), bf16)],
        compiler_params=params(),
        name="first_step_slot0",
    )(at, *blocks, v, part)


def first_step_other(packed, v, part):
    return pl.pallas_call(
        second_kernel,
        in_specs=[VMEM] * 3,
        out_specs=[VMEM] * 3,
        out_shape=first_shapes(v),
        compiler_params=params(),
        name="first_step_slot1",
    )(packed, v, part)


def inside_kernel(d_ref, m_ref, v_ref, w_ref, cur_ref, prev_ref, o_ref):
    applied = dot_n(d_ref[...], v_ref[...]) + dot_n(m_ref[...], w_ref[...])
    applied = applied - CENTER * cur_ref[...].astype(f32)
    o_ref[...] = applied * (2.0 / HALF_WIDTH) - prev_ref[...].astype(f32)


def inside(d, m, v, w, current, previous):
    return pl.pallas_call(
        inside_kernel,
        in_specs=[VMEM] * 6,
        out_specs=VMEM,
        out_shape=jax.ShapeDtypeStruct(v.shape, f32),
        compiler_params=params(),
        name="inside",
    )(d, m, v, w, current, previous)


def outside_kernel(acc_ref, m_ref, halo_ref, new_ref, low_ref):
    new = acc_ref[...] + dot_n(m_ref[...], halo_ref[...]) * (2.0 / HALF_WIDTH)
    new_ref[...] = new
    low_ref[...] = new.astype(bf16)


def outside_last_kernel(acc_ref, m_ref, halo_ref, low_ref):
    new = acc_ref[...] + dot_n(m_ref[...], halo_ref[...]) * (2.0 / HALF_WIDTH)
    low_ref[...] = (new * (1.0 / chebyshev_norm(STEPS))).astype(bf16)


def outside(acc, m, halo, last):
    low = jax.ShapeDtypeStruct(acc.shape, bf16)
    return pl.pallas_call(
        outside_last_kernel if last else outside_kernel,
        in_specs=[VMEM] * 3,
        out_specs=VMEM if last else [VMEM] * 2,
        out_shape=low if last else [jax.ShapeDtypeStruct(acc.shape, f32), low],
        compiler_params=params(),
        name="outside",
    )(acc, m, halo)


def last_kernel(flip_ref, m0_ref, m1_ref, o_ref):
    flip = flip_ref[0]
    o_ref[flip] = m0_ref[...].astype(f32)
    o_ref[1 - flip] = m1_ref[...].astype(f32)


def last_placing(flip, moved):
    rows, columns = moved[0].shape
    part = pl.BlockSpec((rows // 4, columns), lambda i: (i, 0))
    return pl.pallas_call(
        last_kernel,
        grid=(4,),
        in_specs=[SMEM, part, part],
        out_specs=pl.BlockSpec((2, rows // 4, columns), lambda i: (0, i, 0)),
        out_shape=jax.ShapeDtypeStruct((2, rows, columns), f32),
        compiler_params=params(),
        name="last_placing",
    )(flip, *moved)


def sides_kernel(flip_ref, x_ref, pts_ref, sign_ref, o_ref):
    chunk = 512
    for slot in range(2):
        block = x_ref[jnp.bitwise_xor(flip_ref[0], slot)].reshape(64, NG)
        points = pts_ref[slot : slot + 1, :]
        found = jnp.zeros((64, 2 * F), f32)
        for part in range(NG // chunk):
            rows = lax.broadcasted_iota(jnp.int32, (chunk, 2 * F), 0) + part * chunk
            pick = jnp.where(rows == points, 1.0, 0.0).astype(bf16)
            found = found + dot_n(block[:, part * chunk : (part + 1) * chunk], pick)
        value = found[:32] * sign_ref[slot : slot + 1, :]
        flux = 0.5 * value - 0.25 * found[32:]
        for side in range(2):
            lanes = slice(F * side, F * side + F)
            o_ref[slot, 2 * side] = flux[:, lanes].astype(bf16)
            o_ref[slot, 2 * side + 1] = value[:, lanes].astype(bf16)


def local_sides(flip, basis, points, signs):
    return pl.pallas_call(
        sides_kernel,
        grid=(1,),
        in_specs=[
            SMEM,
            pl.BlockSpec((2, 2, 32, NG), lambda d: (0, 0, 0, 0)),
            VMEM,
            VMEM,
        ],
        out_specs=VMEM,
        out_shape=jax.ShapeDtypeStruct((2, 4, 32, F), bf16),
        compiler_params=params(),
        name="local_sides",
    )(flip, basis, points, signs)


def face(a_flux, a_jump, b_flux, b_jump):
    total = dot_t(a_flux, b_jump) + dot_t(a_jump, b_flux)
    return (total * (1.0 / (4.0 * F))).astype(bf16)


def arrange_kernel(rows_ref, b0, b1, b2, b3, z_ref, c_ref, m01_ref, m10_ref, inner):
    outer = (z_ref, c_ref)
    for q, b_ref in enumerate((b0, b1, b2, b3)):
        for r in range(4):
            rows = pl.ds(pl.multiple_of(rows_ref[4 * q + r], 32), 32)
            for slot in range(2):
                for k in range(2):
                    outer[slot][k, rows, :] = b_ref[r, slot, k]
                    inner[slot, k, rows, :] = b_ref[r, slot, 2 + k]
    m01_ref[...] = face(inner[0, 0], inner[0, 1], inner[1, 0], inner[1, 1])
    m10_ref[...] = face(inner[1, 0], inner[1, 1], inner[0, 0], inner[0, 1])


def arrange(rows, blocks):
    return pl.pallas_call(
        arrange_kernel,
        in_specs=[SMEM] + [VMEM] * 4,
        out_specs=[VMEM] * 4,
        out_shape=[jax.ShapeDtypeStruct((2, NB, F), bf16)] * 2
        + [jax.ShapeDtypeStruct((NB, NB), bf16)] * 2,
        scratch_shapes=[pltpu.VMEM((2, 2, NB, F), bf16)],
        compiler_params=params(),
        cost_estimate=LONG,
        name="arrange_sides",
    )(rows, *blocks)


def edge_kernel(z_ref, zr_ref, c_ref, cr_ref, mz_ref, mc_ref):
    mz_ref[...] = face(z_ref[0], z_ref[1], zr_ref[0], zr_ref[1])
    mc_ref[...] = face(c_ref[0], c_ref[1], cr_ref[0], cr_ref[1])


def edge_couplings(*sides):
    return pl.pallas_call(
        edge_kernel,
        in_specs=[VMEM] * 4,
        out_specs=[VMEM] * 2,
        out_shape=[jax.ShapeDtypeStruct((NB, NB), bf16)] * 2,
        compiler_params=params(),
        cost_estimate=TINY,
        name="edge_couplings",
    )(*sides)


def gather_plane(x):
    return gather_second(gather_first(x))


def gather_first(x):
    return jnp.stack([lax.ppermute(x, BOTH, perm) for perm in FIRST])


def gather_second(first):
    return [first] + [lax.ppermute(first, BOTH, perm) for perm in SECOND[1:]]


def per_device(basis, potential, face_index, face_match, vectors):
    elem = lax.axis_index("elem")
    inner = lax.axis_index("inner")
    x_lo, core, chip = elem % 2, inner % 2, inner // 2
    z_even = 1 - (elem // 2) % 2
    pair = core ^ z_even

    slabs = to_slabs(basis).reshape(16, 128, SLAB)
    received = lax.all_to_all(slabs, "inner", 0, 0)

    hits = face_match[:, :, None] == lax.broadcasted_iota(jnp.int32, (1, 1, F), 2)
    left_points = jnp.sum(jnp.where(hits, face_index[:, None, 0, :], 0), axis=2)
    right_points = face_index[:, 1, :]
    own_points = jnp.concatenate((right_points, left_points), axis=1) - chip * SLAB
    own_points = lax.dynamic_slice(own_points, (core, 0), (1, 2 * F))

    lr = jnp.concatenate((left_points, right_points), axis=1)
    rl = jnp.concatenate((right_points, left_points), axis=1)
    slot_points = jnp.where(
        x_lo == 0, jnp.stack((lr[0], rl[1])), jnp.stack((rl[1], lr[0]))
    )
    minus = jnp.repeat(jnp.array([[-1.0, 1.0], [1.0, -1.0]], f32), F, axis=1)
    slot_signs = jnp.where(x_lo == 0, minus, -minus)
    sides = local_sides(x_lo.reshape(1), basis, slot_points, slot_signs)
    first_sides = gather_first(sides)
    start = lax.ppermute(vectors, BOTH, SWAP)
    v0 = lax.dynamic_index_in_dim(start, pair, 0, False)
    v1 = lax.dynamic_index_in_dim(start, 1 - pair, 0, False)
    my_y, my_x = inner // 4, 2 * ((inner // 2) % 2) + x_lo
    q = lax.broadcasted_iota(jnp.int32, (16,), 0) // 4
    r = lax.broadcasted_iota(jnp.int32, (16,), 0) % 4
    from_y = (my_y + jnp.where(core == 0, r, q)) % 4
    from_x = (my_x + jnp.where(core == 0, q, r)) % 4
    rows = 32 * (4 * from_y + from_x)
    pieces_at = jnp.stack(((from_x % 2) ^ pair, PIECE * (2 * from_y + from_x // 2)))
    received, first_sides, v0, v1 = lax.optimization_barrier((received, first_sides, v0, v1))
    blocks = gather_second(first_sides)

    packed = partial_gram(jnp.stack((core, chip)), received, potential, own_points)
    pieces = lax.all_to_all(
        packed.reshape(8, PIECE, 128), "inner", 0, 0, axis_index_groups=CHIPS
    )

    def edges(v0, v1):
        return lax.ppermute(v0, BOTH, Z_EDGE), lax.ppermute(v1, BOTH, C_EDGE)

    blocks, _ = lax.optimization_barrier((blocks, packed))
    z_sides, c_sides, m01, m10 = arrange(rows, blocks)
    z_sides, c_sides, v0, v1, _ = lax.optimization_barrier((z_sides, c_sides, v0, v1, packed))
    z_near, c_near = edges(z_sides, c_sides)
    zv, cv = edges(v0, v1)
    z_near, c_near, zv, cv, pieces = lax.optimization_barrier((z_near, c_near, zv, cv, pieces))
    mz, mc = edge_couplings(z_sides, z_near, c_sides, c_near)
    part0 = dot_n(m01, v1) + dot_n(mz, zv)

    piece = jnp.sum(pieces, axis=0).astype(bf16)
    gathered = gather_plane(piece)
    d0, new0, low0, rest = first_step(pieces_at, gathered, v0, part0)
    cv, _ = lax.optimization_barrier((cv, low0))
    part1 = dot_n(m10, v0) + dot_n(mc, cv)
    d1, new1, low1 = first_step_other(rest, v1, part1)
    previous, current, low = [v0, v1], [new0, new1], [low0, low1]
    for step in range(1, STEPS):
        last = step == STEPS - 1
        zv, cv = edges(*low)
        if step == 1:
            applied = [
                dot_n(d0, low0) + dot_n(m01, low1), dot_n(d1, low1) + dot_n(m10, low0)
            ]
            acc0, acc1 = [
                2.0 * (a - CENTER * c) / HALF_WIDTH - p.astype(f32)
                for a, c, p in zip(applied, current, previous)
            ]
        else:
            acc1 = inside(d1, m10, low[1], low[0], current[1], previous[1])
            acc0 = inside(d0, m01, low[0], low[1], current[0], previous[0])
        next1 = outside(acc1, mc, cv, last)
        if last:
            moved1 = lax.ppermute(next1, BOTH, BACK)
            moved0 = lax.ppermute(outside(acc0, mz, zv, last), BOTH, BACK)
            break
        next0 = outside(acc0, mz, zv, last)
        previous, current = current, [next0[0], next1[0]]
        low = [next0[1], next1[1]]
    moved = [moved0, moved1]
    return last_placing(x_lo.reshape(1), moved)


def solution(mesh):
    placed = (
        P("elem", None, "inner", None),
        P("elem", None),
        P("elem", None, None),
        P("elem", None),
        P("elem", None, "inner"),
    )
    return jax.shard_map(
        per_device, mesh=mesh, in_specs=placed, out_specs=P("elem", None, "inner"), check_vma=False
    )
```

```python
import jax
import jax.numpy as jnp
from jax import lax
from jax.experimental import pallas as pl
from jax.experimental.pallas import tpu as pltpu
from jax.sharding import PartitionSpec as P

NB = 512
NG = 4096
F = 128
STEPS = 6
CENTER = 5.25
HALF_WIDTH = 2.75
NZ, NY, NX = 8, 4, 4
BOTH = ("elem", "inner")
SLAB = NG // 8
PACKED = 10 * 128
PIECE = PACKED // 8
bf16 = jnp.bfloat16
f32 = jnp.float32


def flat(z, y, x, c):
    z, y, x = z % NZ, y % NY, x % NX
    return (z * 2 + x % 2) * 16 + y * 4 + (x // 2) * 2 + c


PLACES = [(z, y, x, c) for z in range(NZ) for y in range(NY) for x in range(NX) for c in range(2)]


def pair_of(z, c):
    return c if z % 2 else 1 - c


def moved_to(z, y, x, c):
    pair, column = x % 2, c
    return z, y, (x // 2) * 2 + column, pair if z % 2 else 1 - pair


def along(place, axis, step):
    z, y, x, c = place
    return (z, y + step, x, c) if c == axis else (z, y, x + step, c)


def pairs_of(move):
    return [(flat(*p), flat(*move(*p))) for p in PLACES]


SWAP = pairs_of(moved_to)
BACK = [(j, i) for i, j in SWAP]
Z_EDGE = pairs_of(lambda z, y, x, c: (z + (1 if pair_of(z, c) else -1), y, x, c))
C_EDGE = pairs_of(lambda z, y, x, c: (z, y, x, 1 - c))
FIRST = [pairs_of(lambda *p: along(moved_to(*p), 0, -r)) for r in range(4)]
SECOND = [pairs_of(lambda *p: along(p, 1, -q)) for q in range(4)]
CHIPS = [[c + 2 * k for k in range(8)] for c in range(2)]


def chebyshev_norm(count):
    ratio = (CENTER - 1.0) / HALF_WIDTH
    root = ratio + (ratio * ratio - 1.0) ** 0.5
    return 0.5 * (root**count + root ** (-count))


def params(mib=16):
    return pltpu.CompilerParams(vmem_limit_bytes=mib * 1024 * 1024)


TINY = pl.CostEstimate(flops=1, bytes_accessed=1, transcendentals=0)
LONG = pl.CostEstimate(flops=0, bytes_accessed=1 << 26, transcendentals=0)
VMEM = pl.BlockSpec(memory_space=pltpu.VMEM)
SMEM = pl.BlockSpec(memory_space=pltpu.SMEM)


def dot_t(a, b):
    return lax.dot_general(a, b, (((1,), (1,)), ((), ())), preferred_element_type=f32)


def dot_n(a, b):
    return lax.dot_general(a, b, (((1,), (0,)), ((), ())), preferred_element_type=f32)


def slab_kernel(x_ref, o_ref):
    for k in range(4):
        o_ref[k] = x_ref[:, :, :, SLAB * k : SLAB * k + SLAB]


def to_slabs(basis):
    return pl.pallas_call(
        slab_kernel,
        grid=(2,),
        in_specs=[pl.BlockSpec((2, 4, 32, 4 * SLAB), lambda d: (0, 0, 0, d))],
        out_specs=pl.BlockSpec((4, 2, 4, 32, SLAB), lambda d: (d, 0, 0, 0, 0)),
        out_shape=jax.ShapeDtypeStruct((8, 2, 4, 32, SLAB), bf16),
        compiler_params=params(58),
        cost_estimate=LONG,
        name="to_slabs",
    )(basis)


def sum_kernel(x_ref, o_ref):
    o_ref[...] = jnp.sum(x_ref[...], axis=0).astype(bf16)


def sum_pieces(pieces):
    return pl.pallas_call(
        sum_kernel,
        in_specs=[VMEM],
        out_specs=VMEM,
        out_shape=jax.ShapeDtypeStruct(pieces.shape[1:], bf16),
        compiler_params=params(),
        name="sum_pieces",
    )(pieces)


def gram_kernel(at_ref, r_ref, pot_ref, pts_ref, o_ref):
    comps = [r_ref[:, 32 * k : 32 * k + 32, :].reshape(NB, SLAB) for k in range(4)]
    lanes = pl.ds(pl.multiple_of(at_ref[1] * SLAB, SLAB), SLAB)
    potential = jnp.where(at_ref[0] == 0, pot_ref[0:1, lanes], pot_ref[1:2, lanes])
    scaled = (jnp.sqrt(potential) * comps[0].astype(f32)).astype(bf16)
    rows = lax.broadcasted_iota(jnp.int32, (SLAB, 2 * F), 0)
    pick = jnp.where(rows == pts_ref[...], 1.0, 0.0).astype(bf16)
    sign = jnp.where(lax.broadcasted_iota(jnp.int32, (1, 2 * F), 1) < F, 1.0, -1.0)
    value = dot_n(comps[0], pick) * sign
    slope = dot_n(comps[1], pick)
    jump = value.astype(bf16)
    flux = (0.5 * value - 0.25 * slope).astype(bf16)
    for big_i, big_j in ((0, 0), (1, 0), (1, 1)):
        left = slice(256 * big_i, 256 * big_i + 256)
        right = slice(256 * big_j, 256 * big_j + 256)
        kinetic = dot_t(comps[1][left], comps[1][right])
        kinetic = kinetic + dot_t(comps[2][left], comps[2][right])
        kinetic = kinetic + dot_t(comps[3][left], comps[3][right])
        total = (dot_t(scaled[left], scaled[right]) + 0.5 * kinetic) * (1.0 / NG)
        face = dot_t(flux[left], jump[right]) + dot_t(jump[left], flux[right])
        total = total + face * (1.0 / (4.0 * F))
        for i in range(2):
            for j in range(2):
                row, column = 2 * big_i + i, 2 * big_j + j
                if row >= column:
                    place = 128 * (row * (row + 1) // 2 + column)
                    block = total[128 * i : 128 * i + 128, 128 * j : 128 * j + 128]
                    o_ref[place : place + 128, :] = block


def partial_gram(at, received, potential, points):
    return pl.pallas_call(
        gram_kernel,
        in_specs=[SMEM] + [VMEM] * 3,
        out_specs=VMEM,
        out_shape=jax.ShapeDtypeStruct((PACKED, 128), f32),
        compiler_params=params(),
        name="partial_gram",
    )(at, received, potential, points)


def unpack(packed, d_ref):
    for row in range(4):
        for column in range(row + 1):
            place = 128 * (row * (row + 1) // 2 + column)
            block = packed[place : place + 128, :]
            r, c = pl.ds(128 * row, 128), pl.ds(128 * column, 128)
            d_ref[r, c] = block
            if row > column:
                d_ref[c, r] = block.astype(f32).T.astype(bf16)


def begin(d_ref, v_ref, part_ref, new_ref, low_ref):
    v = v_ref[...]
    applied = dot_n(d_ref[...], v) + part_ref[...]
    new = (applied - CENTER * v.astype(f32)) * (1.0 / HALF_WIDTH)
    new_ref[...] = new
    low_ref[...] = new.astype(bf16)


def first_kernel(at_ref, b0, b1, b2, b3, v_ref, part_ref, d_ref, new_ref, low_ref, packed_ref):
    for q, b_ref in enumerate((b0, b1, b2, b3)):
        for r in range(4):
            k = 4 * q + r
            rows = pl.ds(pl.multiple_of(at_ref[1, k], PIECE), PIECE)
            packed_ref[at_ref[0, k], rows, :] = b_ref[r]
    unpack(packed_ref.at[0], d_ref)
    begin(d_ref, v_ref, part_ref, new_ref, low_ref)


def second_kernel(packed_ref, v_ref, part_ref, d_ref, new_ref, low_ref):
    unpack(packed_ref.at[1], d_ref)
    begin(d_ref, v_ref, part_ref, new_ref, low_ref)


def first_shapes(v):
    return [
        jax.ShapeDtypeStruct((NB, NB), bf16),
        jax.ShapeDtypeStruct(v.shape, f32),
        jax.ShapeDtypeStruct(v.shape, bf16),
    ]


def first_step(at, blocks, v, part):
    return pl.pallas_call(
        first_kernel,
        in_specs=[SMEM] + [VMEM] * 6,
        out_specs=[VMEM] * 4,
        out_shape=first_shapes(v) + [jax.ShapeDtypeStruct((2, PACKED, 128), bf16)],
        compiler_params=params(),
        name="first_step_slot0",
    )(at, *blocks, v, part)


def first_step_other(packed, v, part):
    return pl.pallas_call(
        second_kernel,
        in_specs=[VMEM] * 3,
        out_specs=[VMEM] * 3,
        out_shape=first_shapes(v),
        compiler_params=params(),
        name="first_step_slot1",
    )(packed, v, part)


def inside_kernel(d_ref, m_ref, v_ref, w_ref, cur_ref, prev_ref, o_ref):
    applied = dot_n(d_ref[...], v_ref[...]) + dot_n(m_ref[...], w_ref[...])
    applied = applied - CENTER * cur_ref[...].astype(f32)
    o_ref[...] = applied * (2.0 / HALF_WIDTH) - prev_ref[...].astype(f32)


def inside(d, m, v, w, current, previous):
    return pl.pallas_call(
        inside_kernel,
        in_specs=[VMEM] * 6,
        out_specs=VMEM,
        out_shape=jax.ShapeDtypeStruct(v.shape, f32),
        compiler_params=params(),
        name="inside",
    )(d, m, v, w, current, previous)


def outside_kernel(acc_ref, m_ref, halo_ref, new_ref, low_ref):
    new = acc_ref[...] + dot_n(m_ref[...], halo_ref[...]) * (2.0 / HALF_WIDTH)
    new_ref[...] = new
    low_ref[...] = new.astype(bf16)


def outside_last_kernel(acc_ref, m_ref, halo_ref, low_ref):
    new = acc_ref[...] + dot_n(m_ref[...], halo_ref[...]) * (2.0 / HALF_WIDTH)
    low_ref[...] = (new * (1.0 / chebyshev_norm(STEPS))).astype(bf16)


def outside(acc, m, halo, last):
    low = jax.ShapeDtypeStruct(acc.shape, bf16)
    return pl.pallas_call(
        outside_last_kernel if last else outside_kernel,
        in_specs=[VMEM] * 3,
        out_specs=VMEM if last else [VMEM] * 2,
        out_shape=low if last else [jax.ShapeDtypeStruct(acc.shape, f32), low],
        compiler_params=params(),
        name="outside",
    )(acc, m, halo)


def last_kernel(at_ref, m_ref, *refs):
    refs[-1][0] = m_ref[...].astype(f32)


def place_last(at, moved, out=None):
    rows, columns = moved.shape
    part = rows // 2
    more = [] if out is None else [out]
    return pl.pallas_call(
        last_kernel,
        grid_spec=pltpu.PrefetchScalarGridSpec(
            num_scalar_prefetch=1,
            grid=(2,),
            in_specs=[pl.BlockSpec((part, columns), lambda i, at: (i, 0))]
            + [pl.BlockSpec(memory_space=pl.ANY)] * len(more),
            out_specs=pl.BlockSpec((1, part, columns), lambda i, at: (at[0], i, 0)),
        ),
        out_shape=jax.ShapeDtypeStruct((2, rows, columns), f32),
        input_output_aliases={2: 0} if more else {},
        compiler_params=params(),
        name="place_last",
    )(at, moved, *more)


def sides_kernel(flip_ref, x_ref, pts_ref, sign_ref, o_ref):
    chunk = 512
    for slot in range(2):
        block = x_ref[jnp.bitwise_xor(flip_ref[0], slot)].reshape(64, NG)
        points = pts_ref[slot : slot + 1, :]
        found = jnp.zeros((64, 2 * F), f32)
        for part in range(NG // chunk):
            rows = lax.broadcasted_iota(jnp.int32, (chunk, 2 * F), 0) + part * chunk
            pick = jnp.where(rows == points, 1.0, 0.0).astype(bf16)
            found = found + dot_n(block[:, part * chunk : (part + 1) * chunk], pick)
        value = found[:32] * sign_ref[slot : slot + 1, :]
        flux = 0.5 * value - 0.25 * found[32:]
        for side in range(2):
            lanes = slice(F * side, F * side + F)
            o_ref[slot, 2 * side] = flux[:, lanes].astype(bf16)
            o_ref[slot, 2 * side + 1] = value[:, lanes].astype(bf16)


def local_sides(flip, basis, points, signs):
    return pl.pallas_call(
        sides_kernel,
        grid=(1,),
        in_specs=[
            SMEM,
            pl.BlockSpec((2, 2, 32, NG), lambda d: (0, 0, 0, 0)),
            VMEM,
            VMEM,
        ],
        out_specs=VMEM,
        out_shape=jax.ShapeDtypeStruct((2, 4, 32, F), bf16),
        compiler_params=params(),
        name="local_sides",
    )(flip, basis, points, signs)


def face(a_flux, a_jump, b_flux, b_jump):
    total = dot_t(a_flux, b_jump) + dot_t(a_jump, b_flux)
    return (total * (1.0 / (4.0 * F))).astype(bf16)


def arrange_kernel(rows_ref, b0, b1, b2, b3, z_ref, c_ref, m01_ref, m10_ref, inner):
    outer = (z_ref, c_ref)
    for q, b_ref in enumerate((b0, b1, b2, b3)):
        for r in range(4):
            rows = pl.ds(pl.multiple_of(rows_ref[4 * q + r], 32), 32)
            for slot in range(2):
                for k in range(2):
                    outer[slot][k, rows, :] = b_ref[r, slot, k]
                    inner[slot, k, rows, :] = b_ref[r, slot, 2 + k]
    m01_ref[...] = face(inner[0, 0], inner[0, 1], inner[1, 0], inner[1, 1])
    m10_ref[...] = face(inner[1, 0], inner[1, 1], inner[0, 0], inner[0, 1])


def arrange(rows, blocks):
    return pl.pallas_call(
        arrange_kernel,
        in_specs=[SMEM] + [VMEM] * 4,
        out_specs=[VMEM] * 4,
        out_shape=[jax.ShapeDtypeStruct((2, NB, F), bf16)] * 2
        + [jax.ShapeDtypeStruct((NB, NB), bf16)] * 2,
        scratch_shapes=[pltpu.VMEM((2, 2, NB, F), bf16)],
        compiler_params=params(),
        cost_estimate=LONG,
        name="arrange_sides",
    )(rows, *blocks)


def edge_kernel(z_ref, zr_ref, c_ref, cr_ref, mz_ref, mc_ref):
    mz_ref[...] = face(z_ref[0], z_ref[1], zr_ref[0], zr_ref[1])
    mc_ref[...] = face(c_ref[0], c_ref[1], cr_ref[0], cr_ref[1])


def edge_couplings(*sides):
    return pl.pallas_call(
        edge_kernel,
        in_specs=[VMEM] * 4,
        out_specs=[VMEM] * 2,
        out_shape=[jax.ShapeDtypeStruct((NB, NB), bf16)] * 2,
        compiler_params=params(),
        cost_estimate=TINY,
        name="edge_couplings",
    )(*sides)


def gather_plane(x):
    return gather_second(gather_first(x))


def gather_first(x):
    return jnp.stack([lax.ppermute(x, BOTH, perm) for perm in FIRST])


def gather_second(first):
    return [first] + [lax.ppermute(first, BOTH, perm) for perm in SECOND[1:]]


def per_device(basis, potential, face_index, face_match, vectors):
    elem = lax.axis_index("elem")
    inner = lax.axis_index("inner")
    x_lo, core, chip = elem % 2, inner % 2, inner // 2
    z_even = 1 - (elem // 2) % 2
    pair = core ^ z_even

    slabs = to_slabs(basis).reshape(16, 128, SLAB)
    received = lax.all_to_all(slabs, "inner", 0, 0)

    hits = face_match[:, :, None] == lax.broadcasted_iota(jnp.int32, (1, 1, F), 2)
    left_points = jnp.sum(jnp.where(hits, face_index[:, None, 0, :], 0), axis=2)
    right_points = face_index[:, 1, :]
    own_points = jnp.concatenate((right_points, left_points), axis=1) - chip * SLAB
    own_points = lax.dynamic_slice(own_points, (core, 0), (1, 2 * F))

    lr = jnp.concatenate((left_points, right_points), axis=1)
    rl = jnp.concatenate((right_points, left_points), axis=1)
    slot_points = jnp.where(
        x_lo == 0, jnp.stack((lr[0], rl[1])), jnp.stack((rl[1], lr[0]))
    )
    minus = jnp.repeat(jnp.array([[-1.0, 1.0], [1.0, -1.0]], f32), F, axis=1)
    slot_signs = jnp.where(x_lo == 0, minus, -minus)
    sides = local_sides(x_lo.reshape(1), basis, slot_points, slot_signs)
    first_sides = gather_first(sides)
    start = lax.ppermute(vectors, BOTH, SWAP)
    v0 = lax.dynamic_index_in_dim(start, pair, 0, False)
    v1 = lax.dynamic_index_in_dim(start, 1 - pair, 0, False)
    my_y, my_x = inner // 4, 2 * ((inner // 2) % 2) + x_lo
    q = lax.broadcasted_iota(jnp.int32, (16,), 0) // 4
    r = lax.broadcasted_iota(jnp.int32, (16,), 0) % 4
    from_y = (my_y + jnp.where(core == 0, r, q)) % 4
    from_x = (my_x + jnp.where(core == 0, q, r)) % 4
    rows = 32 * (4 * from_y + from_x)
    pieces_at = jnp.stack(((from_x % 2) ^ pair, PIECE * (2 * from_y + from_x // 2)))
    received, first_sides, v0, v1 = lax.optimization_barrier((received, first_sides, v0, v1))
    blocks = gather_second(first_sides)

    packed = partial_gram(jnp.stack((core, chip)), received, potential, own_points)
    pieces = lax.all_to_all(
        packed.reshape(8, PIECE, 128), "inner", 0, 0, axis_index_groups=CHIPS
    )

    def edges(v0, v1):
        return lax.ppermute(v0, BOTH, Z_EDGE), lax.ppermute(v1, BOTH, C_EDGE)

    blocks, _ = lax.optimization_barrier((blocks, packed))
    z_sides, c_sides, m01, m10 = arrange(rows, blocks)
    z_sides, c_sides, v0, v1, _ = lax.optimization_barrier((z_sides, c_sides, v0, v1, packed))
    z_near, c_near = edges(z_sides, c_sides)
    zv, cv = edges(v0, v1)
    z_near, c_near, zv, cv, pieces = lax.optimization_barrier((z_near, c_near, zv, cv, pieces))
    mz, mc = edge_couplings(z_sides, z_near, c_sides, c_near)
    part0 = dot_n(m01, v1) + dot_n(mz, zv)

    piece = sum_pieces(pieces)
    gathered = gather_plane(piece)
    d0, new0, low0, rest = first_step(pieces_at, gathered, v0, part0)
    cv, _ = lax.optimization_barrier((cv, low0))
    part1 = dot_n(m10, v0) + dot_n(mc, cv)
    d1, new1, low1 = first_step_other(rest, v1, part1)
    previous, current, low = [v0, v1], [new0, new1], [low0, low1]
    for step in range(1, STEPS):
        last = step == STEPS - 1
        zv, cv = edges(*low)
        if step == 1:
            applied = [
                dot_n(d0, low0) + dot_n(m01, low1), dot_n(d1, low1) + dot_n(m10, low0)
            ]
            acc0, acc1 = [
                2.0 * (a - CENTER * c) / HALF_WIDTH - p.astype(f32)
                for a, c, p in zip(applied, current, previous)
            ]
        else:
            acc1 = inside(d1, m10, low[1], low[0], current[1], previous[1])
            acc0 = inside(d0, m01, low[0], low[1], current[0], previous[0])
        next1 = outside(acc1, mc, cv, last)
        if last:
            moved1 = lax.ppermute(next1, BOTH, BACK)
            moved0 = lax.ppermute(outside(acc0, mz, zv, last), BOTH, BACK)
            break
        next0 = outside(acc0, mz, zv, last)
        previous, current = current, [next0[0], next1[0]]
        low = [next0[1], next1[1]]
    out = place_last((1 - x_lo).reshape(1), moved1)
    return place_last(x_lo.reshape(1), moved0, out)


def solution(mesh):
    placed = (
        P("elem", None, "inner", None),
        P("elem", None),
        P("elem", None, None),
        P("elem", None),
        P("elem", None, "inner"),
    )
    return jax.shard_map(
        per_device, mesh=mesh, in_specs=placed, out_specs=P("elem", None, "inner"), check_vma=False
    )
```

```python
import jax
import jax.numpy as jnp
from jax import lax
from jax.experimental import pallas as pl
from jax.experimental.pallas import tpu as pltpu
from jax.sharding import PartitionSpec as P

NB = 512
NG = 4096
F = 128
STEPS = 6
CENTER = 5.25
HALF_WIDTH = 2.75
NZ, NY, NX = 8, 4, 4
BOTH = ("elem", "inner")
SLAB = NG // 8
PACKED = 10 * 128
PIECE = PACKED // 8
bf16 = jnp.bfloat16
f32 = jnp.float32


def flat(z, y, x, c):
    z, y, x = z % NZ, y % NY, x % NX
    return (z * 2 + x % 2) * 16 + y * 4 + (x // 2) * 2 + c


PLACES = [(z, y, x, c) for z in range(NZ) for y in range(NY) for x in range(NX) for c in range(2)]


def pair_of(z, c):
    return c if z % 2 else 1 - c


def moved_to(z, y, x, c):
    pair, column = x % 2, c
    return z, y, (x // 2) * 2 + column, pair if z % 2 else 1 - pair


def along(place, axis, step):
    z, y, x, c = place
    return (z, y + step, x, c) if c == axis else (z, y, x + step, c)


def pairs_of(move):
    return [(flat(*p), flat(*move(*p))) for p in PLACES]


SWAP = pairs_of(moved_to)
BACK = [(j, i) for i, j in SWAP]
Z_EDGE = pairs_of(lambda z, y, x, c: (z + (1 if pair_of(z, c) else -1), y, x, c))
C_EDGE = pairs_of(lambda z, y, x, c: (z, y, x, 1 - c))
FIRST = [pairs_of(lambda *p: along(moved_to(*p), 0, -r)) for r in range(4)]
SECOND = [pairs_of(lambda *p: along(p, 1, -q)) for q in range(4)]
CHIPS = [[c + 2 * k for k in range(8)] for c in range(2)]


def chebyshev_norm(count):
    ratio = (CENTER - 1.0) / HALF_WIDTH
    root = ratio + (ratio * ratio - 1.0) ** 0.5
    return 0.5 * (root**count + root ** (-count))


def params(mib=16):
    return pltpu.CompilerParams(vmem_limit_bytes=mib * 1024 * 1024)


TINY = pl.CostEstimate(flops=1, bytes_accessed=1, transcendentals=0)
LONG = pl.CostEstimate(flops=0, bytes_accessed=1 << 26, transcendentals=0)
VMEM = pl.BlockSpec(memory_space=pltpu.VMEM)
SMEM = pl.BlockSpec(memory_space=pltpu.SMEM)


def dot_t(a, b):
    return lax.dot_general(a, b, (((1,), (1,)), ((), ())), preferred_element_type=f32)


def dot_n(a, b):
    return lax.dot_general(a, b, (((1,), (0,)), ((), ())), preferred_element_type=f32)


def slab_kernel(x_ref, o_ref):
    for k in range(4):
        o_ref[k] = x_ref[:, :, :, SLAB * k : SLAB * k + SLAB]


def to_slabs(basis):
    return pl.pallas_call(
        slab_kernel,
        grid=(2,),
        in_specs=[pl.BlockSpec((2, 4, 32, 4 * SLAB), lambda d: (0, 0, 0, d))],
        out_specs=pl.BlockSpec((4, 2, 4, 32, SLAB), lambda d: (d, 0, 0, 0, 0)),
        out_shape=jax.ShapeDtypeStruct((8, 2, 4, 32, SLAB), bf16),
        compiler_params=params(58),
        cost_estimate=LONG,
        name="to_slabs",
    )(basis)


def sum_kernel(x_ref, o_ref):
    o_ref[...] = jnp.sum(x_ref[...], axis=0).astype(bf16)


def sum_pieces(pieces):
    return pl.pallas_call(
        sum_kernel,
        in_specs=[VMEM],
        out_specs=VMEM,
        out_shape=jax.ShapeDtypeStruct(pieces.shape[1:], bf16),
        compiler_params=params(),
        name="sum_pieces",
    )(pieces)


def packed_blocks():
    for big_i, big_j in ((0, 0), (1, 0), (1, 1)):
        small = []
        for i in range(2):
            for j in range(2):
                row, column = 2 * big_i + i, 2 * big_j + j
                if row >= column:
                    small.append((128 * i, 128 * j, 128 * (row * (row + 1) // 2 + column)))
        yield slice(256 * big_i, 256 * big_i + 256), slice(256 * big_j, 256 * big_j + 256), small


def gram_kernel(at_ref, r_ref, pot_ref, pts_ref, o_ref):
    one, two = [r_ref[:, 32 * k : 32 * k + 32, :].reshape(NB, SLAB) for k in range(2)]

    @pl.when(pl.program_id(0) == 0)
    def _():
        lanes = pl.ds(pl.multiple_of(at_ref[1] * SLAB, SLAB), SLAB)
        potential = jnp.where(at_ref[0] == 0, pot_ref[0:1, lanes], pot_ref[1:2, lanes])
        scaled = (jnp.sqrt(potential) * one.astype(f32)).astype(bf16)
        rows = lax.broadcasted_iota(jnp.int32, (SLAB, 2 * F), 0)
        pick = jnp.where(rows == pts_ref[...], 1.0, 0.0).astype(bf16)
        sign = jnp.where(lax.broadcasted_iota(jnp.int32, (1, 2 * F), 1) < F, 1.0, -1.0)
        value = dot_n(one, pick) * sign
        slope = dot_n(two, pick)
        jump = value.astype(bf16)
        flux = (0.5 * value - 0.25 * slope).astype(bf16)
        for left, right, small in packed_blocks():
            total = dot_t(scaled[left], scaled[right]) + 0.5 * dot_t(two[left], two[right])
            face = dot_t(flux[left], jump[right]) + dot_t(jump[left], flux[right])
            total = total * (1.0 / NG) + face * (1.0 / (4.0 * F))
            for i, j, place in small:
                o_ref[place : place + 128, :] = total[i : i + 128, j : j + 128]

    @pl.when(pl.program_id(0) == 1)
    def _():
        for left, right, small in packed_blocks():
            total = dot_t(one[left], one[right]) + dot_t(two[left], two[right])
            total = total * (0.5 / NG)
            for i, j, place in small:
                o_ref[place : place + 128, :] += total[i : i + 128, j : j + 128]


def partial_gram(at, received, potential, points):
    return pl.pallas_call(
        gram_kernel,
        grid=(2,),
        in_specs=[SMEM, pl.BlockSpec((16, 64, SLAB), lambda h: (0, h, 0)), VMEM, VMEM],
        out_specs=pl.BlockSpec((PACKED, 128), lambda h: (0, 0)),
        out_shape=jax.ShapeDtypeStruct((PACKED, 128), f32),
        compiler_params=params(),
        name="partial_gram",
    )(at, received, potential, points)


def unpack(packed, d_ref):
    for row in range(4):
        for column in range(row + 1):
            place = 128 * (row * (row + 1) // 2 + column)
            block = packed[place : place + 128, :]
            r, c = pl.ds(128 * row, 128), pl.ds(128 * column, 128)
            d_ref[r, c] = block
            if row > column:
                d_ref[c, r] = block.astype(f32).T.astype(bf16)


def begin(d_ref, v_ref, part_ref, new_ref, low_ref):
    v = v_ref[...]
    applied = dot_n(d_ref[...], v) + part_ref[...]
    new = (applied - CENTER * v.astype(f32)) * (1.0 / HALF_WIDTH)
    new_ref[...] = new
    low_ref[...] = new.astype(bf16)


def first_kernel(at_ref, b0, b1, b2, b3, v_ref, part_ref, d_ref, new_ref, low_ref, packed_ref):
    for q, b_ref in enumerate((b0, b1, b2, b3)):
        for r in range(4):
            k = 4 * q + r
            rows = pl.ds(pl.multiple_of(at_ref[1, k], PIECE), PIECE)
            packed_ref[at_ref[0, k], rows, :] = b_ref[r]
    unpack(packed_ref.at[0], d_ref)
    begin(d_ref, v_ref, part_ref, new_ref, low_ref)


def second_kernel(packed_ref, v_ref, part_ref, d_ref, new_ref, low_ref):
    unpack(packed_ref.at[1], d_ref)
    begin(d_ref, v_ref, part_ref, new_ref, low_ref)


def first_shapes(v):
    return [
        jax.ShapeDtypeStruct((NB, NB), bf16),
        jax.ShapeDtypeStruct(v.shape, f32),
        jax.ShapeDtypeStruct(v.shape, bf16),
    ]


def first_step(at, blocks, v, part):
    return pl.pallas_call(
        first_kernel,
        in_specs=[SMEM] + [VMEM] * 6,
        out_specs=[VMEM] * 4,
        out_shape=first_shapes(v) + [jax.ShapeDtypeStruct((2, PACKED, 128), bf16)],
        compiler_params=params(),
        name="first_step_slot0",
    )(at, *blocks, v, part)


def first_step_other(packed, v, part):
    return pl.pallas_call(
        second_kernel,
        in_specs=[VMEM] * 3,
        out_specs=[VMEM] * 3,
        out_shape=first_shapes(v),
        compiler_params=params(),
        name="first_step_slot1",
    )(packed, v, part)


def inside_kernel(d_ref, m_ref, v_ref, w_ref, cur_ref, prev_ref, o_ref):
    applied = dot_n(d_ref[...], v_ref[...]) + dot_n(m_ref[...], w_ref[...])
    applied = applied - CENTER * cur_ref[...].astype(f32)
    o_ref[...] = applied * (2.0 / HALF_WIDTH) - prev_ref[...].astype(f32)


def inside(d, m, v, w, current, previous):
    return pl.pallas_call(
        inside_kernel,
        in_specs=[VMEM] * 6,
        out_specs=VMEM,
        out_shape=jax.ShapeDtypeStruct(v.shape, f32),
        compiler_params=params(),
        name="inside",
    )(d, m, v, w, current, previous)


def outside_kernel(acc_ref, m_ref, halo_ref, new_ref, low_ref):
    new = acc_ref[...] + dot_n(m_ref[...], halo_ref[...]) * (2.0 / HALF_WIDTH)
    new_ref[...] = new
    low_ref[...] = new.astype(bf16)


def outside_last_kernel(acc_ref, m_ref, halo_ref, low_ref):
    new = acc_ref[...] + dot_n(m_ref[...], halo_ref[...]) * (2.0 / HALF_WIDTH)
    low_ref[...] = (new * (1.0 / chebyshev_norm(STEPS))).astype(bf16)


def outside(acc, m, halo, last):
    low = jax.ShapeDtypeStruct(acc.shape, bf16)
    return pl.pallas_call(
        outside_last_kernel if last else outside_kernel,
        in_specs=[VMEM] * 3,
        out_specs=VMEM if last else [VMEM] * 2,
        out_shape=low if last else [jax.ShapeDtypeStruct(acc.shape, f32), low],
        compiler_params=params(),
        name="outside",
    )(acc, m, halo)


def last_kernel(at_ref, m_ref, *refs):
    refs[-1][0] = m_ref[...].astype(f32)


def place_last(at, moved, out=None):
    rows, columns = moved.shape
    part = rows // 2
    more = [] if out is None else [out]
    return pl.pallas_call(
        last_kernel,
        grid_spec=pltpu.PrefetchScalarGridSpec(
            num_scalar_prefetch=1,
            grid=(2,),
            in_specs=[pl.BlockSpec((part, columns), lambda i, at: (i, 0))]
            + [pl.BlockSpec(memory_space=pl.ANY)] * len(more),
            out_specs=pl.BlockSpec((1, part, columns), lambda i, at: (at[0], i, 0)),
        ),
        out_shape=jax.ShapeDtypeStruct((2, rows, columns), f32),
        input_output_aliases={2: 0} if more else {},
        compiler_params=params(),
        name="place_last",
    )(at, moved, *more)


def sides_kernel(flip_ref, x_ref, pts_ref, sign_ref, o_ref):
    chunk = 512
    for slot in range(2):
        block = x_ref[jnp.bitwise_xor(flip_ref[0], slot)].reshape(64, NG)
        points = pts_ref[slot : slot + 1, :]
        found = jnp.zeros((64, 2 * F), f32)
        for part in range(NG // chunk):
            rows = lax.broadcasted_iota(jnp.int32, (chunk, 2 * F), 0) + part * chunk
            pick = jnp.where(rows == points, 1.0, 0.0).astype(bf16)
            found = found + dot_n(block[:, part * chunk : (part + 1) * chunk], pick)
        value = found[:32] * sign_ref[slot : slot + 1, :]
        flux = 0.5 * value - 0.25 * found[32:]
        for side in range(2):
            lanes = slice(F * side, F * side + F)
            o_ref[slot, 2 * side] = flux[:, lanes].astype(bf16)
            o_ref[slot, 2 * side + 1] = value[:, lanes].astype(bf16)


def local_sides(flip, basis, points, signs):
    return pl.pallas_call(
        sides_kernel,
        grid=(1,),
        in_specs=[
            SMEM,
            pl.BlockSpec((2, 2, 32, NG), lambda d: (0, 0, 0, 0)),
            VMEM,
            VMEM,
        ],
        out_specs=VMEM,
        out_shape=jax.ShapeDtypeStruct((2, 4, 32, F), bf16),
        compiler_params=params(),
        name="local_sides",
    )(flip, basis, points, signs)


def face(a_flux, a_jump, b_flux, b_jump):
    total = dot_t(a_flux, b_jump) + dot_t(a_jump, b_flux)
    return (total * (1.0 / (4.0 * F))).astype(bf16)


def arrange_kernel(rows_ref, b0, b1, b2, b3, z_ref, c_ref, m01_ref, m10_ref, inner):
    outer = (z_ref, c_ref)
    for q, b_ref in enumerate((b0, b1, b2, b3)):
        for r in range(4):
            rows = pl.ds(pl.multiple_of(rows_ref[4 * q + r], 32), 32)
            for slot in range(2):
                for k in range(2):
                    outer[slot][k, rows, :] = b_ref[r, slot, k]
                    inner[slot, k, rows, :] = b_ref[r, slot, 2 + k]
    m01_ref[...] = face(inner[0, 0], inner[0, 1], inner[1, 0], inner[1, 1])
    m10_ref[...] = face(inner[1, 0], inner[1, 1], inner[0, 0], inner[0, 1])


def arrange(rows, blocks):
    return pl.pallas_call(
        arrange_kernel,
        in_specs=[SMEM] + [VMEM] * 4,
        out_specs=[VMEM] * 4,
        out_shape=[jax.ShapeDtypeStruct((2, NB, F), bf16)] * 2
        + [jax.ShapeDtypeStruct((NB, NB), bf16)] * 2,
        scratch_shapes=[pltpu.VMEM((2, 2, NB, F), bf16)],
        compiler_params=params(),
        cost_estimate=LONG,
        name="arrange_sides",
    )(rows, *blocks)


def edge_kernel(z_ref, zr_ref, c_ref, cr_ref, mz_ref, mc_ref):
    mz_ref[...] = face(z_ref[0], z_ref[1], zr_ref[0], zr_ref[1])
    mc_ref[...] = face(c_ref[0], c_ref[1], cr_ref[0], cr_ref[1])


def edge_couplings(*sides):
    return pl.pallas_call(
        edge_kernel,
        in_specs=[VMEM] * 4,
        out_specs=[VMEM] * 2,
        out_shape=[jax.ShapeDtypeStruct((NB, NB), bf16)] * 2,
        compiler_params=params(),
        cost_estimate=TINY,
        name="edge_couplings",
    )(*sides)


def gather_plane(x):
    return gather_second(gather_first(x))


def gather_first(x):
    return jnp.stack([lax.ppermute(x, BOTH, perm) for perm in FIRST])


def gather_second(first):
    return [first] + [lax.ppermute(first, BOTH, perm) for perm in SECOND[1:]]


def per_device(basis, potential, face_index, face_match, vectors):
    elem = lax.axis_index("elem")
    inner = lax.axis_index("inner")
    x_lo, core, chip = elem % 2, inner % 2, inner // 2
    z_even = 1 - (elem // 2) % 2
    pair = core ^ z_even

    slabs = to_slabs(basis).reshape(16, 128, SLAB)
    received = lax.all_to_all(slabs, "inner", 0, 0)

    hits = face_match[:, :, None] == lax.broadcasted_iota(jnp.int32, (1, 1, F), 2)
    left_points = jnp.sum(jnp.where(hits, face_index[:, None, 0, :], 0), axis=2)
    right_points = face_index[:, 1, :]
    own_points = jnp.concatenate((right_points, left_points), axis=1) - chip * SLAB
    own_points = lax.dynamic_slice(own_points, (core, 0), (1, 2 * F))

    lr = jnp.concatenate((left_points, right_points), axis=1)
    rl = jnp.concatenate((right_points, left_points), axis=1)
    slot_points = jnp.where(
        x_lo == 0, jnp.stack((lr[0], rl[1])), jnp.stack((rl[1], lr[0]))
    )
    minus = jnp.repeat(jnp.array([[-1.0, 1.0], [1.0, -1.0]], f32), F, axis=1)
    slot_signs = jnp.where(x_lo == 0, minus, -minus)
    sides = local_sides(x_lo.reshape(1), basis, slot_points, slot_signs)
    first_sides = gather_first(sides)
    vectors, _ = lax.optimization_barrier((vectors, sides))
    start = lax.ppermute(vectors, BOTH, SWAP)
    v0 = lax.dynamic_index_in_dim(start, pair, 0, False)
    v1 = lax.dynamic_index_in_dim(start, 1 - pair, 0, False)
    my_y, my_x = inner // 4, 2 * ((inner // 2) % 2) + x_lo
    q = lax.broadcasted_iota(jnp.int32, (16,), 0) // 4
    r = lax.broadcasted_iota(jnp.int32, (16,), 0) % 4
    from_y = (my_y + jnp.where(core == 0, r, q)) % 4
    from_x = (my_x + jnp.where(core == 0, q, r)) % 4
    rows = 32 * (4 * from_y + from_x)
    pieces_at = jnp.stack(((from_x % 2) ^ pair, PIECE * (2 * from_y + from_x // 2)))
    received, first_sides = lax.optimization_barrier((received, first_sides))
    blocks = gather_second(first_sides)

    packed = partial_gram(jnp.stack((core, chip)), received, potential, own_points)
    pieces = lax.all_to_all(
        packed.reshape(8, PIECE, 128), "inner", 0, 0, axis_index_groups=CHIPS
    )

    def edges(v0, v1):
        return lax.ppermute(v0, BOTH, Z_EDGE), lax.ppermute(v1, BOTH, C_EDGE)

    blocks, _ = lax.optimization_barrier((blocks, packed))
    z_sides, c_sides, m01, m10 = arrange(rows, blocks)
    z_sides, c_sides, v0, v1, _ = lax.optimization_barrier((z_sides, c_sides, v0, v1, packed))
    z_near, c_near = edges(z_sides, c_sides)
    zv, cv = edges(v0, v1)
    z_near, c_near, zv, cv, pieces = lax.optimization_barrier((z_near, c_near, zv, cv, pieces))
    mz, mc = edge_couplings(z_sides, z_near, c_sides, c_near)
    part0 = dot_n(m01, v1) + dot_n(mz, zv)

    piece = sum_pieces(pieces)
    gathered = gather_plane(piece)
    d0, new0, low0, rest = first_step(pieces_at, gathered, v0, part0)
    cv, _ = lax.optimization_barrier((cv, low0))
    part1 = dot_n(m10, v0) + dot_n(mc, cv)
    d1, new1, low1 = first_step_other(rest, v1, part1)
    previous, current, low = [v0, v1], [new0, new1], [low0, low1]
    for step in range(1, STEPS):
        last = step == STEPS - 1
        zv, cv = edges(*low)
        if step == 1:
            applied = [
                dot_n(d0, low0) + dot_n(m01, low1), dot_n(d1, low1) + dot_n(m10, low0)
            ]
            acc0, acc1 = [
                2.0 * (a - CENTER * c) / HALF_WIDTH - p.astype(f32)
                for a, c, p in zip(applied, current, previous)
            ]
        else:
            acc1 = inside(d1, m10, low[1], low[0], current[1], previous[1])
            acc0 = inside(d0, m01, low[0], low[1], current[0], previous[0])
        next1 = outside(acc1, mc, cv, last)
        if last:
            moved1 = lax.ppermute(next1, BOTH, BACK)
            moved0 = lax.ppermute(outside(acc0, mz, zv, last), BOTH, BACK)
            break
        next0 = outside(acc0, mz, zv, last)
        previous, current = current, [next0[0], next1[0]]
        low = [next0[1], next1[1]]
    out = place_last((1 - x_lo).reshape(1), moved1)
    return place_last(x_lo.reshape(1), moved0, out)


def solution(mesh):
    placed = (
        P("elem", None, "inner", None),
        P("elem", None),
        P("elem", None, None),
        P("elem", None),
        P("elem", None, "inner"),
    )
    return jax.shard_map(
        per_device, mesh=mesh, in_specs=placed, out_specs=P("elem", None, "inner"), check_vma=False
    )
```

```python
import jax
import jax.numpy as jnp
from jax import lax
from jax.experimental import pallas as pl
from jax.experimental.pallas import tpu as pltpu
from jax.sharding import PartitionSpec as P

NB = 512
NG = 4096
F = 128
STEPS = 6
CENTER = 5.25
HALF_WIDTH = 2.75
NZ, NY, NX = 8, 4, 4
BOTH = ("elem", "inner")
SLAB = NG // 8
PACKED = 10 * 128
PIECE = PACKED // 8
bf16 = jnp.bfloat16
f32 = jnp.float32


def flat(z, y, x, c):
    z, y, x = z % NZ, y % NY, x % NX
    return (z * 2 + x % 2) * 16 + y * 4 + (x // 2) * 2 + c


PLACES = [(z, y, x, c) for z in range(NZ) for y in range(NY) for x in range(NX) for c in range(2)]


def pair_of(z, c):
    return c if z % 2 else 1 - c


def moved_to(z, y, x, c):
    pair, column = x % 2, c
    return z, y, (x // 2) * 2 + column, pair if z % 2 else 1 - pair


def along(place, axis, step):
    z, y, x, c = place
    return (z, y + step, x, c) if c == axis else (z, y, x + step, c)


def pairs_of(move):
    return [(flat(*p), flat(*move(*p))) for p in PLACES]


SWAP = pairs_of(moved_to)
BACK = [(j, i) for i, j in SWAP]
Z_EDGE = pairs_of(lambda z, y, x, c: (z + (1 if pair_of(z, c) else -1), y, x, c))
C_EDGE = pairs_of(lambda z, y, x, c: (z, y, x, 1 - c))
FIRST = [pairs_of(lambda *p: along(moved_to(*p), 0, -r)) for r in range(4)]
SECOND = [pairs_of(lambda *p: along(p, 1, -q)) for q in range(4)]
CHIPS = [[c + 2 * k for k in range(8)] for c in range(2)]


def chebyshev_norm(count):
    ratio = (CENTER - 1.0) / HALF_WIDTH
    root = ratio + (ratio * ratio - 1.0) ** 0.5
    return 0.5 * (root**count + root ** (-count))


def params(mib=16):
    return pltpu.CompilerParams(vmem_limit_bytes=mib * 1024 * 1024)


TINY = pl.CostEstimate(flops=1, bytes_accessed=1, transcendentals=0)
LONG = pl.CostEstimate(flops=0, bytes_accessed=1 << 26, transcendentals=0)
VMEM = pl.BlockSpec(memory_space=pltpu.VMEM)
SMEM = pl.BlockSpec(memory_space=pltpu.SMEM)


def dot_t(a, b):
    return lax.dot_general(a, b, (((1,), (1,)), ((), ())), preferred_element_type=f32)


def dot_n(a, b):
    return lax.dot_general(a, b, (((1,), (0,)), ((), ())), preferred_element_type=f32)


def slab_kernel(x_ref, o_ref):
    for k in range(4):
        o_ref[k] = x_ref[:, :, :, SLAB * k : SLAB * k + SLAB]


def to_slabs(basis):
    return pl.pallas_call(
        slab_kernel,
        grid=(2,),
        in_specs=[pl.BlockSpec((2, 4, 32, 4 * SLAB), lambda d: (0, 0, 0, d))],
        out_specs=pl.BlockSpec((4, 2, 4, 32, SLAB), lambda d: (d, 0, 0, 0, 0)),
        out_shape=jax.ShapeDtypeStruct((8, 2, 4, 32, SLAB), bf16),
        compiler_params=params(58),
        cost_estimate=LONG,
        name="to_slabs",
    )(basis)


def sum_kernel(x_ref, o_ref):
    o_ref[...] = jnp.sum(x_ref[...], axis=0).astype(bf16)


def sum_pieces(pieces):
    return pl.pallas_call(
        sum_kernel,
        in_specs=[VMEM],
        out_specs=VMEM,
        out_shape=jax.ShapeDtypeStruct(pieces.shape[1:], bf16),
        compiler_params=params(),
        name="sum_pieces",
    )(pieces)


def gram_kernel(at_ref, r_ref, pot_ref, pts_ref, o_ref):
    comps = [r_ref[:, 32 * k : 32 * k + 32, :].reshape(NB, SLAB) for k in range(4)]
    lanes = pl.ds(pl.multiple_of(at_ref[1] * SLAB, SLAB), SLAB)
    potential = jnp.where(at_ref[0] == 0, pot_ref[0:1, lanes], pot_ref[1:2, lanes])
    scaled = (jnp.sqrt(potential) * comps[0].astype(f32)).astype(bf16)
    rows = lax.broadcasted_iota(jnp.int32, (SLAB, 2 * F), 0)
    pick = jnp.where(rows == pts_ref[...], 1.0, 0.0).astype(bf16)
    sign = jnp.where(lax.broadcasted_iota(jnp.int32, (1, 2 * F), 1) < F, 1.0, -1.0)
    value = dot_n(comps[0], pick) * sign
    slope = dot_n(comps[1], pick)
    jump = value.astype(bf16)
    flux = (0.5 * value - 0.25 * slope).astype(bf16)
    for big_i, big_j in ((0, 0), (1, 0), (1, 1)):
        left = slice(256 * big_i, 256 * big_i + 256)
        right = slice(256 * big_j, 256 * big_j + 256)
        kinetic = dot_t(comps[1][left], comps[1][right])
        kinetic = kinetic + dot_t(comps[2][left], comps[2][right])
        kinetic = kinetic + dot_t(comps[3][left], comps[3][right])
        total = (dot_t(scaled[left], scaled[right]) + 0.5 * kinetic) * (1.0 / NG)
        face = dot_t(flux[left], jump[right]) + dot_t(jump[left], flux[right])
        total = total + face * (1.0 / (4.0 * F))
        for i in range(2):
            for j in range(2):
                row, column = 2 * big_i + i, 2 * big_j + j
                if row >= column:
                    place = 128 * (row * (row + 1) // 2 + column)
                    block = total[128 * i : 128 * i + 128, 128 * j : 128 * j + 128]
                    o_ref[place : place + 128, :] = block


def partial_gram(at, received, potential, points):
    return pl.pallas_call(
        gram_kernel,
        in_specs=[SMEM] + [VMEM] * 3,
        out_specs=VMEM,
        out_shape=jax.ShapeDtypeStruct((PACKED, 128), f32),
        compiler_params=params(),
        name="partial_gram",
    )(at, received, potential, points)


def unpack(packed, d_ref):
    for row in range(4):
        for column in range(row + 1):
            place = 128 * (row * (row + 1) // 2 + column)
            block = packed[place : place + 128, :]
            r, c = pl.ds(128 * row, 128), pl.ds(128 * column, 128)
            d_ref[r, c] = block
            if row > column:
                d_ref[c, r] = block.astype(f32).T.astype(bf16)


def begin(d_ref, v_ref, part_ref, new_ref, low_ref):
    v = v_ref[...]
    applied = dot_n(d_ref[...], v) + part_ref[...]
    new = (applied - CENTER * v.astype(f32)) * (1.0 / HALF_WIDTH)
    new_ref[...] = new
    low_ref[...] = new.astype(bf16)


def first_kernel(at_ref, b0, b1, b2, b3, v_ref, part_ref, d_ref, new_ref, low_ref, packed_ref):
    for q, b_ref in enumerate((b0, b1, b2, b3)):
        for r in range(4):
            k = 4 * q + r
            rows = pl.ds(pl.multiple_of(at_ref[1, k], PIECE), PIECE)
            packed_ref[at_ref[0, k], rows, :] = b_ref[r]
    unpack(packed_ref.at[0], d_ref)
    begin(d_ref, v_ref, part_ref, new_ref, low_ref)


def second_kernel(packed_ref, v_ref, part_ref, d_ref, new_ref, low_ref):
    unpack(packed_ref.at[1], d_ref)
    begin(d_ref, v_ref, part_ref, new_ref, low_ref)


def first_shapes(v):
    return [
        jax.ShapeDtypeStruct((NB, NB), bf16),
        jax.ShapeDtypeStruct(v.shape, f32),
        jax.ShapeDtypeStruct(v.shape, bf16),
    ]


def first_step(at, blocks, v, part):
    return pl.pallas_call(
        first_kernel,
        in_specs=[SMEM] + [VMEM] * 6,
        out_specs=[VMEM] * 4,
        out_shape=first_shapes(v) + [jax.ShapeDtypeStruct((2, PACKED, 128), bf16)],
        compiler_params=params(),
        name="first_step_slot0",
    )(at, *blocks, v, part)


def first_step_other(packed, v, part):
    return pl.pallas_call(
        second_kernel,
        in_specs=[VMEM] * 3,
        out_specs=[VMEM] * 3,
        out_shape=first_shapes(v),
        compiler_params=params(),
        name="first_step_slot1",
    )(packed, v, part)


def inside_kernel(d_ref, m_ref, v_ref, w_ref, cur_ref, prev_ref, o_ref):
    applied = dot_n(d_ref[...], v_ref[...]) + dot_n(m_ref[...], w_ref[...])
    applied = applied - CENTER * cur_ref[...].astype(f32)
    o_ref[...] = applied * (2.0 / HALF_WIDTH) - prev_ref[...].astype(f32)


def inside(d, m, v, w, current, previous):
    return pl.pallas_call(
        inside_kernel,
        in_specs=[VMEM] * 6,
        out_specs=VMEM,
        out_shape=jax.ShapeDtypeStruct(v.shape, f32),
        compiler_params=params(),
        name="inside",
    )(d, m, v, w, current, previous)


def outside_kernel(acc_ref, m_ref, halo_ref, new_ref, low_ref):
    new = acc_ref[...] + dot_n(m_ref[...], halo_ref[...]) * (2.0 / HALF_WIDTH)
    new_ref[...] = new
    low_ref[...] = new.astype(bf16)


def outside_last_kernel(acc_ref, m_ref, halo_ref, low_ref):
    new = acc_ref[...] + dot_n(m_ref[...], halo_ref[...]) * (2.0 / HALF_WIDTH)
    low_ref[...] = (new * (1.0 / chebyshev_norm(STEPS))).astype(bf16)


def outside(acc, m, halo, last):
    low = jax.ShapeDtypeStruct(acc.shape, bf16)
    return pl.pallas_call(
        outside_last_kernel if last else outside_kernel,
        in_specs=[VMEM] * 3,
        out_specs=VMEM if last else [VMEM] * 2,
        out_shape=low if last else [jax.ShapeDtypeStruct(acc.shape, f32), low],
        compiler_params=params(),
        name="outside",
    )(acc, m, halo)


def last_kernel(at_ref, m_ref, *refs):
    refs[-1][0] = m_ref[...].astype(f32)


def place_last(at, moved, out=None):
    rows, columns = moved.shape
    part = rows // 2
    more = [] if out is None else [out]
    return pl.pallas_call(
        last_kernel,
        grid_spec=pltpu.PrefetchScalarGridSpec(
            num_scalar_prefetch=1,
            grid=(2,),
            in_specs=[pl.BlockSpec((part, columns), lambda i, at: (i, 0))]
            + [pl.BlockSpec(memory_space=pl.ANY)] * len(more),
            out_specs=pl.BlockSpec((1, part, columns), lambda i, at: (at[0], i, 0)),
        ),
        out_shape=jax.ShapeDtypeStruct((2, rows, columns), f32),
        input_output_aliases={2: 0} if more else {},
        compiler_params=params(),
        name="place_last",
    )(at, moved, *more)


def sides_kernel(flip_ref, x_ref, pts_ref, sign_ref, o_ref):
    chunk = 512
    for slot in range(2):
        block = x_ref[jnp.bitwise_xor(flip_ref[0], slot)].reshape(64, NG)
        points = pts_ref[slot : slot + 1, :]
        found = jnp.zeros((64, 2 * F), f32)
        for part in range(NG // chunk):
            rows = lax.broadcasted_iota(jnp.int32, (chunk, 2 * F), 0) + part * chunk
            pick = jnp.where(rows == points, 1.0, 0.0).astype(bf16)
            found = found + dot_n(block[:, part * chunk : (part + 1) * chunk], pick)
        value = found[:32] * sign_ref[slot : slot + 1, :]
        flux = 0.5 * value - 0.25 * found[32:]
        for side in range(2):
            lanes = slice(F * side, F * side + F)
            o_ref[slot, 2 * side] = flux[:, lanes].astype(bf16)
            o_ref[slot, 2 * side + 1] = value[:, lanes].astype(bf16)


def local_sides(flip, basis, points, signs):
    return pl.pallas_call(
        sides_kernel,
        grid=(1,),
        in_specs=[
            SMEM,
            pl.BlockSpec((2, 2, 32, NG), lambda d: (0, 0, 0, 0)),
            VMEM,
            VMEM,
        ],
        out_specs=VMEM,
        out_shape=jax.ShapeDtypeStruct((2, 4, 32, F), bf16),
        compiler_params=params(),
        name="local_sides",
    )(flip, basis, points, signs)


def face(a_flux, a_jump, b_flux, b_jump):
    total = dot_t(a_flux, b_jump) + dot_t(a_jump, b_flux)
    return (total * (1.0 / (4.0 * F))).astype(bf16)


def arrange_kernel(rows_ref, b0, b1, b2, b3, z_ref, c_ref, m01_ref, m10_ref, inner):
    outer = (z_ref, c_ref)
    for q, b_ref in enumerate((b0, b1, b2, b3)):
        for r in range(4):
            rows = pl.ds(pl.multiple_of(rows_ref[4 * q + r], 32), 32)
            for slot in range(2):
                for k in range(2):
                    outer[slot][k, rows, :] = b_ref[r, slot, k]
                    inner[slot, k, rows, :] = b_ref[r, slot, 2 + k]
    m01_ref[...] = face(inner[0, 0], inner[0, 1], inner[1, 0], inner[1, 1])
    m10_ref[...] = face(inner[1, 0], inner[1, 1], inner[0, 0], inner[0, 1])


def arrange(rows, blocks):
    return pl.pallas_call(
        arrange_kernel,
        in_specs=[SMEM] + [VMEM] * 4,
        out_specs=[VMEM] * 4,
        out_shape=[jax.ShapeDtypeStruct((2, NB, F), bf16)] * 2
        + [jax.ShapeDtypeStruct((NB, NB), bf16)] * 2,
        scratch_shapes=[pltpu.VMEM((2, 2, NB, F), bf16)],
        compiler_params=params(),
        cost_estimate=LONG,
        name="arrange_sides",
    )(rows, *blocks)


def edge_kernel(z_ref, zr_ref, c_ref, cr_ref, mz_ref, mc_ref):
    mz_ref[...] = face(z_ref[0], z_ref[1], zr_ref[0], zr_ref[1])
    mc_ref[...] = face(c_ref[0], c_ref[1], cr_ref[0], cr_ref[1])


def edge_couplings(*sides):
    return pl.pallas_call(
        edge_kernel,
        in_specs=[VMEM] * 4,
        out_specs=[VMEM] * 2,
        out_shape=[jax.ShapeDtypeStruct((NB, NB), bf16)] * 2,
        compiler_params=params(),
        cost_estimate=TINY,
        name="edge_couplings",
    )(*sides)


def gather_plane(x):
    return gather_second(gather_first(x))


def gather_first(x):
    return jnp.stack([lax.ppermute(x, BOTH, perm) for perm in FIRST])


def gather_second(first):
    return [first] + [lax.ppermute(first, BOTH, perm) for perm in SECOND[1:]]


def per_device(basis, potential, face_index, face_match, vectors):
    elem = lax.axis_index("elem")
    inner = lax.axis_index("inner")
    x_lo, core, chip = elem % 2, inner % 2, inner // 2
    z_even = 1 - (elem // 2) % 2
    pair = core ^ z_even

    slabs = to_slabs(basis).reshape(16, 128, SLAB)
    received = lax.all_to_all(slabs, "inner", 0, 0)

    hits = face_match[:, :, None] == lax.broadcasted_iota(jnp.int32, (1, 1, F), 2)
    left_points = jnp.sum(jnp.where(hits, face_index[:, None, 0, :], 0), axis=2)
    right_points = face_index[:, 1, :]
    own_points = jnp.concatenate((right_points, left_points), axis=1) - chip * SLAB
    own_points = lax.dynamic_slice(own_points, (core, 0), (1, 2 * F))

    lr = jnp.concatenate((left_points, right_points), axis=1)
    rl = jnp.concatenate((right_points, left_points), axis=1)
    slot_points = jnp.where(
        x_lo == 0, jnp.stack((lr[0], rl[1])), jnp.stack((rl[1], lr[0]))
    )
    minus = jnp.repeat(jnp.array([[-1.0, 1.0], [1.0, -1.0]], f32), F, axis=1)
    slot_signs = jnp.where(x_lo == 0, minus, -minus)
    sides = local_sides(x_lo.reshape(1), basis, slot_points, slot_signs)
    first_sides = gather_first(sides)
    start = lax.ppermute(vectors, BOTH, SWAP)
    v0 = lax.dynamic_index_in_dim(start, pair, 0, False)
    v1 = lax.dynamic_index_in_dim(start, 1 - pair, 0, False)
    my_y, my_x = inner // 4, 2 * ((inner // 2) % 2) + x_lo
    q = lax.broadcasted_iota(jnp.int32, (16,), 0) // 4
    r = lax.broadcasted_iota(jnp.int32, (16,), 0) % 4
    from_y = (my_y + jnp.where(core == 0, r, q)) % 4
    from_x = (my_x + jnp.where(core == 0, q, r)) % 4
    rows = 32 * (4 * from_y + from_x)
    pieces_at = jnp.stack(((from_x % 2) ^ pair, PIECE * (2 * from_y + from_x // 2)))
    received, first_sides, v0, v1 = lax.optimization_barrier((received, first_sides, v0, v1))
    blocks = gather_second(first_sides)

    packed = partial_gram(jnp.stack((core, chip)), received, potential, own_points)
    pieces = lax.all_to_all(
        packed.reshape(8, PIECE, 128), "inner", 0, 0, axis_index_groups=CHIPS
    )

    def edges(v0, v1):
        return lax.ppermute(v0, BOTH, Z_EDGE), lax.ppermute(v1, BOTH, C_EDGE)

    blocks, _ = lax.optimization_barrier((blocks, packed))
    z_sides, c_sides, m01, m10 = arrange(rows, blocks)
    z_sides, c_sides, v0, v1, _ = lax.optimization_barrier((z_sides, c_sides, v0, v1, packed))
    z_near, c_near = edges(z_sides, c_sides)
    zv, cv = edges(v0, v1)
    z_near, c_near, pieces = lax.optimization_barrier((z_near, c_near, pieces))
    mz, mc = edge_couplings(z_sides, z_near, c_sides, c_near)
    part0 = dot_n(m01, v1) + dot_n(mz, zv)

    piece = sum_pieces(pieces)
    gathered = gather_plane(piece)
    d0, new0, low0, rest = first_step(pieces_at, gathered, v0, part0)
    cv, _ = lax.optimization_barrier((cv, low0))
    part1 = dot_n(m10, v0) + dot_n(mc, cv)
    d1, new1, low1 = first_step_other(rest, v1, part1)
    previous, current, low = [v0, v1], [new0, new1], [low0, low1]
    for step in range(1, STEPS):
        last = step == STEPS - 1
        zv, cv = edges(*low)
        if step == 1:
            applied = [
                dot_n(d0, low0) + dot_n(m01, low1), dot_n(d1, low1) + dot_n(m10, low0)
            ]
            acc0, acc1 = [
                2.0 * (a - CENTER * c) / HALF_WIDTH - p.astype(f32)
                for a, c, p in zip(applied, current, previous)
            ]
        else:
            acc1 = inside(d1, m10, low[1], low[0], current[1], previous[1])
            acc0 = inside(d0, m01, low[0], low[1], current[0], previous[0])
        next1 = outside(acc1, mc, cv, last)
        if last:
            moved1 = lax.ppermute(next1, BOTH, BACK)
            moved0 = lax.ppermute(outside(acc0, mz, zv, last), BOTH, BACK)
            break
        next0 = outside(acc0, mz, zv, last)
        previous, current = current, [next0[0], next1[0]]
        low = [next0[1], next1[1]]
    out = place_last((1 - x_lo).reshape(1), moved1)
    return place_last(x_lo.reshape(1), moved0, out)


def solution(mesh):
    placed = (
        P("elem", None, "inner", None),
        P("elem", None),
        P("elem", None, None),
        P("elem", None),
        P("elem", None, "inner"),
    )
    return jax.shard_map(
        per_device, mesh=mesh, in_specs=placed, out_specs=P("elem", None, "inner"), check_vma=False
    )
```

```python
import jax
import jax.numpy as jnp
from jax import lax
from jax.experimental import pallas as pl
from jax.experimental.pallas import tpu as pltpu
from jax.sharding import PartitionSpec as P

NB = 512
NG = 4096
F = 128
STEPS = 6
CENTER = 5.25
HALF_WIDTH = 2.75
NZ, NY, NX = 8, 4, 4
BOTH = ("elem", "inner")
SLAB = NG // 8
PACKED = 10 * 128
PIECE = PACKED // 8
bf16 = jnp.bfloat16
f32 = jnp.float32


def flat(z, y, x, c):
    z, y, x = z % NZ, y % NY, x % NX
    return (z * 2 + x % 2) * 16 + y * 4 + (x // 2) * 2 + c


PLACES = [(z, y, x, c) for z in range(NZ) for y in range(NY) for x in range(NX) for c in range(2)]


def pair_of(z, c):
    return c if z % 2 else 1 - c


def moved_to(z, y, x, c):
    pair, column = x % 2, c
    return z, y, (x // 2) * 2 + column, pair if z % 2 else 1 - pair


def along(place, axis, step):
    z, y, x, c = place
    return (z, y + step, x, c) if c == axis else (z, y, x + step, c)


def pairs_of(move):
    return [(flat(*p), flat(*move(*p))) for p in PLACES]


SWAP = pairs_of(moved_to)
BACK = [(j, i) for i, j in SWAP]
Z_EDGE = pairs_of(lambda z, y, x, c: (z + (1 if pair_of(z, c) else -1), y, x, c))
C_EDGE = pairs_of(lambda z, y, x, c: (z, y, x, 1 - c))
FIRST = [pairs_of(lambda *p: along(moved_to(*p), 0, -r)) for r in range(4)]
SECOND = [pairs_of(lambda *p: along(p, 1, -q)) for q in range(4)]
CHIPS = [[c + 2 * k for k in range(8)] for c in range(2)]


def chebyshev_norm(count):
    ratio = (CENTER - 1.0) / HALF_WIDTH
    root = ratio + (ratio * ratio - 1.0) ** 0.5
    return 0.5 * (root**count + root ** (-count))


def params(mib=16):
    return pltpu.CompilerParams(vmem_limit_bytes=mib * 1024 * 1024)


TINY = pl.CostEstimate(flops=1, bytes_accessed=1, transcendentals=0)
LONG = pl.CostEstimate(flops=0, bytes_accessed=1 << 26, transcendentals=0)
VMEM = pl.BlockSpec(memory_space=pltpu.VMEM)
SMEM = pl.BlockSpec(memory_space=pltpu.SMEM)


def dot_t(a, b):
    return lax.dot_general(a, b, (((1,), (1,)), ((), ())), preferred_element_type=f32)


def dot_n(a, b):
    return lax.dot_general(a, b, (((1,), (0,)), ((), ())), preferred_element_type=f32)


def slab_kernel(x_ref, o_ref):
    for k in range(4):
        o_ref[k] = x_ref[:, :, :, SLAB * k : SLAB * k + SLAB]


def to_slabs(basis):
    return pl.pallas_call(
        slab_kernel,
        grid=(2,),
        in_specs=[pl.BlockSpec((2, 4, 32, 4 * SLAB), lambda d: (0, 0, 0, d))],
        out_specs=pl.BlockSpec((4, 2, 4, 32, SLAB), lambda d: (d, 0, 0, 0, 0)),
        out_shape=jax.ShapeDtypeStruct((8, 2, 4, 32, SLAB), bf16),
        compiler_params=params(58),
        cost_estimate=LONG,
        name="to_slabs",
    )(basis)


def sum_kernel(x_ref, o_ref):
    o_ref[...] = jnp.sum(x_ref[...], axis=0).astype(bf16)


def sum_pieces(pieces):
    return pl.pallas_call(
        sum_kernel,
        in_specs=[VMEM],
        out_specs=VMEM,
        out_shape=jax.ShapeDtypeStruct(pieces.shape[1:], bf16),
        compiler_params=params(),
        name="sum_pieces",
    )(pieces)


def gram_kernel(at_ref, r_ref, pot_ref, pts_ref, o_ref):
    comps = [r_ref[:, 32 * k : 32 * k + 32, :].reshape(NB, SLAB) for k in range(4)]
    lanes = pl.ds(pl.multiple_of(at_ref[1] * SLAB, SLAB), SLAB)
    potential = jnp.where(at_ref[0] == 0, pot_ref[0:1, lanes], pot_ref[1:2, lanes])
    scaled = (jnp.sqrt(potential) * comps[0].astype(f32)).astype(bf16)
    rows = lax.broadcasted_iota(jnp.int32, (SLAB, 2 * F), 0)
    pick = jnp.where(rows == pts_ref[...], 1.0, 0.0).astype(bf16)
    sign = jnp.where(lax.broadcasted_iota(jnp.int32, (1, 2 * F), 1) < F, 1.0, -1.0)
    value = dot_n(comps[0], pick) * sign
    slope = dot_n(comps[1], pick)
    jump = value.astype(bf16)
    flux = (0.5 * value - 0.25 * slope).astype(bf16)
    for big_i, big_j in ((0, 0), (1, 0), (1, 1)):
        left = slice(256 * big_i, 256 * big_i + 256)
        right = slice(256 * big_j, 256 * big_j + 256)
        kinetic = dot_t(comps[1][left], comps[1][right])
        kinetic = kinetic + dot_t(comps[2][left], comps[2][right])
        kinetic = kinetic + dot_t(comps[3][left], comps[3][right])
        total = (dot_t(scaled[left], scaled[right]) + 0.5 * kinetic) * (1.0 / NG)
        face = dot_t(flux[left], jump[right]) + dot_t(jump[left], flux[right])
        total = total + face * (1.0 / (4.0 * F))
        for i in range(2):
            for j in range(2):
                row, column = 2 * big_i + i, 2 * big_j + j
                if row >= column:
                    place = 128 * (row * (row + 1) // 2 + column)
                    block = total[128 * i : 128 * i + 128, 128 * j : 128 * j + 128]
                    o_ref[place : place + 128, :] = block


def partial_gram(at, received, potential, points):
    return pl.pallas_call(
        gram_kernel,
        in_specs=[SMEM] + [VMEM] * 3,
        out_specs=VMEM,
        out_shape=jax.ShapeDtypeStruct((PACKED, 128), f32),
        compiler_params=params(),
        name="partial_gram",
    )(at, received, potential, points)


def unpack(packed, d_ref):
    for row in range(4):
        for column in range(row + 1):
            place = 128 * (row * (row + 1) // 2 + column)
            block = packed[place : place + 128, :]
            r, c = pl.ds(128 * row, 128), pl.ds(128 * column, 128)
            d_ref[r, c] = block
            if row > column:
                d_ref[c, r] = block.astype(f32).T.astype(bf16)


def begin(d_ref, v_ref, part_ref, new_ref, low_ref):
    v = v_ref[...]
    applied = dot_n(d_ref[...], v) + part_ref[...]
    new = (applied - CENTER * v.astype(f32)) * (1.0 / HALF_WIDTH)
    new_ref[...] = new
    low_ref[...] = new.astype(bf16)


def first_kernel(at_ref, b0, b1, b2, b3, v_ref, part_ref, d_ref, new_ref, low_ref, packed_ref):
    for q, b_ref in enumerate((b0, b1, b2, b3)):
        for r in range(4):
            k = 4 * q + r
            rows = pl.ds(pl.multiple_of(at_ref[1, k], PIECE), PIECE)
            packed_ref[at_ref[0, k], rows, :] = b_ref[r]
    unpack(packed_ref.at[0], d_ref)
    begin(d_ref, v_ref, part_ref, new_ref, low_ref)


def second_kernel(packed_ref, v_ref, part_ref, d_ref, new_ref, low_ref):
    unpack(packed_ref.at[1], d_ref)
    begin(d_ref, v_ref, part_ref, new_ref, low_ref)


def first_shapes(v):
    return [
        jax.ShapeDtypeStruct((NB, NB), bf16),
        jax.ShapeDtypeStruct(v.shape, f32),
        jax.ShapeDtypeStruct(v.shape, bf16),
    ]


def first_step(at, blocks, v, part):
    return pl.pallas_call(
        first_kernel,
        in_specs=[SMEM] + [VMEM] * 6,
        out_specs=[VMEM] * 4,
        out_shape=first_shapes(v) + [jax.ShapeDtypeStruct((2, PACKED, 128), bf16)],
        compiler_params=params(),
        name="first_step_slot0",
    )(at, *blocks, v, part)


def first_step_other(packed, v, part):
    return pl.pallas_call(
        second_kernel,
        in_specs=[VMEM] * 3,
        out_specs=[VMEM] * 3,
        out_shape=first_shapes(v),
        compiler_params=params(),
        name="first_step_slot1",
    )(packed, v, part)


def inside_kernel(d_ref, m_ref, v_ref, w_ref, cur_ref, prev_ref, o_ref):
    applied = dot_n(d_ref[...], v_ref[...]) + dot_n(m_ref[...], w_ref[...])
    applied = applied - CENTER * cur_ref[...].astype(f32)
    o_ref[...] = applied * (2.0 / HALF_WIDTH) - prev_ref[...].astype(f32)


def inside(d, m, v, w, current, previous):
    return pl.pallas_call(
        inside_kernel,
        in_specs=[VMEM] * 6,
        out_specs=VMEM,
        out_shape=jax.ShapeDtypeStruct(v.shape, f32),
        compiler_params=params(),
        name="inside",
    )(d, m, v, w, current, previous)


def outside_kernel(acc_ref, m_ref, halo_ref, new_ref, low_ref):
    new = acc_ref[...] + dot_n(m_ref[...], halo_ref[...]) * (2.0 / HALF_WIDTH)
    new_ref[...] = new
    low_ref[...] = new.astype(bf16)


def outside_last_kernel(acc_ref, m_ref, halo_ref, low_ref):
    new = acc_ref[...] + dot_n(m_ref[...], halo_ref[...]) * (2.0 / HALF_WIDTH)
    low_ref[...] = (new * (1.0 / chebyshev_norm(STEPS))).astype(bf16)


def outside(acc, m, halo, last):
    low = jax.ShapeDtypeStruct(acc.shape, bf16)
    return pl.pallas_call(
        outside_last_kernel if last else outside_kernel,
        in_specs=[VMEM] * 3,
        out_specs=VMEM if last else [VMEM] * 2,
        out_shape=low if last else [jax.ShapeDtypeStruct(acc.shape, f32), low],
        compiler_params=params(),
        name="outside",
    )(acc, m, halo)


def last_kernel(at_ref, m_ref, *refs):
    refs[-1][0] = m_ref[...].astype(f32)


def place_last(at, moved, out=None):
    rows, columns = moved.shape
    part = rows // 2
    more = [] if out is None else [out]
    return pl.pallas_call(
        last_kernel,
        grid_spec=pltpu.PrefetchScalarGridSpec(
            num_scalar_prefetch=1,
            grid=(2,),
            in_specs=[pl.BlockSpec((part, columns), lambda i, at: (i, 0))]
            + [pl.BlockSpec(memory_space=pl.ANY)] * len(more),
            out_specs=pl.BlockSpec((1, part, columns), lambda i, at: (at[0], i, 0)),
        ),
        out_shape=jax.ShapeDtypeStruct((2, rows, columns), f32),
        input_output_aliases={2: 0} if more else {},
        compiler_params=params(),
        name="place_last",
    )(at, moved, *more)


def sides_kernel(flip_ref, x_ref, pts_ref, sign_ref, o_ref):
    chunk = 512
    for slot in range(2):
        block = x_ref[jnp.bitwise_xor(flip_ref[0], slot)].reshape(64, NG)
        points = pts_ref[slot : slot + 1, :]
        found = jnp.zeros((64, 2 * F), f32)
        for part in range(NG // chunk):
            rows = lax.broadcasted_iota(jnp.int32, (chunk, 2 * F), 0) + part * chunk
            pick = jnp.where(rows == points, 1.0, 0.0).astype(bf16)
            found = found + dot_n(block[:, part * chunk : (part + 1) * chunk], pick)
        value = found[:32] * sign_ref[slot : slot + 1, :]
        flux = 0.5 * value - 0.25 * found[32:]
        for side in range(2):
            lanes = slice(F * side, F * side + F)
            o_ref[slot, 2 * side] = flux[:, lanes].astype(bf16)
            o_ref[slot, 2 * side + 1] = value[:, lanes].astype(bf16)


def local_sides(flip, basis, points, signs):
    return pl.pallas_call(
        sides_kernel,
        grid=(1,),
        in_specs=[
            SMEM,
            pl.BlockSpec((2, 2, 32, NG), lambda d: (0, 0, 0, 0)),
            VMEM,
            VMEM,
        ],
        out_specs=VMEM,
        out_shape=jax.ShapeDtypeStruct((2, 4, 32, F), bf16),
        compiler_params=params(),
        name="local_sides",
    )(flip, basis, points, signs)


def face(a_flux, a_jump, b_flux, b_jump):
    total = dot_t(a_flux, b_jump) + dot_t(a_jump, b_flux)
    return (total * (1.0 / (4.0 * F))).astype(bf16)


def arrange_kernel(rows_ref, b0, b1, b2, b3, z_ref, c_ref, m01_ref, m10_ref, inner):
    outer = (z_ref, c_ref)
    for q, b_ref in enumerate((b0, b1, b2, b3)):
        for r in range(4):
            rows = pl.ds(pl.multiple_of(rows_ref[4 * q + r], 32), 32)
            for slot in range(2):
                for k in range(2):
                    outer[slot][k, rows, :] = b_ref[r, slot, k]
                    inner[slot, k, rows, :] = b_ref[r, slot, 2 + k]
    m01_ref[...] = face(inner[0, 0], inner[0, 1], inner[1, 0], inner[1, 1])
    m10_ref[...] = face(inner[1, 0], inner[1, 1], inner[0, 0], inner[0, 1])


def arrange(rows, blocks):
    return pl.pallas_call(
        arrange_kernel,
        in_specs=[SMEM] + [VMEM] * 4,
        out_specs=[VMEM] * 4,
        out_shape=[jax.ShapeDtypeStruct((2, NB, F), bf16)] * 2
        + [jax.ShapeDtypeStruct((NB, NB), bf16)] * 2,
        scratch_shapes=[pltpu.VMEM((2, 2, NB, F), bf16)],
        compiler_params=params(),
        cost_estimate=LONG,
        name="arrange_sides",
    )(rows, *blocks)


def edge_kernel(z_ref, zr_ref, c_ref, cr_ref, mz_ref, mc_ref):
    mz_ref[...] = face(z_ref[0], z_ref[1], zr_ref[0], zr_ref[1])
    mc_ref[...] = face(c_ref[0], c_ref[1], cr_ref[0], cr_ref[1])


def edge_couplings(*sides):
    return pl.pallas_call(
        edge_kernel,
        in_specs=[VMEM] * 4,
        out_specs=[VMEM] * 2,
        out_shape=[jax.ShapeDtypeStruct((NB, NB), bf16)] * 2,
        compiler_params=params(),
        cost_estimate=TINY,
        name="edge_couplings",
    )(*sides)


def gather_plane(x):
    return gather_second(gather_first(x))


def gather_first(x):
    return jnp.stack([lax.ppermute(x, BOTH, perm) for perm in FIRST])


def gather_second(first):
    return [first] + [lax.ppermute(first, BOTH, perm) for perm in SECOND[1:]]


def per_device(basis, potential, face_index, face_match, vectors):
    elem = lax.axis_index("elem")
    inner = lax.axis_index("inner")
    x_lo, core, chip = elem % 2, inner % 2, inner // 2
    z_even = 1 - (elem // 2) % 2
    pair = core ^ z_even

    slabs = to_slabs(basis).reshape(16, 128, SLAB)
    received = lax.all_to_all(slabs, "inner", 0, 0)

    hits = face_match[:, :, None] == lax.broadcasted_iota(jnp.int32, (1, 1, F), 2)
    left_points = jnp.sum(jnp.where(hits, face_index[:, None, 0, :], 0), axis=2)
    right_points = face_index[:, 1, :]
    own_points = jnp.concatenate((right_points, left_points), axis=1) - chip * SLAB
    own_points = lax.dynamic_slice(own_points, (core, 0), (1, 2 * F))

    lr = jnp.concatenate((left_points, right_points), axis=1)
    rl = jnp.concatenate((right_points, left_points), axis=1)
    slot_points = jnp.where(
        x_lo == 0, jnp.stack((lr[0], rl[1])), jnp.stack((rl[1], lr[0]))
    )
    minus = jnp.repeat(jnp.array([[-1.0, 1.0], [1.0, -1.0]], f32), F, axis=1)
    slot_signs = jnp.where(x_lo == 0, minus, -minus)
    sides = local_sides(x_lo.reshape(1), basis, slot_points, slot_signs)
    first_sides = gather_first(sides)
    start = lax.ppermute(vectors, BOTH, SWAP)
    v0 = lax.dynamic_index_in_dim(start, pair, 0, False)
    v1 = lax.dynamic_index_in_dim(start, 1 - pair, 0, False)
    my_y, my_x = inner // 4, 2 * ((inner // 2) % 2) + x_lo
    q = lax.broadcasted_iota(jnp.int32, (16,), 0) // 4
    r = lax.broadcasted_iota(jnp.int32, (16,), 0) % 4
    from_y = (my_y + jnp.where(core == 0, r, q)) % 4
    from_x = (my_x + jnp.where(core == 0, q, r)) % 4
    rows = 32 * (4 * from_y + from_x)
    pieces_at = jnp.stack(((from_x % 2) ^ pair, PIECE * (2 * from_y + from_x // 2)))
    received, v0, v1 = lax.optimization_barrier((received, v0, v1))

    packed = partial_gram(jnp.stack((core, chip)), received, potential, own_points)
    pieces = lax.all_to_all(
        packed.reshape(8, PIECE, 128), "inner", 0, 0, axis_index_groups=CHIPS
    )

    def edges(v0, v1):
        return lax.ppermute(v0, BOTH, Z_EDGE), lax.ppermute(v1, BOTH, C_EDGE)

    first_sides, _ = lax.optimization_barrier((first_sides, packed))
    blocks = gather_second(first_sides)
    z_sides, c_sides, m01, m10 = arrange(rows, blocks)
    z_sides, c_sides, v0, v1, _ = lax.optimization_barrier((z_sides, c_sides, v0, v1, packed))
    z_near, c_near = edges(z_sides, c_sides)
    zv, cv = edges(v0, v1)
    z_near, c_near, pieces = lax.optimization_barrier((z_near, c_near, pieces))
    mz, mc = edge_couplings(z_sides, z_near, c_sides, c_near)
    part0 = dot_n(m01, v1) + dot_n(mz, zv)

    piece = sum_pieces(pieces)
    gathered = gather_plane(piece)
    d0, new0, low0, rest = first_step(pieces_at, gathered, v0, part0)
    cv, _ = lax.optimization_barrier((cv, low0))
    part1 = dot_n(m10, v0) + dot_n(mc, cv)
    d1, new1, low1 = first_step_other(rest, v1, part1)
    previous, current, low = [v0, v1], [new0, new1], [low0, low1]
    for step in range(1, STEPS):
        last = step == STEPS - 1
        zv, cv = edges(*low)
        if step == 1:
            applied = [
                dot_n(d0, low0) + dot_n(m01, low1), dot_n(d1, low1) + dot_n(m10, low0)
            ]
            acc0, acc1 = [
                2.0 * (a - CENTER * c) / HALF_WIDTH - p.astype(f32)
                for a, c, p in zip(applied, current, previous)
            ]
        else:
            acc1 = inside(d1, m10, low[1], low[0], current[1], previous[1])
            acc0 = inside(d0, m01, low[0], low[1], current[0], previous[0])
        next1 = outside(acc1, mc, cv, last)
        if last:
            moved1 = lax.ppermute(next1, BOTH, BACK)
            moved0 = lax.ppermute(outside(acc0, mz, zv, last), BOTH, BACK)
            break
        next0 = outside(acc0, mz, zv, last)
        previous, current = current, [next0[0], next1[0]]
        low = [next0[1], next1[1]]
    out = place_last((1 - x_lo).reshape(1), moved1)
    return place_last(x_lo.reshape(1), moved0, out)


def solution(mesh):
    placed = (
        P("elem", None, "inner", None),
        P("elem", None),
        P("elem", None, None),
        P("elem", None),
        P("elem", None, "inner"),
    )
    return jax.shard_map(
        per_device, mesh=mesh, in_specs=placed, out_specs=P("elem", None, "inner"), check_vma=False
    )
```
